32 devices in a mesh: blk: 8 (over y, x, core), tp: 4 (over z).
Axes of the slice: x: 2, y: 2, z: 4, core: 2. Of those that a mesh axis runs over, the one named last changes fastest.
Arguments:
- frames: bfloat16 [20, 512, 1024], P(None, 'blk'), may hold values from -6 to 6
- text_states: bfloat16 [20, 2, 64, 1024], replicated, may hold values from -6 to 6
- clip_lengths: int32 [20, 2], replicated, may hold values from 0 to 512, as said below
- text_lengths: int32 [20, 2], replicated, may hold values from 1 to 64
- cotangent: bfloat16 [20, 512, 1024], P(None, 'blk'), may hold values from -6 to 6
- norm_gain: float32 [3, 1024], replicated, may hold values from 0.5 to 1.5
- norm_bias: float32 [3, 1024], replicated, may hold values from -1.5 to 1.5
- self_proj: bfloat16 [3, 1024, 1024], P(None, None, 'tp'), may hold values from -0.1875 to 0.1875
- self_out: bfloat16 [1024, 1024], P('tp'), may hold values from -0.5 to 0.5
- cross_query: bfloat16 [1024, 1024], P(None, 'tp'), may hold values from -0.1875 to 0.1875
- cross_mem: bfloat16 [2, 1024, 1024], P(None, None, 'tp'), may hold values from -0.1875 to 0.1875
- cross_out: bfloat16 [1024, 1024], P('tp'), may hold values from -0.5 to 0.5
- ffn_up: bfloat16 [1024, 4096], P(None, 'tp'), may hold values from -0.1875 to 0.1875
- ffn_down: bfloat16 [4096, 1024], P('tp'), may hold values from -0.09375 to 0.09375
Outputs:
- out_frames: float32 [20, 512, 1024], P(None, 'blk')
- grad_frames: float32 [20, 512, 1024], P(None, 'blk')
- grad_text: float32 [20, 2, 64, 1024], replicated
- grad_gain: float32 [3, 1024], P(None, 'blk')
- grad_bias: float32 [3, 1024], P(None, 'blk')
- grad_self_proj: float32 [3, 1024, 1024], P(None, 'blk', 'tp')
- grad_self_out: float32 [1024, 1024], P('tp', 'blk')
- grad_cross_query: float32 [1024, 1024], P('blk', 'tp')
- grad_cross_mem: float32 [2, 1024, 1024], P(None, 'blk', 'tp')
- grad_cross_out: float32 [1024, 1024], P('tp', 'blk')
- grad_ffn_up: float32 [1024, 4096], P('blk', 'tp')
- grad_ffn_down: float32 [4096, 1024], P('tp', 'blk')
The draws below stay inside these ranges and needn't reach their ends.
Inputs may be any that keep to these rules, and one draw needn't show every extreme that they name: `clip_lengths`: each stream's clip lengths add up to 512. In one stream, drawn from the seed, the first clip holds all 512 frames and the other slots none; every other stream holds one clip of 128 frames and one of 384 frames in its first two slots, in an order drawn from the seed, and its later slots are empty.
All inputs are finite; a program needn't handle non-finite values.
Results may differ from the reference program's by a relative error of at most 0.028.
Values may be sent and summed in bfloat16 or wider, within the bound.
No kernel may reach another device: no remote copies, remote signals or barrier semaphores. Data moves between devices by JAX's collectives and lax.ppermute only.
A program may use at most 512 MiB of HBM per device.

```python
import math
import jax
import jax.numpy as jnp
from jax import lax

D = 1024
HEADS = 16
HEAD_DIM = 64
FF = 4096
TEXT = 64
CLIPS = 2
STREAMS = 20
SEQ = 512


def draw_clip_lengths(key, part):
    key = jax.random.fold_in(key, 11)
    full_key, order_key = jax.random.split(key)
    chosen = jax.random.randint(full_key, (), 0, STREAMS)
    short_first = jax.random.randint(order_key, (STREAMS,), 0, 2)
    short_len = SEQ // 4
    long_len = SEQ - short_len
    first_len = jnp.where(short_first == 1, short_len, long_len).astype(jnp.int32)
    second_len = (SEQ - first_len).astype(jnp.int32)
    paired = jnp.stack([first_len, second_len], axis=1)
    single_clip = jnp.zeros((STREAMS, 2), jnp.int32).at[:, 0].set(SEQ)
    is_chosen = jnp.arange(STREAMS, dtype=jnp.int32)[:, None] == chosen
    leading = jnp.where(is_chosen, single_clip, paired).astype(jnp.int32)
    trailing = jnp.zeros((STREAMS, CLIPS - 2), jnp.int32)
    return jnp.concatenate([leading, trailing], axis=1).astype(jnp.int32)


def draw_text_lengths(key, part):
    key = jax.random.fold_in(key, 23)
    first_key, second_key = jax.random.split(key)
    drawn_lengths = jax.random.randint(first_key, (STREAMS * CLIPS,), 1, TEXT + 1)
    chosen = jax.random.randint(second_key, (), 0, STREAMS * CLIPS)
    flattened = jnp.where(jnp.arange(STREAMS * CLIPS, dtype=jnp.int32) == chosen, TEXT, drawn_lengths)
    return flattened.reshape(STREAMS, CLIPS).astype(jnp.int32)


def raised(values, stream_key, source, target, shards_of, factor):
    def block_of(axis_at):
        return (jnp.arange(values.shape[axis_at]) // (values.shape[axis_at] // shards_of)).reshape((-1,) + (1,) * (values.ndim - 1 - axis_at))

    near = jax.random.permutation(stream_key, shards_of)[block_of(target)]
    other_side = (block_of(target) + shards_of // 2) % shards_of
    return jnp.where((block_of(source) == near) | (block_of(source) == other_side), factor * values, values)


def levels(rng, dims, cuts, low, largest):
    factor_of, own = 1.0, jax.random.fold_in(rng, 6)
    for dim, parts in cuts:
        heights = jnp.exp(jax.random.uniform(jax.random.fold_in(own, dim), (parts,), jnp.float32, low / len(cuts), largest / len(cuts)))
        factor_of = factor_of * jnp.repeat(heights, dims[dim] // parts).reshape([-1 if axis == dim else 1 for axis in range(len(dims))])
    return factor_of


def bell_draw(rng, shape, deviation, limit, pieces=(), kind=jnp.bfloat16):
    array = deviation * jax.random.normal(rng, shape, jnp.float32)
    if pieces:
        array = array * levels(rng, shape, pieces, -0.22, 0.18)
    return jnp.clip(array, -limit, limit).astype(kind)


def heavy_noise(stream_key, dims, scale, bound, pieces, heavy, held_as=jnp.bfloat16):
    values = scale * jax.random.normal(stream_key, dims, jnp.float32)
    if pieces:
        values = values * levels(stream_key, dims, pieces, -0.22, 0.18)
    return jnp.clip(raised(values, jax.random.fold_in(stream_key, 3), *heavy), -bound, bound).astype(held_as)


def setup_inputs(seed: int = 0) -> dict:
    keys = jax.random.split(jax.random.key(seed), 15)
    frames = bell_draw(keys[0], (STREAMS, SEQ, D), 1.0, 6.0, ((1, 8),))
    text_states = bell_draw(keys[1], (STREAMS, CLIPS, TEXT, D), 1.0, 6.0)
    clip_lengths = draw_clip_lengths(jax.random.fold_in(keys[14], 71), 0)
    text_lengths = draw_text_lengths(jax.random.fold_in(keys[14], 71), 0)
    cotangent = heavy_noise(keys[4], (STREAMS, SEQ, D), 1.0, 6.0, ((1, 8),), (1, 2, 8, 2.0))
    norm_gain = jnp.clip(1.0 + 0.1 * jax.random.normal(keys[5], (3, D), jnp.float32), 0.5, 1.5)
    norm_bias = bell_draw(keys[6], (3, D), 0.3, 1.5, (), jnp.float32)
    self_proj = bell_draw(keys[7], (3, D, D), D ** -0.5, 0.1875, ((2, 4),))
    self_out = bell_draw(keys[8], (D, D), (D // 8) ** -0.5, 0.5, ((0, 4),))
    cross_query = bell_draw(keys[9], (D, D), D ** -0.5, 0.1875, ((1, 4),))
    cross_mem = bell_draw(keys[10], (2, D, D), D ** -0.5, 0.1875, ((2, 4),))
    cross_out = bell_draw(keys[11], (D, D), (D // 8) ** -0.5, 0.5, ((0, 4),))
    ffn_up = bell_draw(keys[12], (D, FF), D ** -0.5, 0.1875, ((1, 4),))
    ffn_down = bell_draw(keys[13], (FF, D), FF ** -0.5, 0.09375, ((0, 4),))
    return {"frames": frames, "text_states": text_states, "clip_lengths": clip_lengths, "text_lengths": text_lengths, "cotangent": cotangent, "norm_gain": norm_gain, "norm_bias": norm_bias, "self_proj": self_proj, "self_out": self_out, "cross_query": cross_query, "cross_mem": cross_mem, "cross_out": cross_out, "ffn_up": ffn_up, "ffn_down": ffn_down}


@jax.custom_vjp
def low(v):
    return lax.optimization_barrier(v.astype(jnp.bfloat16)).astype(jnp.float32)

@jax.custom_vjp
def low_back(v):
    return v

def low_keep(v):
    return (low(v), None)

def low_pass(kept, grad):
    return (grad,)

def back_keep(v):
    return (v, None)

def back_low(kept, grad):
    return (low(grad),)
low.defvjp(low_keep, low_pass)
low_back.defvjp(back_keep, back_low)
highest = lax.Precision.HIGHEST
score_scale = 0.125
masked_value = -1e+30
norm_eps = 1e-05

def rounded(values):
    return low_back(low(values))

def layer_norm(values, norm_scale, norm_shift):
    centre = values - lax.optimization_barrier(jnp.mean(values, axis=-1, keepdims=True))
    spread = lax.optimization_barrier(jnp.mean(centre * centre, axis=-1, keepdims=True))
    return centre * lax.rsqrt(spread + norm_eps) * norm_scale + norm_shift

def clip_index(lengths, positions):
    clip_ends = jnp.cumsum(lengths, axis=1)
    return lax.optimization_barrier(jnp.sum((clip_ends[:, None, :] <= positions[None, :, None]).astype(jnp.int32), axis=2))

def attend(queries, key_heads, value_heads, allowed):
    scores = low_back(jnp.einsum('qhe,khe->hqk', queries, key_heads, precision=highest) * score_scale)
    weights = low(jax.nn.softmax(jnp.where(allowed[None], scores, masked_value), axis=-1))
    return jnp.einsum('hqk,khe->qhe', weights, value_heads, precision=highest)

def blockwise(queries, key_heads, value_heads, allowed_for):
    streams = queries.shape[0]
    length = queries.shape[1]
    block_rows = math.gcd(length, 512)
    count_blocks = length // block_rows

    def one_block(indices):
        stream, block_no = indices
        first_row = (block_no * block_rows).astype(jnp.int32)
        query_part = lax.dynamic_slice_in_dim(queries[stream], first_row, block_rows, 0)
        return attend(query_part, key_heads[stream], value_heads[stream], allowed_for(stream, first_row, block_rows))
    stream_ids = jnp.repeat(jnp.arange(streams, dtype=jnp.int32), count_blocks)
    block_ids = jnp.tile(jnp.arange(count_blocks, dtype=jnp.int32), streams)
    outputs = lax.map(jax.checkpoint(one_block), (stream_ids, block_ids))
    return outputs.reshape(queries.shape)

def reference(frames, text_states, clip_lengths, text_lengths, cotangent, norm_gain, norm_bias, self_proj, self_out, cross_query, cross_mem, cross_out, ffn_up, ffn_down):
    positions = jnp.arange(SEQ, dtype=jnp.int32)
    clips = clip_index(clip_lengths, positions)
    text_rows = CLIPS * TEXT
    row_ids = jnp.arange(text_rows, dtype=jnp.int32)
    row_clip = row_ids // TEXT
    row_valid = (row_ids % TEXT)[None, :] < jnp.repeat(text_lengths, TEXT, axis=1)

    def causal_allowed(stream, first_row, block_rows):
        query_pos = first_row + jnp.arange(block_rows, dtype=jnp.int32)
        query_clip = lax.dynamic_slice_in_dim(clips[stream], first_row, block_rows, 0)
        return (positions[None, :] <= query_pos[:, None]) & (clips[stream][None, :] == query_clip[:, None])

    def cross_allowed(stream, first_row, block_rows):
        query_clip = lax.dynamic_slice_in_dim(clips[stream], first_row, block_rows, 0)
        return (row_clip[None, :] == query_clip[:, None]) & row_valid[stream][None, :]

    def forward(inputs, texts, norm_scale, norm_shift, proj_weight, self_weight, query_weight, memory_weight, cross_weight, up_weight, down_weight):
        normed_one = low(layer_norm(inputs, norm_scale[0], norm_shift[0]))
        projected = rounded(jnp.einsum('std,kde->kste', normed_one, proj_weight, precision=highest))
        heads = projected.reshape(3, STREAMS, SEQ, HEADS, HEAD_DIM)
        attention = rounded(blockwise(heads[0], heads[1], heads[2], causal_allowed))
        self_branch = low_back(jnp.einsum('ste,ed->std', attention.reshape(STREAMS, SEQ, D), self_weight, precision=highest))
        second = inputs + self_branch
        normed_two = low(layer_norm(second, norm_scale[1], norm_shift[1]))
        cross_heads = rounded(jnp.einsum('std,de->ste', normed_two, query_weight, precision=highest)).reshape(STREAMS, SEQ, HEADS, HEAD_DIM)
        memory = rounded(jnp.einsum('scxd,kde->kscxe', texts, memory_weight, precision=highest)).reshape(2, STREAMS, text_rows, HEADS, HEAD_DIM)
        cross_attention = rounded(blockwise(cross_heads, memory[0], memory[1], cross_allowed))
        cross_branch = low_back(jnp.einsum('ste,ed->std', cross_attention.reshape(STREAMS, SEQ, D), cross_weight, precision=highest))
        third = second + cross_branch
        normed_three = low(layer_norm(third, norm_scale[2], norm_shift[2]))
        hidden = low_back(jnp.einsum('std,df->stf', normed_three, up_weight, precision=highest))
        active = low(jax.nn.gelu(hidden, approximate=False))
        return third + low_back(jnp.einsum('stf,fd->std', active, down_weight, precision=highest))
    result, pullback = jax.vjp(forward, frames.astype(jnp.float32), text_states.astype(jnp.float32), norm_gain, norm_bias, self_proj.astype(jnp.float32), self_out.astype(jnp.float32), cross_query.astype(jnp.float32), cross_mem.astype(jnp.float32), cross_out.astype(jnp.float32), ffn_up.astype(jnp.float32), ffn_down.astype(jnp.float32))
    grads = pullback(cotangent.astype(jnp.float32))
    return (result, grads[0], grads[1], grads[2], grads[3], grads[4], grads[5], grads[6], grads[7], grads[8], grads[9], grads[10])
```

```python
import functools

import jax
import jax.numpy as jnp
from jax import lax
from jax.experimental import pallas as pl
from jax.experimental.pallas import tpu as pltpu
from jax.sharding import PartitionSpec as P

HEAD_DIM = 64
SCALE = 0.125
MASKED = -1e30
EPS = 1e-05
LANES = 128
BF = jnp.bfloat16
F32 = jnp.float32


def dot(a, b, dims):
    return lax.dot_general(a, b, (dims, ((), ())), preferred_element_type=F32)


NN = ((1,), (0,))
NT = ((1,), (1,))
TN = ((0,), (0,))


def head_masks(width):
    lane = lax.broadcasted_iota(jnp.int32, (1, width), 1) // HEAD_DIM
    return [lane == h for h in range(width // HEAD_DIM)]


def pick(mask, values):
    return jnp.where(mask, values, jnp.zeros_like(values))


def causal_probs(ends_ref, stream, slots, q, k, first, block):
    rows = first + lax.broadcasted_iota(jnp.int32, (block, 1), 0)
    begin = jnp.zeros((block, 1), jnp.int32)
    for c in range(slots):
        end = ends_ref[stream, c]
        begin = jnp.where(rows >= end, jnp.maximum(begin, end), begin)
    cols = lax.broadcasted_iota(jnp.int32, (block, k.shape[0]), 1)
    allowed = (cols <= rows) & (cols >= begin)
    scores = jnp.where(allowed, dot(q, k, NT), MASKED)
    weights = jnp.exp(scores - jnp.max(scores, axis=1, keepdims=True))
    return weights * (1.0 / jnp.sum(weights, axis=1, keepdims=True))


def self_forward_kernel(ends_ref, qkv_ref, out_ref, *, slots, width, block):
    stream = pl.program_id(0)
    parts, _, rows, _ = qkv_ref.shape
    length = parts * rows
    qkv = qkv_ref[...].reshape(length, 3 * width)
    q = qkv[:, :width] * jnp.asarray(SCALE, BF)
    k = qkv[:, width : 2 * width]
    v = qkv[:, 2 * width :]
    masks = head_masks(width)
    q_of = [pick(m, q) for m in masks]
    v_of = [pick(m, v) for m in masks]
    per = block // rows
    for first in range(0, length, block):
        top = first + block
        total = jnp.zeros((block, width), F32)
        for h in range(len(masks)):
            probs = causal_probs(
                ends_ref, stream, slots, q_of[h][first:top], k[:top], first, block
            )
            total += dot(probs.astype(BF), v_of[h][:top], NN)
        at = first // rows
        out_ref[at : at + per, 0] = total.astype(BF).reshape(per, rows, width)


def self_backward_kernel(ends_ref, qkv_ref, grad_ref, out_ref, dk_ref, dv_ref, *, slots, width, block):
    stream = pl.program_id(0)
    parts, _, rows, _ = qkv_ref.shape
    length = parts * rows
    qkv = qkv_ref[...].reshape(length, 3 * width)
    q = qkv[:, :width] * jnp.asarray(SCALE, BF)
    k = qkv[:, width : 2 * width]
    v = qkv[:, 2 * width :]
    grad = grad_ref[...].reshape(length, width)
    masks = head_masks(width)
    q_of = [pick(m, q) for m in masks]
    k_of = [pick(m, k) for m in masks]
    g_of = [pick(m, grad) for m in masks]
    dk_ref[...] = jnp.zeros_like(dk_ref)
    dv_ref[...] = jnp.zeros_like(dv_ref)
    per = block // rows
    for first in range(0, length, block):
        top = first + block
        dq = jnp.zeros((block, width), F32)
        for h in range(len(masks)):
            q_part = q_of[h][first:top]
            g_part = g_of[h][first:top]
            probs = causal_probs(ends_ref, stream, slots, q_part, k[:top], first, block)
            d_probs = dot(g_part, v[:top], NT)
            delta = jnp.sum(probs * d_probs, axis=1, keepdims=True)
            d_scores = (probs * (d_probs - delta)).astype(BF)
            dq += dot(d_scores, k_of[h][:top], NN)
            dk_ref[:top] += dot(d_scores, q_part, TN)
            dv_ref[:top] += dot(probs.astype(BF), g_part, TN)
        at = first // rows
        out_ref[at : at + per, 0, :, :width] = (dq * SCALE).astype(BF).reshape(per, rows, width)
    out_ref[:, 0, :, width : 2 * width] = dk_ref[...].astype(BF).reshape(parts, rows, width)
    out_ref[:, 0, :, 2 * width :] = dv_ref[...].astype(BF).reshape(parts, rows, width)


def piece_spec(parts, rows, width):
    return pl.BlockSpec((parts, 1, rows, width), lambda s, *_: (0, s, 0, 0))


def block_rows(rows):
    return rows * max(1, 256 // rows)


def self_forward(ends, qkv, width):
    parts, streams, rows, _ = qkv.shape
    length = parts * rows
    kernel = functools.partial(
        self_forward_kernel, slots=ends.shape[1], width=width, block=min(length, block_rows(rows))
    )
    work = streams * (width // HEAD_DIM) * length * length
    return pl.pallas_call(
        kernel,
        out_shape=jax.ShapeDtypeStruct((parts, streams, rows, width), BF),
        grid_spec=pltpu.PrefetchScalarGridSpec(
            num_scalar_prefetch=1,
            grid=(streams,),
            in_specs=[piece_spec(parts, rows, 3 * width)],
            out_specs=piece_spec(parts, rows, width),
        ),
        compiler_params=pltpu.CompilerParams(vmem_limit_bytes=48 << 20),
        cost_estimate=pl.CostEstimate(
            flops=4 * work * HEAD_DIM, bytes_accessed=8 * streams * length * width, transcendentals=work
        ),
        name="self_forward",
    )(ends, qkv)


def self_backward(ends, qkv, grad, width):
    parts, streams, rows, _ = qkv.shape
    length = parts * rows
    kernel = functools.partial(
        self_backward_kernel, slots=ends.shape[1], width=width, block=min(length, block_rows(rows))
    )
    work = streams * (width // HEAD_DIM) * length * length
    return pl.pallas_call(
        kernel,
        out_shape=jax.ShapeDtypeStruct((parts, streams, rows, 3 * width), BF),
        grid_spec=pltpu.PrefetchScalarGridSpec(
            num_scalar_prefetch=1,
            grid=(streams,),
            in_specs=[piece_spec(parts, rows, 3 * width), piece_spec(parts, rows, width)],
            out_specs=piece_spec(parts, rows, 3 * width),
            scratch_shapes=[pltpu.VMEM((length, width), F32), pltpu.VMEM((length, width), F32)],
        ),
        compiler_params=pltpu.CompilerParams(vmem_limit_bytes=48 << 20),
        cost_estimate=pl.CostEstimate(
            flops=10 * work * HEAD_DIM, bytes_accessed=14 * streams * length * width, transcendentals=work
        ),
        name="self_backward",
    )(ends, qkv, grad)


def cross_allowed(info_ref, stream, slots, rows, keys):
    text = keys // slots
    pos = info_ref[stream, 2 * slots] + lax.broadcasted_iota(jnp.int32, (rows, 1), 0)
    clip = jnp.zeros((rows, 1), jnp.int32)
    for c in range(slots):
        clip += jnp.where(pos >= info_ref[stream, c], 1, 0)
    begin = clip * text
    count = jnp.zeros((rows, 1), jnp.int32)
    for c in range(slots):
        count = jnp.where(clip == c, info_ref[stream, slots + c], count)
    key = lax.broadcasted_iota(jnp.int32, (rows, keys), 1)
    return (key >= begin) & (key < begin + count)


def stacked_heads(values):
    masks = head_masks(values.shape[1])
    return jnp.concatenate([pick(m, values) for m in masks], axis=0)


def merged_heads(values, rows):
    masks = head_masks(values.shape[1])
    total = values[:rows]
    for h in range(1, len(masks)):
        total = jnp.where(masks[h], values[h * rows : (h + 1) * rows], total)
    return total


def cross_probs(q, k, allowed):
    scores = jnp.where(allowed, dot(q, k, NT), MASKED)
    weights = jnp.exp(scores - jnp.max(scores, axis=1, keepdims=True))
    return weights * (1.0 / jnp.sum(weights, axis=1, keepdims=True))


def cross_forward_kernel(info_ref, q_ref, kv_ref, out_ref, *, slots):
    stream = pl.program_id(0)
    rows, width = q_ref.shape[1:]
    keys = kv_ref.shape[1]
    once = cross_allowed(info_ref, stream, slots, rows, keys)
    allowed = jnp.concatenate([once] * (LANES // HEAD_DIM), axis=0)
    for at in range(0, width, LANES):
        q = stacked_heads(q_ref[0, :, at : at + LANES] * jnp.asarray(SCALE, BF))
        probs = cross_probs(q, kv_ref[0, :, at : at + LANES], allowed)
        result = dot(probs.astype(BF), kv_ref[0, :, width + at : width + at + LANES], NN)
        out_ref[0, :, at : at + LANES] = merged_heads(result, rows).astype(BF)


def cross_backward_kernel(info_ref, q_ref, kv_ref, grad_ref, dq_ref, dkv_ref, *, slots):
    stream = pl.program_id(0)
    rows, width = q_ref.shape[1:]
    keys = kv_ref.shape[1]
    once = cross_allowed(info_ref, stream, slots, rows, keys)
    allowed = jnp.concatenate([once] * (LANES // HEAD_DIM), axis=0)
    for at in range(0, width, LANES):
        k = kv_ref[0, :, at : at + LANES]
        v = kv_ref[0, :, width + at : width + at + LANES]
        q = stacked_heads(q_ref[0, :, at : at + LANES] * jnp.asarray(SCALE, BF))
        grad = stacked_heads(grad_ref[0, :, at : at + LANES])
        probs = cross_probs(q, k, allowed)
        d_probs = dot(grad, v, NT)
        delta = jnp.sum(probs * d_probs, axis=1, keepdims=True)
        d_scores = (probs * (d_probs - delta)).astype(BF)
        dq = merged_heads(dot(d_scores, k, NN), rows) * SCALE
        dq_ref[0, :, at : at + LANES] = dq.astype(BF)
        dkv_ref[0, :, at : at + LANES] = dot(d_scores, q, TN).astype(BF)
        dkv_ref[0, :, width + at : width + at + LANES] = dot(probs.astype(BF), grad, TN).astype(BF)


def stream_spec(array):
    return pl.BlockSpec((1,) + array.shape[1:], lambda s, *_: (s, 0, 0))


def cross_call(kernel, info, arrays, outs, name):
    streams, rows, width = arrays[0].shape
    keys = arrays[1].shape[1]
    slots = info.shape[1] // 2
    work = streams * (width // HEAD_DIM) * rows * keys
    return pl.pallas_call(
        functools.partial(kernel, slots=slots),
        out_shape=outs,
        grid_spec=pltpu.PrefetchScalarGridSpec(
            num_scalar_prefetch=1,
            grid=(streams,),
            in_specs=[stream_spec(a) for a in arrays],
            out_specs=[stream_spec(o) for o in outs],
        ),
        compiler_params=pltpu.CompilerParams(vmem_limit_bytes=48 << 20),
        cost_estimate=pl.CostEstimate(
            flops=8 * work * HEAD_DIM,
            bytes_accessed=2 * sum(a.size for a in (*arrays, *outs)),
            transcendentals=work,
        ),
        name=name,
    )(info, *arrays)


def normalize(values):
    centre = values - jnp.mean(values, axis=-1, keepdims=True)
    inverse = lax.rsqrt(jnp.mean(centre * centre, axis=-1, keepdims=True) + EPS)
    return centre * inverse, inverse


def norm_backward(normal, inverse, gain, upstream):
    g = upstream * gain
    mean_g = jnp.mean(g, axis=-1, keepdims=True)
    mean_gn = jnp.mean(g * normal, axis=-1, keepdims=True)
    d_values = inverse * (g - mean_g - normal * mean_gn)
    return d_values, jnp.sum(upstream * normal, axis=0), jnp.sum(upstream, axis=0)


def gelu_parts(u):
    cdf = 0.5 * (1.0 + lax.erf(u * (0.5**0.5)))
    slope = cdf + u * jnp.exp(-0.5 * u * u) * (0.5 / jnp.pi) ** 0.5
    return u * cdf, slope


def shards(
    frames,
    text_states,
    clip_lengths,
    text_lengths,
    cotangent,
    norm_gain,
    norm_bias,
    self_proj,
    self_out,
    cross_query,
    cross_mem,
    cross_out,
    ffn_up,
    ffn_down,
):
    streams, rows, model = frames.shape
    slots, text = text_states.shape[1:3]
    text_rows = slots * text
    blk, tp = lax.axis_size("blk"), lax.axis_size("tp")
    b, t = lax.axis_index("blk"), lax.axis_index("tp")
    mine = streams // tp
    head_parts = min(blk, model // HEAD_DIM)
    stream_parts = blk // head_parts
    width = model // head_parts
    group = -(-mine // stream_parts)
    local = self_out.shape[0]
    per = local // width
    share = model // blk
    hidden = ffn_up.shape[1]
    count = mine * rows

    def of_rank(values, rank):
        return lax.dynamic_slice_in_dim(values, rank * mine, mine, 0)

    def share_rows(w):
        return lax.dynamic_slice_in_dim(w, b * share, share, w.ndim - 2)

    def share_cols(w):
        return lax.dynamic_slice_in_dim(w, b * share, share, 1).T

    first = share_rows(self_proj).reshape(3, share, per, width)
    first = first.transpose(1, 2, 0, 3).reshape(share, 3 * local)
    first = lax.all_gather(first, "tp").transpose(1, 0, 2).reshape(share, tp * 3 * local)
    w_qkv = lax.all_gather(first, "blk", axis=0, tiled=True)

    mem = share_rows(cross_mem)
    second = jnp.stack(
        [share_cols(self_out), share_rows(cross_query), share_cols(cross_out), mem[0], mem[1]]
    )
    second = lax.all_gather(second, "tp").transpose(2, 1, 0, 3).reshape(share, 5 * model)
    w_attn = lax.all_gather(second, "blk", axis=0, tiled=True)
    w_out, w_query, w_cross_out = (w_attn[:, i * model : (i + 1) * model] for i in range(3))
    w_mem = w_attn[:, 3 * model :]

    groups = tp // 2
    piece = jnp.concatenate([share_rows(ffn_up), share_cols(ffn_down)], axis=1)
    up_parts, down_parts = [ffn_up], [ffn_down.T]
    if groups > 1:
        others = [
            lax.ppermute(piece, "tp", [(i, (i + 2 * j) % tp) for i in range(tp)])
            for j in range(1, groups)
        ]
        w_others = lax.all_gather(jnp.concatenate(others, axis=1), "blk", axis=0, tiled=True)
        for j in range(groups - 1):
            up_parts.append(w_others[:, 2 * j * hidden : (2 * j + 1) * hidden])
            down_parts.append(w_others[:, (2 * j + 1) * hidden : (2 * j + 2) * hidden])
    w_up = jnp.concatenate(up_parts, axis=1)
    w_down = jnp.concatenate(down_parts, axis=1)

    ends = jnp.cumsum(of_rank(clip_lengths, t), axis=1).astype(jnp.int32)
    info = jnp.concatenate(
        [ends, of_rank(text_lengths, t), jnp.full((mine, 1), b * rows, jnp.int32)], axis=1
    )
    x = of_rank(frames, t).reshape(count, model).astype(F32)
    n1, r1 = normalize(x)
    h1 = (n1 * norm_gain[0] + norm_bias[0]).astype(BF)

    def to_heads(values):
        c = values.shape[1] // head_parts
        values = values.reshape(mine, rows, head_parts, c)
        if stream_parts > 1:
            values = jnp.pad(values, ((0, stream_parts * group - mine),) + ((0, 0),) * 3)
        values = values.reshape(stream_parts, group, rows, head_parts, c).transpose(0, 3, 1, 2, 4)
        return lax.all_to_all(values.reshape(blk, group, rows, c), "blk", 0, 0)

    def to_rows(values):
        c = values.shape[3]
        swapped = lax.all_to_all(values, "blk", 0, 0)
        swapped = swapped.reshape(stream_parts, head_parts, group, rows, c).transpose(0, 2, 3, 1, 4)
        swapped = swapped.reshape(stream_parts * group, rows, head_parts * c)
        return swapped[:mine].reshape(count, head_parts * c)

    own_ends = ends
    if stream_parts > 1:
        own_ends = jnp.pad(ends, ((0, stream_parts * group - mine), (0, 0)))
        own_ends = lax.dynamic_slice_in_dim(own_ends, b // head_parts * group, group, 0)

    qkv = to_heads(dot(h1, w_qkv, NN).astype(BF))
    attn = to_rows(self_forward(own_ends, qkv, width))
    x2 = x + dot(attn, w_out, NT)

    n2, r2 = normalize(x2)
    h2 = (n2 * norm_gain[1] + norm_bias[1]).astype(BF)
    cq = dot(h2, w_query, NN).astype(BF).reshape(mine, rows, model)
    texts = of_rank(text_states, t).reshape(mine * text_rows, model)
    ckv = dot(texts, w_mem, NN).astype(BF).reshape(mine, text_rows, 2 * model)
    (cattn,) = cross_call(
        cross_forward_kernel, info, (cq, ckv), [jax.ShapeDtypeStruct(cq.shape, BF)], "cross_forward"
    )
    cattn = cattn.reshape(count, model)
    x3 = x2 + dot(cattn, w_cross_out, NT)

    n3, r3 = normalize(x3)
    h3 = (n3 * norm_gain[2] + norm_bias[2]).astype(BF)
    swap = [(i, i ^ 1) for i in range(tp)]
    partner = t ^ 1
    h3_pair = jnp.concatenate([h3, lax.ppermute(h3, "tp", swap)], axis=0)
    ct = of_rank(cotangent, t).reshape(count, model)
    ct_pair = jnp.concatenate([ct, of_rank(cotangent, partner).reshape(count, model)], axis=0)
    up = dot(h3_pair, w_up, NN)
    act, slope = gelu_parts(up)
    act = act.astype(BF)
    d_up = (dot(ct_pair, w_down, NN) * slope).astype(BF)

    def pair_sum(partial):
        sent = lax.ppermute(partial[count:].astype(BF), "tp", swap)
        return partial[:count] + sent.astype(F32)

    d_h3 = pair_sum(dot(d_up, w_up, NT))
    out = x3 + pair_sum(dot(act, w_down, NT))
    g_up = dot(h3_pair, d_up, TN).astype(BF)
    g_down = dot(ct_pair, act, TN).astype(BF)

    def over_frames(parts):
        joined = jnp.concatenate(parts, axis=1) if len(parts) > 1 else parts[0]
        return lax.psum_scatter(joined, "blk", scatter_dimension=0, tiled=True)

    g_ffn = over_frames([g_up, g_down])
    g_ffn = g_ffn.reshape(share, 2, groups, hidden)
    ffn_total = g_ffn[:, :, 0].astype(F32)
    for j in range(1, groups):
        back = [((i + 2 * j) % tp, i) for i in range(tp)]
        ffn_total += lax.ppermute(g_ffn[:, :, j], "tp", back).astype(F32)
    grad_ffn_up = ffn_total[:, 0]
    grad_ffn_down = ffn_total[:, 1].T

    d_n3, gain3, bias3 = norm_backward(n3, r3, norm_gain[2], d_h3)
    d_x3 = ct.astype(F32) + d_n3

    d_c = d_x3.astype(BF)
    g_cross_out = dot(d_c, cattn, TN).astype(BF)
    d_cattn = dot(d_c, w_cross_out, NN).astype(BF).reshape(mine, rows, model)
    d_cq, d_ckv = cross_call(
        cross_backward_kernel,
        info,
        (cq, ckv, d_cattn),
        [jax.ShapeDtypeStruct(cq.shape, BF), jax.ShapeDtypeStruct(ckv.shape, BF)],
        "cross_backward",
    )
    d_cq = d_cq.reshape(count, model)
    g_query = dot(h2, d_cq, TN).astype(BF)
    d_h2 = dot(d_cq, w_query, NT)
    d_n2, gain2, bias2 = norm_backward(n2, r2, norm_gain[1], d_h2)
    d_x2 = d_x3 + d_n2

    d_ckv = lax.psum_scatter(
        d_ckv.reshape(mine * text_rows, 2 * model), "blk", scatter_dimension=0, tiled=True
    )
    text_part = mine * text_rows // blk
    g_mem = dot(lax.dynamic_slice_in_dim(texts, b * text_part, text_part, 0), d_ckv, TN).astype(BF)
    d_text = dot(d_ckv, w_mem, NT).astype(BF)
    d_text = lax.all_gather(lax.all_gather(d_text, "tp"), "blk")
    grad_text = d_text.transpose(1, 0, 2, 3).reshape(streams, slots, text, model)
    grad_text = grad_text.astype(F32)

    d_a = d_x2.astype(BF)
    g_out = dot(d_a, attn, TN).astype(BF)
    d_attn = to_heads(dot(d_a, w_out, NN).astype(BF))
    d_qkv = to_rows(self_backward(own_ends, qkv, d_attn, width))
    g_qkv = dot(h1, d_qkv, TN).astype(BF)
    d_h1 = dot(d_qkv, w_qkv, NT)
    d_n1, gain1, bias1 = norm_backward(n1, r1, norm_gain[0], d_h1)
    d_x = d_x2 + d_n1

    def over_ranks(values):
        return lax.psum_scatter(values, "tp", scatter_dimension=0).astype(F32)

    g_attn = over_frames([g_out, g_query, g_cross_out, g_mem])
    g_attn = over_ranks(g_attn.reshape(share, 5, tp, local).transpose(2, 1, 0, 3))
    grad_self_out = g_attn[0].T
    grad_cross_query = g_attn[1]
    grad_cross_out = g_attn[2].T
    grad_cross_mem = g_attn[3:]
    g_qkv = over_frames([g_qkv])
    g_qkv = over_ranks(g_qkv.reshape(share, tp, 3 * local).transpose(1, 0, 2))
    grad_self_proj = g_qkv.reshape(share, per, 3, width).transpose(2, 0, 1, 3)
    grad_self_proj = grad_self_proj.reshape(3, share, local)

    norms = lax.psum(jnp.stack([gain1, gain2, gain3, bias1, bias2, bias3]), ("blk", "tp"))
    norms = lax.dynamic_slice_in_dim(norms, b * share, share, 1)

    def to_ranks(values):
        gathered = lax.all_gather(values.astype(BF), "tp", axis=0, tiled=True)
        return gathered.reshape(streams, rows, model).astype(F32)

    return (
        to_ranks(out),
        to_ranks(d_x),
        grad_text,
        norms[:3],
        norms[3:],
        grad_self_proj,
        grad_self_out,
        grad_cross_query,
        grad_cross_mem,
        grad_cross_out,
        grad_ffn_up,
        grad_ffn_down,
    )


def solution(mesh):
    in_specs = (
        P(None, "blk", None),
        P(),
        P(),
        P(),
        P(None, "blk", None),
        P(),
        P(),
        P(None, None, "tp"),
        P("tp", None),
        P(None, "tp"),
        P(None, None, "tp"),
        P("tp", None),
        P(None, "tp"),
        P("tp", None),
    )
    out_specs = (
        P(None, "blk", None),
        P(None, "blk", None),
        P(),
        P(None, "blk"),
        P(None, "blk"),
        P(None, "blk", "tp"),
        P("tp", "blk"),
        P("blk", "tp"),
        P(None, "blk", "tp"),
        P("tp", "blk"),
        P("blk", "tp"),
        P("tp", "blk"),
    )
    return jax.shard_map(shards, mesh=mesh, in_specs=in_specs, out_specs=out_specs, check_vma=False)
```

```python
import functools

import jax
import jax.numpy as jnp
from jax import lax
from jax.experimental import pallas as pl
from jax.experimental.pallas import tpu as pltpu
from jax.sharding import PartitionSpec as P

HEAD_DIM = 64
SCALE = 0.125
MASKED = -1e30
EPS = 1e-05
LANES = 128
BF = jnp.bfloat16
F32 = jnp.float32
MIB = 1 << 20

NN = ((1,), (0,))
NT = ((1,), (1,))
TN = ((0,), (0,))


def dot(a, b, dims):
    return lax.dot_general(a, b, (dims, ((), ())), preferred_element_type=F32)


def whole_spec(array):
    zeros = (0,) * len(array.shape)
    return pl.BlockSpec(tuple(array.shape), lambda *_: zeros)


def call(kernel, name, grid, ins, outs, scalars=(), scratch=(), deps=(), flops=0, exps=0):
    count = len(ins)

    def body(*refs):
        kept = len(scalars) + count
        kernel(*refs[:kept], *refs[kept + len(deps) :])

    specs = [whole_spec(a) if s is None else s for a, s in ins]
    specs += [pl.BlockSpec(memory_space=pl.ANY)] * len(deps)
    moved = sum(a.size * a.dtype.itemsize for a, _ in (*ins, *outs))
    return pl.pallas_call(
        body,
        out_shape=[o for o, _ in outs],
        grid_spec=pltpu.PrefetchScalarGridSpec(
            num_scalar_prefetch=len(scalars),
            grid=grid,
            in_specs=specs,
            out_specs=[whole_spec(o) if s is None else s for o, s in outs],
            scratch_shapes=list(scratch),
        ),
        compiler_params=pltpu.CompilerParams(vmem_limit_bytes=56 * MIB),
        cost_estimate=pl.CostEstimate(flops=flops, bytes_accessed=moved, transcendentals=exps),
        name=name,
    )(*scalars, *[a for a, _ in ins], *deps)


def struct(shape, dtype=BF):
    return jax.ShapeDtypeStruct(tuple(shape), dtype)


def assemble(whole_ref, near_ref, far_ref, device, parts=1):
    chips, ranks, share, cols = near_ref.shape
    c = cols // parts
    core = device % 2
    for chip in range(chips):
        for ref, k in ((near_ref, core), (far_ref, 1 - core)):
            rows = pl.ds(pl.multiple_of((2 * chip + k) * share, share), share)
            for p in range(parts):
                for r in range(ranks):
                    to = (p * ranks + r) * c
                    whole_ref[rows, to : to + c] = ref[chip, r, :, p * c : (p + 1) * c]


def columns(pair, size, place):
    return [
        (w, pl.BlockSpec(w.shape[:3] + (size,), lambda *_: (0, 0, 0, place))) for w in pair
    ]


def normalize(values):
    centre = values - jnp.mean(values, axis=-1, keepdims=True)
    inverse = lax.rsqrt(jnp.mean(centre * centre, axis=-1, keepdims=True) + EPS)
    return centre * inverse, inverse


def normed(values, gain, bias):
    return (normalize(values)[0] * gain + bias).astype(BF)


def norm_backward(values, gain, upstream):
    normal, inverse = normalize(values)
    g = upstream * gain
    mean_g = jnp.mean(g, axis=-1, keepdims=True)
    mean_gn = jnp.mean(g * normal, axis=-1, keepdims=True)
    d_values = inverse * (g - mean_g - normal * mean_gn)
    gain_sum = jnp.sum(upstream * normal, axis=0, keepdims=True)
    return d_values, gain_sum, jnp.sum(upstream, axis=0, keepdims=True)


def head_masks(width):
    lane = lax.broadcasted_iota(jnp.int32, (1, width), 1) // HEAD_DIM
    return [lane == h for h in range(width // HEAD_DIM)]


def pick(mask, values):
    return jnp.where(mask, values, jnp.zeros_like(values))


def stacked_heads(values):
    return jnp.concatenate([pick(m, values) for m in head_masks(values.shape[1])], axis=0)


def merged_heads(values, rows):
    total = values[:rows]
    for h, mask in enumerate(head_masks(values.shape[1])):
        if h:
            total = jnp.where(mask, values[h * rows : (h + 1) * rows], total)
    return total


def softmax(scores, allowed):
    scores = jnp.where(allowed, scores, MASKED)
    weights = jnp.exp(scores - jnp.max(scores, axis=1, keepdims=True))
    return weights * (1.0 / jnp.sum(weights, axis=1, keepdims=True))


def qkv_kernel(x_ref, norm_ref, w_ref, out_ref, h_ref):
    width = out_ref.shape[3] // 3
    x = x_ref[...].reshape(-1, x_ref.shape[-1]).astype(F32)
    h = normed(x, norm_ref[0:1], norm_ref[1:2])
    h_ref[...] = h
    for k in range(3):
        result = dot(h, w_ref[k], NN).astype(BF)
        for p in range(out_ref.shape[1]):
            out_ref[0, p, :, k * width : (k + 1) * width] = result[:, p * width : (p + 1) * width]


def qkv_pieces(frames, norm, weights, slices, parts, width, deps=()):
    streams, rows, model = frames.shape
    group = streams // slices
    out = struct((slices, parts, group * rows, 3 * width))
    return call(
        qkv_kernel,
        "qkv",
        (slices,),
        [
            (frames, pl.BlockSpec((group, rows, model), lambda i: (i, 0, 0))),
            (norm, None),
            (weights, None),
        ],
        [
            (out, pl.BlockSpec((1,) + out.shape[1:], lambda i: (i, 0, 0, 0))),
            (
                struct((streams * rows, model)),
                pl.BlockSpec((group * rows, model), lambda i: (i, 0)),
            ),
        ],
        deps=deps,
        flops=2 * streams * rows * weights.size,
    )


def qkv_grad_kernel(grad_ref, w_ref, out_ref, merged_ref):
    parts, width = grad_ref.shape[1], grad_ref.shape[3] // 3
    local = parts * width
    for p in range(parts):
        for k in range(3):
            to = k * local + p * width
            merged_ref[:, to : to + width] = grad_ref[0, p, :, k * width : (k + 1) * width]
    total = 0.0
    for k in range(3):
        total += dot(merged_ref[:, k * local : (k + 1) * local], w_ref[k], NT)
    out_ref[0] = total.astype(BF)


def last_kernel(parts_ref, x_ref, dx2_ref, norm_ref, dx_ref, sums_ref):
    d_h1 = parts_ref[0].astype(F32)
    for r in range(1, parts_ref.shape[0]):
        d_h1 += parts_ref[r].astype(F32)
    d_v, gain, bias = norm_backward(x_ref[...].astype(F32), norm_ref[0:1], d_h1)
    sums_ref[0:1] = gain
    sums_ref[1:2] = bias
    d_x = (dx2_ref[...] + d_v).astype(BF)
    for r in range(dx_ref.shape[0]):
        dx_ref[r] = d_x


def causal_probs(ends_ref, stream, slots, q, k, first):
    block = q.shape[0]
    rows = first + lax.broadcasted_iota(jnp.int32, (block, 1), 0)
    begin = jnp.zeros((block, 1), jnp.int32)
    for c in range(slots):
        end = ends_ref[stream, c]
        begin = jnp.where(rows >= end, jnp.maximum(begin, end), begin)
    cols = lax.broadcasted_iota(jnp.int32, (block, k.shape[0]), 1)
    return softmax(dot(q, k, NT), (cols <= rows) & (cols >= begin))


def self_forward_kernel(ends_ref, qkv_ref, out_ref, *, slots, width, block):
    stream = pl.program_id(0)
    parts, _, rows, _ = qkv_ref.shape
    length = parts * rows
    qkv = qkv_ref[...].reshape(length, 3 * width)
    q = qkv[:, :width] * jnp.asarray(SCALE, BF)
    k = qkv[:, width : 2 * width]
    v = qkv[:, 2 * width :]
    masks = head_masks(width)
    q_of = [pick(m, q) for m in masks]
    v_of = [pick(m, v) for m in masks]
    per = block // rows
    for first in range(0, length, block):
        top = first + block
        total = jnp.zeros((block, width), F32)
        for h in range(len(masks)):
            probs = causal_probs(ends_ref, stream, slots, q_of[h][first:top], k[:top], first)
            total += dot(probs.astype(BF), v_of[h][:top], NN)
        at = first // rows
        out_ref[at : at + per, 0] = total.astype(BF).reshape(per, rows, width)


def self_backward_kernel(ends_ref, qkv_ref, grad_ref, out_ref, dk_ref, dv_ref, *, slots, width, block):
    stream = pl.program_id(0)
    parts, _, rows, _ = qkv_ref.shape
    length = parts * rows
    qkv = qkv_ref[...].reshape(length, 3 * width)
    q = qkv[:, :width] * jnp.asarray(SCALE, BF)
    k = qkv[:, width : 2 * width]
    v = qkv[:, 2 * width :]
    grad = grad_ref[...].reshape(length, width)
    masks = head_masks(width)
    q_of = [pick(m, q) for m in masks]
    k_of = [pick(m, k) for m in masks]
    g_of = [pick(m, grad) for m in masks]
    dk_ref[...] = jnp.zeros_like(dk_ref)
    dv_ref[...] = jnp.zeros_like(dv_ref)
    per = block // rows
    for first in range(0, length, block):
        top = first + block
        dq = jnp.zeros((block, width), F32)
        for h in range(len(masks)):
            q_part = q_of[h][first:top]
            g_part = g_of[h][first:top]
            probs = causal_probs(ends_ref, stream, slots, q_part, k[:top], first)
            d_probs = dot(g_part, v[:top], NT)
            delta = jnp.sum(probs * d_probs, axis=1, keepdims=True)
            d_scores = (probs * (d_probs - delta)).astype(BF)
            dq += dot(d_scores, k_of[h][:top], NN)
            dk_ref[:top] += dot(d_scores, q_part, TN)
            dv_ref[:top] += dot(probs.astype(BF), g_part, TN)
        at = first // rows
        out_ref[at : at + per, 0, :, :width] = (dq * SCALE).astype(BF).reshape(per, rows, width)
    out_ref[:, 0, :, width : 2 * width] = dk_ref[...].astype(BF).reshape(parts, rows, width)
    out_ref[:, 0, :, 2 * width :] = dv_ref[...].astype(BF).reshape(parts, rows, width)


def self_attention(ends, arrays, width, kernel, out_width, scratch, name, deps=()):
    parts, streams, rows, _ = arrays[0].shape
    length = parts * rows
    block = min(length, rows * max(1, 256 // rows))
    work = streams * (width // HEAD_DIM) * length * length

    def spec(c):
        return pl.BlockSpec((parts, 1, rows, c), lambda s, *_: (0, s, 0, 0))

    out = struct((parts, streams, rows, out_width))
    return call(
        functools.partial(kernel, slots=ends.shape[1], width=width, block=block),
        name,
        (streams,),
        [(a, spec(a.shape[3])) for a in arrays],
        [(out, spec(out_width))],
        scalars=(ends,),
        scratch=[pltpu.VMEM((length, width), F32)] * scratch,
        deps=deps,
        flops=4 * len(arrays) * work * HEAD_DIM,
        exps=work,
    )[0]


def first_kernel(device_ref, x_ref, norm_ref, near_ref, far_ref, *refs):
    pieces, (x2_ref, h2_ref, cq_ref, attn_out_ref, w_ref) = refs[:-5], refs[-5:]
    model = x2_ref.shape[1]
    assemble(w_ref, near_ref, far_ref, device_ref[0], 2)
    for j, ref in enumerate(pieces):
        piece = jnp.concatenate([ref[p] for p in range(ref.shape[0])], axis=1)
        local = piece.shape[1]
        to = pl.multiple_of((device_ref[1] ^ j) * local, local)
        attn_out_ref[:, pl.ds(to, local)] = piece
    attn = attn_out_ref[...]
    x2 = x_ref[...].astype(F32) + dot(attn, w_ref[:, :model], NT)
    x2_ref[...] = x2
    h2 = normed(x2, norm_ref[0:1], norm_ref[1:2])
    h2_ref[...] = h2
    cq_ref[...] = dot(h2, w_ref[:, model:], NN).astype(BF)


def memory_kernel(device_ref, text_ref, near_ref, far_ref, out_ref, w_ref):
    assemble(w_ref, near_ref, far_ref, device_ref[0])
    out_ref[...] = dot(text_ref[...], w_ref[...], NN).astype(BF)


def text_grad_kernel(device_ref, rows_ref, near_ref, far_ref, out_ref, w_ref):
    assemble(w_ref, near_ref, far_ref, device_ref[0], 2)
    out_ref[...] = dot(rows_ref[...], w_ref[...], NT).astype(BF)


def cross_allowed(info_ref, stream, slots, rows, keys):
    text = keys // slots
    pos = info_ref[stream, 2 * slots] + lax.broadcasted_iota(jnp.int32, (rows, 1), 0)
    clip = jnp.zeros((rows, 1), jnp.int32)
    for c in range(slots):
        clip += jnp.where(pos >= info_ref[stream, c], 1, 0)
    begin = clip * text
    count = jnp.zeros((rows, 1), jnp.int32)
    for c in range(slots):
        count = jnp.where(clip == c, info_ref[stream, slots + c], count)
    key = lax.broadcasted_iota(jnp.int32, (rows, keys), 1)
    return (key >= begin) & (key < begin + count)


CROSS_LANES = 256


def second_kernel(
    info_ref, x2_ref, cq_ref, kv_ref, norm_ref, near_ref, far_ref, *refs, slots, rows
):
    cattn_ref, x3_ref, h3_ref, wo_ref = refs
    stream = pl.program_id(0)
    model = x2_ref.shape[1]
    keys = kv_ref.shape[1]
    mine = pl.ds(pl.multiple_of(stream * rows, rows), rows)
    once = cross_allowed(info_ref, stream, slots, rows, keys)
    allowed = jnp.concatenate([once] * (CROSS_LANES // HEAD_DIM), axis=0)
    for at in range(0, model, CROSS_LANES):
        cols = slice(at, at + CROSS_LANES)
        q = stacked_heads(cq_ref[mine, cols] * jnp.asarray(SCALE, BF))
        probs = softmax(dot(q, kv_ref[0, :, cols], NT), allowed)
        result = dot(probs.astype(BF), kv_ref[0, :, model + at : model + at + CROSS_LANES], NN)
        cattn_ref[mine, cols] = merged_heads(result, rows).astype(BF)

    @pl.when(stream == pl.num_programs(0) - 1)
    def _():
        assemble(wo_ref, near_ref, far_ref, info_ref[0, 2 * slots + 1])
        x3 = x2_ref[...] + dot(cattn_ref[...], wo_ref[...], NT)
        x3_ref[...] = x3
        h3_ref[...] = normed(x3, norm_ref[0:1], norm_ref[1:2])


def third_kernel(
    info_ref,
    dh_ref,
    received_ref,
    x3_ref,
    ct_ref,
    x2_ref,
    cq_ref,
    kv_ref,
    gain_ref,
    near1_ref,
    far1_ref,
    near2_ref,
    far2_ref,
    dc_ref,
    dcq_ref,
    dx2_ref,
    da_ref,
    dattn_ref,
    dkv_ref,
    sums_ref,
    dx3_ref,
    dcattn_ref,
    w_first_ref,
    w_cross_ref,
    *,
    slots,
    rows,
):
    device = info_ref[0, 2 * slots + 1]
    stream = pl.program_id(0)
    model = x2_ref.shape[1]
    keys = kv_ref.shape[1]

    @pl.when(stream == 0)
    def _():
        d_h3 = dh_ref[...] + received_ref[...].astype(F32)
        d_v, gain, bias = norm_backward(x3_ref[...], gain_ref[2:3], d_h3)
        sums_ref[1:2] = gain
        sums_ref[3:4] = bias
        d_x3 = ct_ref[...].astype(F32) + d_v
        dx3_ref[...] = d_x3
        d_c = d_x3.astype(BF)
        dc_ref[...] = d_c
        assemble(w_cross_ref, near2_ref, far2_ref, device)
        dcattn_ref[...] = dot(d_c, w_cross_ref[...], NN).astype(BF)

    mine = pl.ds(pl.multiple_of(stream * rows, rows), rows)
    once = cross_allowed(info_ref, stream, slots, rows, keys)
    allowed = jnp.concatenate([once] * (CROSS_LANES // HEAD_DIM), axis=0)
    for at in range(0, model, CROSS_LANES):
        cols = slice(at, at + CROSS_LANES)
        k = kv_ref[0, :, cols]
        v = kv_ref[0, :, model + at : model + at + CROSS_LANES]
        q = stacked_heads(cq_ref[mine, cols] * jnp.asarray(SCALE, BF))
        grad = stacked_heads(dcattn_ref[mine, cols])
        probs = softmax(dot(q, k, NT), allowed)
        d_probs = dot(grad, v, NT)
        delta = jnp.sum(probs * d_probs, axis=1, keepdims=True)
        d_scores = (probs * (d_probs - delta)).astype(BF)
        dcq_ref[mine, cols] = (merged_heads(dot(d_scores, k, NN), rows) * SCALE).astype(BF)
        d_k = dot(d_scores, q, TN).astype(BF)
        d_v = dot(probs.astype(BF), grad, TN).astype(BF)
        dkv_ref[0, :, cols] = d_k
        dkv_ref[0, :, model + at : model + at + CROSS_LANES] = d_v

    @pl.when(stream == pl.num_programs(0) - 1)
    def _():
        assemble(w_first_ref, near1_ref, far1_ref, device, 2)
        d_h2 = dot(dcq_ref[...], w_first_ref[:, model:], NT)
        d_v, gain, bias = norm_backward(x2_ref[...], gain_ref[1:2], d_h2)
        sums_ref[0:1] = gain
        sums_ref[2:3] = bias
        d_x2 = dx3_ref[...] + d_v
        dx2_ref[...] = d_x2
        d_a = d_x2.astype(BF)
        da_ref[...] = d_a
        d_attn = dot(d_a, w_first_ref[:, :model], NN).astype(BF)
        ranks, parts, _, width = dattn_ref.shape
        for p in range(ranks * parts):
            to = (p // parts) ^ info_ref[0, 2 * slots + 2]
            dattn_ref[to, p % parts] = d_attn[:, p * width : (p + 1) * width]


def ffn_kernel(h_ref, ct_ref, *refs, groups, tiles):
    act_ref, dup_ref, dh_ref, out_ref, dh_acc, out_acc = refs[2 * groups :]
    step = pl.program_id(0)

    @pl.when(step == 0)
    def _():
        dh_acc[...] = jnp.zeros_like(dh_acc)
        out_acc[...] = jnp.zeros_like(out_acc)

    for g in range(groups):

        @pl.when(step // tiles == g)
        def _(g=g):
            w_up, w_down = refs[2 * g][...], refs[2 * g + 1][...]
            into, out_of = (NN, NT) if g else (NT, NN)
            up = dot(h_ref[...], w_up, NN)
            d_act = dot(ct_ref[...], w_down, into)
            cdf = 0.5 * (1.0 + lax.erf(up * (0.5**0.5)))
            slope = cdf + up * jnp.exp(-0.5 * up * up) * 0.3989422804014327
            act = (up * cdf).astype(BF)
            d_up = (d_act * slope).astype(BF)
            act_ref[...] = act
            dup_ref[...] = d_up
            dh_acc[...] += dot(d_up, w_up, NT)
            out_acc[...] += dot(act, w_down, out_of)

    @pl.when(step == groups * tiles - 1)
    def _():
        dh_ref[...] = dh_acc[...].astype(dh_ref.dtype)
        out_ref[...] = out_acc[...].astype(out_ref.dtype)


def feed_forward(h, ct, own, others, hidden, dtype, deps=()):
    count, model = h.shape
    groups = 1 + len(others)
    tile = min(hidden, 512)
    tiles = hidden // tile

    def place(g):
        return lambda i: jnp.clip(i - g * tiles, 0, tiles - 1)

    ins = [(h, None), (ct, None)]
    ins.append((own[0], pl.BlockSpec((model, tile), lambda i: (0, place(0)(i)))))
    ins.append((own[1], pl.BlockSpec((tile, model), lambda i: (place(0)(i), 0))))
    for g, w in enumerate(others, 1):
        for first in (0, tiles):
            spec = pl.BlockSpec((model, tile), lambda i, g=g, f=first: (0, f + place(g)(i)))
            ins.append((w, spec))
    wide = struct((count, groups * hidden))
    narrow = struct((count, model), dtype)
    column = pl.BlockSpec((count, tile), lambda i: (0, i))
    return call(
        functools.partial(ffn_kernel, groups=groups, tiles=tiles),
        "feed_forward",
        (groups * tiles,),
        ins,
        [(wide, column), (wide, column), (narrow, None), (narrow, None)],
        scratch=[pltpu.VMEM((count, model), F32)] * 2,
        deps=deps,
        flops=8 * count * model * groups * hidden,
        exps=2 * count * groups * hidden,
    )


def weight_grad_kernel(index_ref, *refs, sums, chips, plus, apart):
    outs = refs[-chips:] if apart else [refs[-1].at[j] for j in range(chips)]
    plus_ref = refs[-chips - 1 if apart else -2]
    at = 0
    for p, terms in enumerate(sums):
        total = 0.0
        for _ in range(terms):
            left = jnp.concatenate([r[...] for r in refs[at : at + chips]], axis=1)
            total += dot(left, refs[at + chips][...], TN)
            at += chips + 1
        share = total.shape[0] // chips
        for j in range(chips):
            block = total[j * share : (j + 1) * share]
            if plus:
                block += plus_ref[j, p].astype(F32)
            outs[j][p] = block.astype(BF)


def weight_grad_blocks(index, sums, share, plus=None, apart=False, deps=()):
    model = sums[0][0][0].shape[1]
    cols = sums[0][0][1][2]
    chips = model // (2 * share)
    if share % LANES:
        parts = []
        for terms in sums:
            total = 0.0
            for left, (right, first, _) in terms:
                left = left.reshape(-1, 2 * chips, share)[:, index]
                right = right[:, first : first + cols]
                total += dot(left.reshape(-1, chips * share), right, TN)
            parts.append(total.reshape(chips, share, cols))
        blocks = jnp.stack(parts, axis=1)
        blocks = (blocks if plus is None else blocks + plus.astype(F32)).astype(BF)
        return [blocks[j] for j in range(chips)] if apart else blocks
    tile = 512 if cols % 512 == 0 else cols
    ins = []
    flops = 0
    for terms in sums:
        for left, (right, first, _) in terms:
            for j in range(chips):
                ins.append((left, pl.BlockSpec((left.shape[0], share), lambda i, w, j=j: (0, w[j]))))
            spec = pl.BlockSpec(
                (right.shape[0], tile), lambda i, w, first=first: (0, first // tile + i)
            )
            ins.append((right, spec))
            flops += right.shape[0] * model * cols
    every = struct((chips, len(sums), share, cols))
    every_spec = pl.BlockSpec((chips, len(sums), share, tile), lambda i, w: (0, 0, 0, i))
    one_spec = pl.BlockSpec((len(sums), share, tile), lambda i, w: (0, 0, i))
    outs = [(every, every_spec)]
    if plus is not None:
        ins.append((plus, every_spec))
    if apart:
        outs = [(struct(every.shape[1:]), one_spec)] * chips
    result = call(
        functools.partial(
            weight_grad_kernel,
            sums=[len(terms) for terms in sums],
            chips=chips,
            plus=plus is not None,
            apart=apart,
        ),
        "weight_grad",
        (cols // tile,),
        ins,
        outs,
        scalars=(index,),
        deps=deps,
        flops=flops,
    )
    return result if apart else result[0]


def tie_kernel(*refs):
    pass


def tied(value, *first):
    anywhere = pl.BlockSpec(memory_space=pl.ANY)
    return pl.pallas_call(
        tie_kernel,
        out_shape=struct(value.shape, value.dtype),
        in_specs=[anywhere] * (1 + len(first)),
        out_specs=anywhere,
        input_output_aliases={0: 0},
        cost_estimate=pl.CostEstimate(flops=0, bytes_accessed=0, transcendentals=0),
        name="tied",
    )(value, *first)


def text_kernel(in_ref, out_ref):
    part = in_ref.shape[2]
    for i in range(in_ref.shape[0]):
        out_ref[0, i * part : (i + 1) * part] = in_ref[i, 0].astype(F32)


def shards(
    frames,
    text_states,
    clip_lengths,
    text_lengths,
    cotangent,
    norm_gain,
    norm_bias,
    self_proj,
    self_out,
    cross_query,
    cross_mem,
    cross_out,
    ffn_up,
    ffn_down,
):
    streams, rows, model = frames.shape
    slots, text = text_states.shape[1:3]
    text_rows = slots * text
    blk, tp = lax.axis_size("blk"), lax.axis_size("tp")
    b, t = lax.axis_index("blk"), lax.axis_index("tp")
    mine = streams // tp
    count = mine * rows
    core, chips = b % 2, blk // 2
    local = self_out.shape[0]
    per = min(blk // tp, local // HEAD_DIM)
    width = local // per
    slices = blk // per
    group = -(-streams // slices)
    share = model // blk
    hidden = ffn_up.shape[1]
    groups = tp // 2
    device = jnp.stack([b, t]).astype(jnp.int32)
    plane = [[2 * c + k for c in range(chips)] for k in range(2)]
    chip = b // 2
    all_chips = jnp.arange(chips, dtype=jnp.int32)
    near_chips = chip ^ jnp.arange(chips, dtype=jnp.int32)

    def swapped(size, j):
        return [(i, i ^ j) for i in range(size)]

    def of_rank(values, rank):
        return lax.dynamic_slice_in_dim(values, rank * mine, mine, 0)

    def norm_rows(i):
        return jnp.stack([norm_gain[i], norm_bias[i]])

    def at(values, i):
        return lax.dynamic_index_in_dim(values, i, 0, keepdims=False)

    def from_ranks(values):
        return [values[0]] + [
            lax.ppermute(values[j], "tp", swapped(tp, j)) for j in range(1, tp)
        ]

    def over_chips(blocks):
        return lax.all_to_all(blocks, "blk", 0, 0, axis_index_groups=plane)

    def other_core(values):
        return lax.ppermute(values, "blk", swapped(blk, 1))

    def spread(w):
        near = over_chips(jnp.broadcast_to(w, (chips,) + w.shape))
        return near, other_core(near)

    def weight_grads(sums, order, apart, deps=(), later=()):
        sums = [
            [(left, r if isinstance(r, tuple) else (r, 0, r.shape[1])) for left, r in terms]
            for terms in sums
        ]
        send = weight_grad_blocks(2 * order + 1 - core, sums, share, deps=deps)
        return weight_grad_blocks(
            2 * order + core, sums, share, other_core(send), apart=apart, deps=later
        )

    def from_chips(blocks):
        return [blocks[0]] + [
            lax.ppermute(blocks[j], "blk", swapped(blk, 2 * j)) for j in range(1, chips)
        ]

    def added(values):
        total = values[0].astype(F32)
        for v in values[1:]:
            total += v.astype(F32)
        return total

    def over_ranks(total):
        parts, _, c = total.shape
        split = total.astype(BF).reshape(parts, share, tp, c // tp).transpose(2, 0, 1, 3)
        return added(from_ranks([at(split, t ^ j) for j in range(tp)]))

    def share_rows(w):
        return lax.dynamic_slice_in_dim(w, b * share, share, w.ndim - 2)

    def share_cols(w):
        return lax.dynamic_slice_in_dim(w, b * share, share, 1).T

    mem = share_rows(cross_mem)
    shared = [mem[0], mem[1], share_cols(self_out), share_rows(cross_query), share_cols(cross_out)]
    shared = jnp.concatenate(shared, axis=1)
    piece = jnp.concatenate([share_rows(ffn_up), share_cols(ffn_down)], axis=1)

    padded = frames
    if slices * group > streams:
        padded = jnp.pad(frames, ((0, slices * group - streams), (0, 0), (0, 0)))
    pieces, h_all = qkv_pieces(
        padded, norm_rows(0), self_proj, slices, per, width, deps=(shared, piece)
    )
    qkv = lax.all_to_all(pieces.reshape(blk, group, rows, 3 * width), "blk", 0, 0)
    all_ends = jnp.cumsum(clip_lengths, axis=1).astype(jnp.int32)
    ends = of_rank(all_ends, t)
    own_ends = jnp.pad(all_ends, ((0, slices * group - streams), (0, 0)))
    own_ends = lax.dynamic_slice_in_dim(own_ends, b // per * group, group, 0)
    shared = lax.all_gather(shared, "tp")
    attn_own = self_attention(
        own_ends, [qkv], width, self_forward_kernel, width, 0, "self_forward"
    )
    even = slices == tp and group == mine

    attn_rows = lax.all_to_all(attn_own, "blk", 0, 0)
    if even:
        attn = attn_rows.reshape(tp, per, count, width)
    else:
        attn = attn_rows.reshape(slices, per, group, rows, width).transpose(0, 2, 1, 3, 4)
        attn = attn.reshape(slices * group, per, rows, width)[:streams]
        attn = attn.reshape(tp, mine, per, rows, width).transpose(0, 2, 1, 3, 4)
        attn = attn.reshape(tp, per, count, width)
    attn = from_ranks([at(attn, t ^ j) for j in range(tp)])

    weights = spread(tied(shared, *attn))
    w_mem = columns(weights, 2 * local, 0)
    w_first = columns(weights, 2 * local, 1)
    w_cross_out = columns(weights, local, 4)
    piece = tied(piece, *attn)
    pieces_of = [lax.ppermute(piece, "tp", swapped(tp, 2 * j)) for j in range(1, groups)]
    ffn_others = [
        lax.all_gather(tied(p, weights[0]), "blk", axis=0, tiled=True) for p in pieces_of
    ]

    info = jnp.concatenate(
        [
            ends,
            of_rank(text_lengths, t),
            jnp.full((mine, 1), b * rows, jnp.int32),
            jnp.full((mine, 1), b, jnp.int32),
            jnp.full((mine, 1), t, jnp.int32),
        ],
        axis=1,
    )
    x = of_rank(frames, t).reshape(count, model)
    flat = struct((count, model))
    wide = struct((count, model), F32)
    x2, h2, cq, attn = call(
        first_kernel,
        "to_cross",
        (1,),
        [
            (x, None),
            (norm_rows(1), None),
            *w_first,
            *[(a, None) for a in attn],
        ],
        [(wide, None), (flat, None), (flat, None), (flat, None)],
        scalars=(device,),
        scratch=[pltpu.VMEM((model, 2 * model), BF)],
        deps=pieces_of,
        flops=4 * count * model * model,
    )
    texts = of_rank(text_states, t).reshape(mine * text_rows, model)
    tile = model // 2
    (ckv,) = call(
        memory_kernel,
        "memory",
        (4,),
        [
            (texts, None),
            *[
                (
                    w,
                    pl.BlockSpec(
                        (chips, tp // 2, share, local), lambda i, _: (0, i % 2, 0, i // 2)
                    ),
                )
                for w in weights
            ],
        ],
        [
            (
                struct((mine * text_rows, 2 * model)),
                pl.BlockSpec((mine * text_rows, tile), lambda i, _: (0, i)),
            )
        ],
        scalars=(device,),
        scratch=[pltpu.VMEM((model, tile), BF)],
        deps=(cq,),
        flops=4 * texts.shape[0] * model * model,
    )
    ckv = ckv.reshape(mine, text_rows, 2 * model)
    kv_spec = pl.BlockSpec((1, text_rows, 2 * model), lambda s, *_: (s, 0, 0))
    cross_work = count * (model // HEAD_DIM) * text_rows
    cattn, x3, h3 = call(
        functools.partial(second_kernel, slots=slots, rows=rows),
        "cross_forward",
        (mine,),
        [
            (x2, None),
            (cq, None),
            (ckv, kv_spec),
            (norm_rows(2), None),
            *w_cross_out,
        ],
        [(flat, None), (wide, None), (flat, None)],
        scalars=(info,),
        scratch=[pltpu.VMEM((model, model), BF)],
        flops=2 * count * model * model + 4 * cross_work * HEAD_DIM,
        exps=cross_work,
    )

    swap = swapped(tp, 1)
    h3_other = lax.ppermute(h3, "tp", swap)
    ct = of_rank(cotangent, t).reshape(count, model)
    ct_other = of_rank(cotangent, t ^ 1).reshape(count, model)
    own_weights = (ffn_up, ffn_down)
    act_other, d_up_other, d_h3_other, out_other = feed_forward(
        h3_other, ct_other, own_weights, ffn_others, hidden, BF
    )
    d_h3_got = lax.ppermute(d_h3_other, "tp", swap)
    act, d_up, d_h3, out = feed_forward(
        h3, ct, own_weights, ffn_others, hidden, F32, deps=(out_other,)
    )
    out_got = lax.ppermute(tied(out_other, d_h3_got), "tp", swap)
    out = x3 + out + out_got.astype(F32)

    ffn_blocks = weight_grads(
        [[(h3, d_up), (h3_other, d_up_other)], [(ct, act), (ct_other, act_other)]],
        all_chips,
        False,
        deps=(d_h3_got,),
    )
    ffn_got = over_chips(ffn_blocks)
    g_ffn = jnp.sum(ffn_got.astype(F32), axis=0)
    split = g_ffn.reshape(2, share, groups, hidden)

    d_c, d_cq, d_x2, d_a, d_attn, d_ckv, early = call(
        functools.partial(third_kernel, slots=slots, rows=rows),
        "cross_backward",
        (mine,),
        [
            (d_h3, None),
            (d_h3_got, None),
            (x3, None),
            (ct, None),
            (x2, None),
            (cq, None),
            (ckv, kv_spec),
            (norm_gain, None),
            *w_first,
            *w_cross_out,
        ],
        [
            (flat, None),
            (flat, None),
            (wide, None),
            (flat, None),
            (struct((tp, per, count, width)), None),
            (struct(ckv.shape), kv_spec),
            (struct((4, model), F32), None),
        ],
        scalars=(info,),
        scratch=[
            pltpu.VMEM((count, model), F32),
            pltpu.VMEM((count, model), BF),
            pltpu.VMEM((model, 2 * model), BF),
            pltpu.VMEM((model, model), BF),
        ],
        deps=(ffn_blocks,),
        flops=6 * count * model * model + 10 * cross_work * HEAD_DIM,
        exps=cross_work,
    )

    d_attn = from_ranks([d_attn[j] for j in range(tp)])
    attn_blocks = weight_grads(
        [[(d_a, attn)], [(h2, d_cq)], [(d_c, cattn)]], near_chips, True, deps=(d_attn[-1],)
    )

    d_attn = jnp.stack(d_attn)[jnp.arange(tp) ^ t]
    if not even:
        d_attn = d_attn.reshape(tp, per, mine, rows, width).transpose(0, 2, 1, 3, 4)
        d_attn = d_attn.reshape(streams, per, rows, width)
        d_attn = jnp.pad(d_attn, ((0, slices * group - streams), (0, 0), (0, 0), (0, 0)))
        d_attn = d_attn.reshape(slices, group, per, rows, width).transpose(0, 2, 1, 3, 4)
    d_attn = d_attn.reshape(blk, group, rows, width)
    d_attn = lax.all_to_all(tied(d_attn, ffn_got), "blk", 0, 0)
    d_qkv_own = self_attention(
        own_ends,
        [qkv, d_attn],
        width,
        self_backward_kernel,
        3 * width,
        2,
        "self_backward",
        deps=(out_got, attn_blocks[0]),
    )
    out_all = lax.all_gather(out.astype(BF), "tp", axis=0, tiled=True)

    part = mine * text_rows // blk
    d_ckv = d_ckv.reshape(chips, 2, part, 2 * model)
    received = other_core(lax.dynamic_index_in_dim(d_ckv, 1 - core, 1, keepdims=False))
    d_ckv = lax.dynamic_index_in_dim(d_ckv, core, 1, keepdims=False).astype(F32)
    d_ckv = tied((d_ckv + received.astype(F32)).astype(BF), d_attn)
    d_ckv = jnp.sum(over_chips(d_ckv).astype(F32), axis=0).astype(BF)

    d_qkv = lax.all_to_all(tied(d_qkv_own, d_ckv), "blk", 0, 0)
    texts = lax.dynamic_slice_in_dim(texts, b * part, part, 0)
    (d_text,) = call(
        text_grad_kernel,
        "text_grad",
        (1,),
        [(d_ckv, None), *w_mem],
        [(struct((part, model)), None)],
        scalars=(device,),
        scratch=[pltpu.VMEM((model, 2 * model), BF)],
        deps=(d_qkv_own,),
        flops=4 * part * model * model,
    )
    d_text = jnp.stack(from_ranks([d_text] * tp))[jnp.arange(tp) ^ t]

    d_qkv = d_qkv.reshape(slices, per, group * rows, 3 * width)
    padded_rows = slices * group * rows
    parts, d_qkv = call(
        qkv_grad_kernel,
        "qkv_grad",
        (slices,),
        [
            (d_qkv, pl.BlockSpec((1,) + d_qkv.shape[1:], lambda i: (i, 0, 0, 0))),
            (self_proj, None),
        ],
        [
            (
                struct((slices, group * rows, model)),
                pl.BlockSpec((1, group * rows, model), lambda i: (i, 0, 0)),
            ),
            (
                struct((padded_rows, 3 * local)),
                pl.BlockSpec((group * rows, 3 * local), lambda i: (i, 0)),
            ),
        ],
        deps=(d_text,),
        flops=6 * padded_rows * model * local,
    )
    parts_own = parts.reshape(padded_rows, model)[: streams * rows].reshape(tp, count, model)
    parts = lax.all_to_all(parts_own, "tp", 0, 0)
    qkv_blocks = weight_grads(
        [[(h_all, d_qkv)]], near_chips, True, deps=(parts_own,)
    )
    qkv_got = from_chips(qkv_blocks)
    mem_blocks = weight_grads(
        [[(texts, (d_ckv, 0, model))], [(texts, (d_ckv, model, model))]],
        near_chips,
        True,
        deps=(parts_own,),
    )
    mem_got = from_chips(mem_blocks)
    attn_got = from_chips([tied(w, d_qkv) for w in attn_blocks])

    d_x, late = call(
        last_kernel,
        "to_frames",
        (1,),
        [(parts, None), (x, None), (d_x2, None), (norm_rows(0), None)],
        [(struct((tp, count, model)), None), (struct((2, model), F32), None)],
        deps=(*attn_got[1:], qkv_blocks[0], mem_blocks[0]),
        flops=20 * count * model,
    )
    grad_frames = lax.all_to_all(d_x, "tp", 0, 0).reshape(streams, rows, model).astype(F32)

    ffn_total = split[:, :, 0]
    ffn_back = [
        lax.ppermute(tied(split[:, :, j].astype(BF), d_x), "tp", swapped(tp, 2 * j)) for j in range(1, groups)
    ]
    for back in ffn_back:
        ffn_total += back.astype(F32)
    grad_ffn_up = ffn_total[0]
    grad_ffn_down = ffn_total[1].T
    g_attn_own = over_ranks(tied(added(attn_got), d_x))
    grad_cross_mem = over_ranks(added(mem_got))
    grad_self_out = g_attn_own[0].T
    grad_cross_query = g_attn_own[1]
    grad_cross_out = g_attn_own[2].T
    (g_qkv,) = added(qkv_got)
    grad_self_proj = g_qkv.reshape(share, 3, local).transpose(1, 0, 2)

    d_text = lax.all_gather(d_text, "blk")
    if part % 16:
        d_text = d_text.transpose(1, 0, 2, 3)
        grad_text = d_text.reshape(streams, slots, text, model).astype(F32)
    else:
        (grad_text,) = call(
            text_kernel,
            "text_out",
            (tp,),
            [(d_text, pl.BlockSpec((blk, 1, part, model), lambda i: (0, i, 0, 0)))],
            [
                (
                    struct((tp, mine * text_rows, model), F32),
                    pl.BlockSpec((1, mine * text_rows, model), lambda i: (i, 0, 0)),
                )
            ],
        )
        grad_text = grad_text.reshape(streams, slots, text, model)

    sums = jnp.concatenate([early, late], axis=0)
    for axis, size in (("blk", blk), ("tp", tp)):
        step = 1
        while step < size:
            sums = sums + lax.ppermute(sums, axis, swapped(size, step))
            step *= 2
    sums = lax.dynamic_slice_in_dim(sums, b * share, share, 1)
    grad_gain = jnp.stack([sums[4], sums[0], sums[1]])
    grad_bias = jnp.stack([sums[5], sums[2], sums[3]])

    out_frames = out_all.reshape(streams, rows, model).astype(F32)

    return (
        out_frames,
        grad_frames,
        grad_text,
        grad_gain,
        grad_bias,
        grad_self_proj,
        grad_self_out,
        grad_cross_query,
        grad_cross_mem,
        grad_cross_out,
        grad_ffn_up,
        grad_ffn_down,
    )


def solution(mesh):
    in_specs = (
        P(None, "blk", None),
        P(),
        P(),
        P(),
        P(None, "blk", None),
        P(),
        P(),
        P(None, None, "tp"),
        P("tp", None),
        P(None, "tp"),
        P(None, None, "tp"),
        P("tp", None),
        P(None, "tp"),
        P("tp", None),
    )
    out_specs = (
        P(None, "blk", None),
        P(None, "blk", None),
        P(),
        P(None, "blk"),
        P(None, "blk"),
        P(None, "blk", "tp"),
        P("tp", "blk"),
        P("blk", "tp"),
        P(None, "blk", "tp"),
        P("tp", "blk"),
        P("blk", "tp"),
        P("tp", "blk"),
    )
    return jax.shard_map(shards, mesh=mesh, in_specs=in_specs, out_specs=out_specs, check_vma=False)
```

```python
import functools

import jax
import jax.numpy as jnp
from jax import lax
from jax.experimental import pallas as pl
from jax.experimental.pallas import tpu as pltpu
from jax.sharding import PartitionSpec as P

HEAD_DIM = 64
SCALE = 0.125
MASKED = -1e30
EPS = 1e-05
LANES = 128
BF = jnp.bfloat16
F32 = jnp.float32
MIB = 1 << 20

NN = ((1,), (0,))
NT = ((1,), (1,))
TN = ((0,), (0,))


def dot(a, b, dims):
    return lax.dot_general(a, b, (dims, ((), ())), preferred_element_type=F32)


def whole_spec(array):
    zeros = (0,) * len(array.shape)
    return pl.BlockSpec(tuple(array.shape), lambda *_: zeros)


def call(kernel, name, grid, ins, outs, scalars=(), scratch=(), deps=(), flops=0, exps=0):
    count = len(ins)

    def body(*refs):
        kept = len(scalars) + count
        kernel(*refs[:kept], *refs[kept + len(deps) :])

    specs = [whole_spec(a) if s is None else s for a, s in ins]
    specs += [pl.BlockSpec(memory_space=pl.ANY)] * len(deps)
    moved = sum(a.size * a.dtype.itemsize for a, _ in (*ins, *outs))
    return pl.pallas_call(
        body,
        out_shape=[o for o, _ in outs],
        grid_spec=pltpu.PrefetchScalarGridSpec(
            num_scalar_prefetch=len(scalars),
            grid=grid,
            in_specs=specs,
            out_specs=[whole_spec(o) if s is None else s for o, s in outs],
            scratch_shapes=list(scratch),
        ),
        compiler_params=pltpu.CompilerParams(vmem_limit_bytes=56 * MIB),
        cost_estimate=pl.CostEstimate(flops=flops, bytes_accessed=moved, transcendentals=exps),
        name=name,
    )(*scalars, *[a for a, _ in ins], *deps)


def struct(shape, dtype=BF):
    return jax.ShapeDtypeStruct(tuple(shape), dtype)


def assemble(whole_ref, near_ref, far_ref, device, parts=1):
    chips, ranks, share, cols = near_ref.shape
    c = cols // parts
    core = device % 2
    for chip in range(chips):
        for ref, k in ((near_ref, core), (far_ref, 1 - core)):
            rows = pl.ds(pl.multiple_of((2 * chip + k) * share, share), share)
            for p in range(parts):
                for r in range(ranks):
                    to = (p * ranks + r) * c
                    whole_ref[rows, to : to + c] = ref[chip, r, :, p * c : (p + 1) * c]


def columns(pair, size, place):
    return [
        (w, pl.BlockSpec(w.shape[:3] + (size,), lambda *_: (0, 0, 0, place))) for w in pair
    ]


def normalize(values):
    centre = values - jnp.mean(values, axis=-1, keepdims=True)
    inverse = lax.rsqrt(jnp.mean(centre * centre, axis=-1, keepdims=True) + EPS)
    return centre * inverse, inverse


def normed(values, gain, bias):
    return (normalize(values)[0] * gain + bias).astype(BF)


def norm_backward(values, gain, upstream):
    normal, inverse = normalize(values)
    g = upstream * gain
    mean_g = jnp.mean(g, axis=-1, keepdims=True)
    mean_gn = jnp.mean(g * normal, axis=-1, keepdims=True)
    d_values = inverse * (g - mean_g - normal * mean_gn)
    gain_sum = jnp.sum(upstream * normal, axis=0, keepdims=True)
    return d_values, gain_sum, jnp.sum(upstream, axis=0, keepdims=True)


def head_masks(width):
    lane = lax.broadcasted_iota(jnp.int32, (1, width), 1) // HEAD_DIM
    return [lane == h for h in range(width // HEAD_DIM)]


def pick(mask, values):
    return jnp.where(mask, values, jnp.zeros_like(values))


def stacked_heads(values):
    return jnp.concatenate([pick(m, values) for m in head_masks(values.shape[1])], axis=0)


def merged_heads(values, rows):
    total = values[:rows]
    for h, mask in enumerate(head_masks(values.shape[1])):
        if h:
            total = jnp.where(mask, values[h * rows : (h + 1) * rows], total)
    return total


def softmax(scores, allowed):
    scores = jnp.where(allowed, scores, MASKED)
    weights = jnp.exp(scores - jnp.max(scores, axis=1, keepdims=True))
    return weights * (1.0 / jnp.sum(weights, axis=1, keepdims=True))


def qkv_kernel(x_ref, norm_ref, w_ref, out_ref, h_ref):
    width = out_ref.shape[3] // 3
    x = x_ref[...].reshape(-1, x_ref.shape[-1]).astype(F32)
    h = normed(x, norm_ref[0:1], norm_ref[1:2])
    h_ref[...] = h
    for k in range(3):
        result = dot(h, w_ref[k], NN).astype(BF)
        for p in range(out_ref.shape[1]):
            out_ref[0, p, :, k * width : (k + 1) * width] = result[:, p * width : (p + 1) * width]


def qkv_pieces(frames, norm, weights, slices, parts, width, deps=()):
    streams, rows, model = frames.shape
    group = streams // slices
    out = struct((slices, parts, group * rows, 3 * width))
    return call(
        qkv_kernel,
        "qkv",
        (slices,),
        [
            (frames, pl.BlockSpec((group, rows, model), lambda i: (i, 0, 0))),
            (norm, None),
            (weights, None),
        ],
        [
            (out, pl.BlockSpec((1,) + out.shape[1:], lambda i: (i, 0, 0, 0))),
            (
                struct((streams * rows, model)),
                pl.BlockSpec((group * rows, model), lambda i: (i, 0)),
            ),
        ],
        deps=deps,
        flops=2 * streams * rows * weights.size,
    )


def qkv_grad_kernel(grad_ref, w_ref, out_ref, merged_ref):
    parts, width = grad_ref.shape[1], grad_ref.shape[3] // 3
    local = parts * width
    for p in range(parts):
        for k in range(3):
            to = k * local + p * width
            merged_ref[:, to : to + width] = grad_ref[0, p, :, k * width : (k + 1) * width]
    total = 0.0
    for k in range(3):
        total += dot(merged_ref[:, k * local : (k + 1) * local], w_ref[k], NT)
    out_ref[0] = total.astype(BF)


def first_norm_kernel(parts_ref, x_ref, sums_ref):
    d_h1 = parts_ref[0].astype(F32)
    normal, _ = normalize(x_ref[0].astype(F32))
    sums = [jnp.sum(d_h1 * normal, axis=0, keepdims=True), jnp.sum(d_h1, axis=0, keepdims=True)]

    @pl.when(pl.program_id(0) == 0)
    def _():
        sums_ref[...] = jnp.zeros_like(sums_ref)

    sums_ref[...] += jnp.concatenate(sums, axis=0)


def last_kernel(parts_ref, x_ref, dx2_ref, norm_ref, dx_ref):
    d_h1 = parts_ref[0].astype(F32)
    for r in range(1, parts_ref.shape[0]):
        d_h1 += parts_ref[r].astype(F32)
    d_v, _, _ = norm_backward(x_ref[...].astype(F32), norm_ref[0:1], d_h1)
    d_x = (dx2_ref[...] + d_v).astype(BF)
    for r in range(dx_ref.shape[0]):
        dx_ref[r] = d_x


def causal_probs(ends_ref, stream, slots, q, k, first):
    block = q.shape[0]
    rows = first + lax.broadcasted_iota(jnp.int32, (block, 1), 0)
    begin = jnp.zeros((block, 1), jnp.int32)
    for c in range(slots):
        end = ends_ref[stream, c]
        begin = jnp.where(rows >= end, jnp.maximum(begin, end), begin)
    cols = lax.broadcasted_iota(jnp.int32, (block, k.shape[0]), 1)
    return softmax(dot(q, k, NT), (cols <= rows) & (cols >= begin))


def self_forward_kernel(ends_ref, qkv_ref, out_ref, *, slots, width, block):
    stream = pl.program_id(0)
    parts, _, rows, _ = qkv_ref.shape
    length = parts * rows
    qkv = qkv_ref[...].reshape(length, 3 * width)
    q = qkv[:, :width] * jnp.asarray(SCALE, BF)
    k = qkv[:, width : 2 * width]
    v = qkv[:, 2 * width :]
    masks = head_masks(width)
    q_of = [pick(m, q) for m in masks]
    v_of = [pick(m, v) for m in masks]
    per = block // rows
    firsts = range(0, length, block)
    pairs = [(h, first) for first in firsts for h in range(len(masks))]
    probs = [
        causal_probs(
            ends_ref, stream, slots, q_of[h][first : first + block], k[: first + block], first
        ).astype(BF)
        for h, first in pairs
    ]
    results = [
        dot(p, v_of[h][: first + block], NN) for p, (h, first) in zip(probs, pairs)
    ]
    for first in firsts:
        total = sum(r for r, (_, f) in zip(results, pairs) if f == first)
        at = first // rows
        out_ref[at : at + per, 0] = total.astype(BF).reshape(per, rows, width)


def self_backward_kernel(ends_ref, qkv_ref, grad_ref, out_ref, dk_ref, dv_ref, *, slots, width, block):
    stream = pl.program_id(0)
    parts, _, rows, _ = qkv_ref.shape
    length = parts * rows
    qkv = qkv_ref[...].reshape(length, 3 * width)
    q = qkv[:, :width] * jnp.asarray(SCALE, BF)
    k = qkv[:, width : 2 * width]
    v = qkv[:, 2 * width :]
    grad = grad_ref[...].reshape(length, width)
    masks = head_masks(width)
    q_of = [pick(m, q) for m in masks]
    k_of = [pick(m, k) for m in masks]
    g_of = [pick(m, grad) for m in masks]
    dk_ref[...] = jnp.zeros_like(dk_ref)
    dv_ref[...] = jnp.zeros_like(dv_ref)
    per = block // rows
    for first in range(0, length, block):
        top = first + block
        dq = jnp.zeros((block, width), F32)
        for h in range(len(masks)):
            q_part = q_of[h][first:top]
            g_part = g_of[h][first:top]
            probs = causal_probs(ends_ref, stream, slots, q_part, k[:top], first)
            d_probs = dot(g_part, v[:top], NT)
            delta = jnp.sum(probs * d_probs, axis=1, keepdims=True)
            d_scores = (probs * (d_probs - delta)).astype(BF)
            dq += dot(d_scores, k_of[h][:top], NN)
            dk_ref[:top] += dot(d_scores, q_part, TN)
            dv_ref[:top] += dot(probs.astype(BF), g_part, TN)
        at = first // rows
        out_ref[at : at + per, 0, :, :width] = (dq * SCALE).astype(BF).reshape(per, rows, width)
    out_ref[:, 0, :, width : 2 * width] = dk_ref[...].astype(BF).reshape(parts, rows, width)
    out_ref[:, 0, :, 2 * width :] = dv_ref[...].astype(BF).reshape(parts, rows, width)


def self_attention(ends, arrays, width, kernel, out_width, scratch, name, deps=()):
    parts, streams, rows, _ = arrays[0].shape
    length = parts * rows
    block = min(length, rows * max(1, 256 // rows))
    work = streams * (width // HEAD_DIM) * length * length

    def spec(c):
        return pl.BlockSpec((parts, 1, rows, c), lambda s, *_: (0, s, 0, 0))

    out = struct((parts, streams, rows, out_width))
    return call(
        functools.partial(kernel, slots=ends.shape[1], width=width, block=block),
        name,
        (streams,),
        [(a, spec(a.shape[3])) for a in arrays],
        [(out, spec(out_width))],
        scalars=(ends,),
        scratch=[pltpu.VMEM((length, width), F32)] * scratch,
        deps=deps,
        flops=4 * len(arrays) * work * HEAD_DIM,
        exps=work,
    )[0]


def first_kernel(device_ref, x_ref, norm_ref, near_ref, far_ref, *refs):
    pieces, (x2_ref, h2_ref, cq_ref, attn_out_ref, w_ref) = refs[:-5], refs[-5:]
    model = x2_ref.shape[1]
    assemble(w_ref, near_ref, far_ref, device_ref[0], 2)
    for j, ref in enumerate(pieces):
        piece = jnp.concatenate([ref[p] for p in range(ref.shape[0])], axis=1)
        local = piece.shape[1]
        to = pl.multiple_of((device_ref[1] ^ j) * local, local)
        attn_out_ref[:, pl.ds(to, local)] = piece
    attn = attn_out_ref[...]
    x2 = x_ref[...].astype(F32) + dot(attn, w_ref[:, :model], NT)
    x2_ref[...] = x2
    h2 = normed(x2, norm_ref[0:1], norm_ref[1:2])
    h2_ref[...] = h2
    cq_ref[...] = dot(h2, w_ref[:, model:], NN).astype(BF)


def memory_kernel(device_ref, text_ref, near_ref, far_ref, out_ref, w_ref):
    assemble(w_ref, near_ref, far_ref, device_ref[0])
    out_ref[...] = dot(text_ref[...], w_ref[...], NN).astype(BF)


def text_grad_kernel(device_ref, rows_ref, near_ref, far_ref, out_ref, w_ref):
    assemble(w_ref, near_ref, far_ref, device_ref[0], 2)
    out_ref[...] = dot(rows_ref[...], w_ref[...], NT).astype(BF)


def cross_allowed(info_ref, stream, slots, rows, keys):
    text = keys // slots
    pos = info_ref[stream, 2 * slots] + lax.broadcasted_iota(jnp.int32, (rows, 1), 0)
    clip = jnp.zeros((rows, 1), jnp.int32)
    for c in range(slots):
        clip += jnp.where(pos >= info_ref[stream, c], 1, 0)
    begin = clip * text
    count = jnp.zeros((rows, 1), jnp.int32)
    for c in range(slots):
        count = jnp.where(clip == c, info_ref[stream, slots + c], count)
    key = lax.broadcasted_iota(jnp.int32, (rows, keys), 1)
    return (key >= begin) & (key < begin + count)


CROSS_LANES = 256


def second_kernel(
    info_ref, x2_ref, cq_ref, kv_ref, norm_ref, near_ref, far_ref, *refs, slots, rows
):
    cattn_ref, x3_ref, h3_ref, wo_ref = refs
    stream = pl.program_id(0)
    model = x2_ref.shape[1]
    keys = kv_ref.shape[1]
    mine = pl.ds(pl.multiple_of(stream * rows, rows), rows)
    once = cross_allowed(info_ref, stream, slots, rows, keys)
    allowed = jnp.concatenate([once] * (CROSS_LANES // HEAD_DIM), axis=0)
    every = [slice(at, at + CROSS_LANES) for at in range(0, model, CROSS_LANES)]
    q = [stacked_heads(cq_ref[mine, c] * jnp.asarray(SCALE, BF)) for c in every]
    scores = [dot(a, kv_ref[0, :, c], NT) for a, c in zip(q, every)]
    probs = [softmax(a, allowed).astype(BF) for a in scores]
    values = [kv_ref[0, :, model + c.start : model + c.stop] for c in every]
    results = [dot(a, v, NN) for a, v in zip(probs, values)]
    for c, a in zip(every, results):
        cattn_ref[mine, c] = merged_heads(a, rows).astype(BF)

    @pl.when(stream == pl.num_programs(0) - 1)
    def _():
        assemble(wo_ref, near_ref, far_ref, info_ref[0, 2 * slots + 1])
        x3 = x2_ref[...] + dot(cattn_ref[...], wo_ref[...], NT)
        x3_ref[...] = x3
        h3_ref[...] = normed(x3, norm_ref[0:1], norm_ref[1:2])


def third_kernel(
    info_ref,
    dh_ref,
    received_ref,
    x3_ref,
    ct_ref,
    x2_ref,
    cq_ref,
    kv_ref,
    gain_ref,
    near1_ref,
    far1_ref,
    near2_ref,
    far2_ref,
    dc_ref,
    dcq_ref,
    dx2_ref,
    da_ref,
    dattn_ref,
    dkv_ref,
    sums_ref,
    dx3_ref,
    dcattn_ref,
    w_first_ref,
    w_cross_ref,
    *,
    slots,
    rows,
):
    device = info_ref[0, 2 * slots + 1]
    stream = pl.program_id(0)
    model = x2_ref.shape[1]
    keys = kv_ref.shape[1]

    @pl.when(stream == 0)
    def _():
        d_h3 = dh_ref[...] + received_ref[0].astype(F32)
        d_v, gain, bias = norm_backward(x3_ref[...], gain_ref[2:3], d_h3)
        sums_ref[1:2] = gain
        sums_ref[3:4] = bias
        d_x3 = ct_ref[...].astype(F32) + d_v
        dx3_ref[...] = d_x3
        d_c = d_x3.astype(BF)
        dc_ref[...] = d_c
        assemble(w_cross_ref, near2_ref, far2_ref, device)
        dcattn_ref[...] = dot(d_c, w_cross_ref[...], NN).astype(BF)

    mine = pl.ds(pl.multiple_of(stream * rows, rows), rows)
    once = cross_allowed(info_ref, stream, slots, rows, keys)
    allowed = jnp.concatenate([once] * (CROSS_LANES // HEAD_DIM), axis=0)
    every = [slice(at, at + CROSS_LANES) for at in range(0, model, CROSS_LANES)]
    k = [kv_ref[0, :, c] for c in every]
    v = [kv_ref[0, :, model + c.start : model + c.stop] for c in every]
    q = [stacked_heads(cq_ref[mine, c] * jnp.asarray(SCALE, BF)) for c in every]
    grad = [stacked_heads(dcattn_ref[mine, c]) for c in every]
    scores = [dot(a, b, NT) for a, b in zip(q, k)]
    d_probs = [dot(a, b, NT) for a, b in zip(grad, v)]
    probs = [softmax(a, allowed) for a in scores]
    delta = [jnp.sum(a * b, axis=1, keepdims=True) for a, b in zip(probs, d_probs)]
    d_scores = [(a * (b - c)).astype(BF) for a, b, c in zip(probs, d_probs, delta)]
    d_q = [dot(a, b, NN) for a, b in zip(d_scores, k)]
    d_k = [dot(a, b, TN) for a, b in zip(d_scores, q)]
    d_v = [dot(a.astype(BF), b, TN) for a, b in zip(probs, grad)]
    for i, c in enumerate(every):
        dcq_ref[mine, c] = (merged_heads(d_q[i], rows) * SCALE).astype(BF)
        dkv_ref[0, :, c] = d_k[i].astype(BF)
        dkv_ref[0, :, model + c.start : model + c.stop] = d_v[i].astype(BF)

    @pl.when(stream == pl.num_programs(0) - 1)
    def _():
        assemble(w_first_ref, near1_ref, far1_ref, device, 2)
        d_h2 = dot(dcq_ref[...], w_first_ref[:, model:], NT)
        d_v, gain, bias = norm_backward(x2_ref[...], gain_ref[1:2], d_h2)
        sums_ref[0:1] = gain
        sums_ref[2:3] = bias
        d_x2 = dx3_ref[...] + d_v
        dx2_ref[...] = d_x2
        d_a = d_x2.astype(BF)
        da_ref[...] = d_a
        d_attn = dot(d_a, w_first_ref[:, :model], NN).astype(BF)
        ranks, parts, _, width = dattn_ref.shape
        for p in range(ranks * parts):
            to = (p // parts) ^ info_ref[0, 2 * slots + 2]
            dattn_ref[to, p % parts] = d_attn[:, p * width : (p + 1) * width]


def ffn_kernel(h_ref, ct_ref, *refs, groups, tiles):
    (act_ref, dup_ref), results = refs[2 * groups : 2 * groups + 2], refs[2 * groups + 2 : -2]
    dh_acc, out_acc = refs[-2:]
    step = pl.program_id(0)

    @pl.when(step == 0)
    def _():
        dh_acc[...] = jnp.zeros_like(dh_acc)
        out_acc[...] = jnp.zeros_like(out_acc)

    for g in range(groups):

        @pl.when(step // tiles == g)
        def _(g=g):
            w_up, w_down = refs[2 * g][...], refs[2 * g + 1][...]
            into, out_of = (NN, NT) if g else (NT, NN)
            up = dot(h_ref[...], w_up, NN)
            d_act = dot(ct_ref[...], w_down, into)
            cdf = 0.5 * (1.0 + lax.erf(up * (0.5**0.5)))
            slope = cdf + up * jnp.exp(-0.5 * up * up) * 0.3989422804014327
            act = (up * cdf).astype(BF)
            d_up = (d_act * slope).astype(BF)
            act_ref[...] = act
            dup_ref[...] = d_up
            dh_acc[...] += dot(d_up, w_up, NT)
            out_acc[...] += dot(act, w_down, out_of)

    @pl.when(step == groups * tiles - 1)
    def _():
        if len(results) == 2:
            results[0][...] = dh_acc[...]
            results[1][...] = out_acc[...]
        else:
            results[0][0] = dh_acc[...].astype(BF)
            results[0][1] = out_acc[...].astype(BF)


def feed_forward(h, ct, own, others, hidden, paired, deps=()):
    count, model = h.shape
    groups = 1 + len(others)
    tile = min(hidden, 512)
    tiles = hidden // tile

    def place(g):
        return lambda i: jnp.clip(i - g * tiles, 0, tiles - 1)

    ins = [(h, None), (ct, None)]
    ins.append((own[0], pl.BlockSpec((model, tile), lambda i: (0, place(0)(i)))))
    ins.append((own[1], pl.BlockSpec((tile, model), lambda i: (place(0)(i), 0))))
    for g, w in enumerate(others, 1):
        for first in (0, tiles):
            spec = pl.BlockSpec((model, tile), lambda i, g=g, f=first: (0, f + place(g)(i)))
            ins.append((w, spec))
    wide = struct((count, groups * hidden))
    results = [(struct((count, model), F32), None)] * 2
    if paired:
        results = [(struct((2, count, model)), None)]
    column = pl.BlockSpec((count, tile), lambda i: (0, i))
    return call(
        functools.partial(ffn_kernel, groups=groups, tiles=tiles),
        "feed_forward",
        (groups * tiles,),
        ins,
        [(wide, column), (wide, column), *results],
        scratch=[pltpu.VMEM((count, model), F32)] * 2,
        deps=deps,
        flops=8 * count * model * groups * hidden,
        exps=2 * count * groups * hidden,
    )


def weight_grad_kernel(index_ref, *refs, sums, chips, plus, apart):
    outs = refs[-chips:] if apart else [refs[-1].at[j] for j in range(chips)]
    at = 0
    for p, terms in enumerate(sums):
        total = 0.0
        for _ in range(terms):
            left = jnp.concatenate([r[...] for r in refs[at : at + chips]], axis=1)
            total += dot(left, refs[at + chips][...], TN)
            at += chips + 1
        share = total.shape[0] // chips
        for j in range(chips):
            block = total[j * share : (j + 1) * share]
            if plus:
                block += refs[sum(sums) * (chips + 1) + j][p].astype(F32)
            outs[j][p] = block.astype(BF)


def weight_grad_blocks(index, sums, share, plus=None, apart=False, deps=()):
    model = sums[0][0][0].shape[1]
    cols = sums[0][0][1][2]
    chips = model // (2 * share)
    if share % LANES:
        parts = []
        for terms in sums:
            total = 0.0
            for left, (right, first, _) in terms:
                left = left.reshape(-1, 2 * chips, share)[:, index]
                right = right[:, first : first + cols]
                total += dot(left.reshape(-1, chips * share), right, TN)
            parts.append(total.reshape(chips, share, cols))
        blocks = jnp.stack(parts, axis=1)
        if plus is not None:
            blocks += jnp.stack(plus).astype(F32)
        blocks = blocks.astype(BF)
        return [blocks[j] for j in range(chips)] if apart else blocks
    tile = 512 if cols % 512 == 0 else cols
    ins = []
    flops = 0
    for terms in sums:
        for left, (right, first, _) in terms:
            for j in range(chips):
                ins.append((left, pl.BlockSpec((left.shape[0], share), lambda i, w, j=j: (0, w[j]))))
            spec = pl.BlockSpec(
                (right.shape[0], tile), lambda i, w, first=first: (0, first // tile + i)
            )
            ins.append((right, spec))
            flops += right.shape[0] * model * cols
    every = struct((chips, len(sums), share, cols))
    every_spec = pl.BlockSpec((chips, len(sums), share, tile), lambda i, w: (0, 0, 0, i))
    one_spec = pl.BlockSpec((len(sums), share, tile), lambda i, w: (0, 0, i))
    outs = [(every, every_spec)]
    if plus is not None:
        ins += [(p, one_spec) for p in plus]
    if apart:
        outs = [(struct(every.shape[1:]), one_spec)] * chips
    result = call(
        functools.partial(
            weight_grad_kernel,
            sums=[len(terms) for terms in sums],
            chips=chips,
            plus=plus is not None,
            apart=apart,
        ),
        "weight_grad",
        (cols // tile,),
        ins,
        outs,
        scalars=(index,),
        deps=deps,
        flops=flops,
    )
    return result if apart else result[0]


def ffn_sum_kernel(in_ref, own_ref, *others):
    total = in_ref[0].astype(F32)
    for c in range(1, in_ref.shape[0]):
        total += in_ref[c].astype(F32)
    hidden = own_ref.shape[2]
    own_ref[...] = total[:, :, :hidden]
    for j, ref in enumerate(others, 1):
        ref[...] = total[:, :, j * hidden : (j + 1) * hidden].astype(BF)


def tie_kernel(*refs):
    pass


def tied(value, *first):
    anywhere = pl.BlockSpec(memory_space=pl.ANY)
    return pl.pallas_call(
        tie_kernel,
        out_shape=struct(value.shape, value.dtype),
        in_specs=[anywhere] * (1 + len(first)),
        out_specs=anywhere,
        input_output_aliases={0: 0},
        cost_estimate=pl.CostEstimate(flops=0, bytes_accessed=0, transcendentals=0),
        name="tied",
    )(value, *first)


def text_kernel(in_ref, out_ref):
    part = in_ref.shape[2]
    for i in range(in_ref.shape[0]):
        out_ref[0, i * part : (i + 1) * part] = in_ref[i, 0].astype(F32)


def shards(
    frames,
    text_states,
    clip_lengths,
    text_lengths,
    cotangent,
    norm_gain,
    norm_bias,
    self_proj,
    self_out,
    cross_query,
    cross_mem,
    cross_out,
    ffn_up,
    ffn_down,
):
    streams, rows, model = frames.shape
    slots, text = text_states.shape[1:3]
    text_rows = slots * text
    blk, tp = lax.axis_size("blk"), lax.axis_size("tp")
    b, t = lax.axis_index("blk"), lax.axis_index("tp")
    mine = streams // tp
    count = mine * rows
    core, chips = b % 2, blk // 2
    local = self_out.shape[0]
    per = min(blk // tp, local // HEAD_DIM)
    width = local // per
    slices = blk // per
    group = -(-streams // slices)
    share = model // blk
    hidden = ffn_up.shape[1]
    groups = tp // 2
    device = jnp.stack([b, t]).astype(jnp.int32)
    plane = [[2 * c + k for c in range(chips)] for k in range(2)]
    chip = b // 2
    all_chips = jnp.arange(chips, dtype=jnp.int32)
    near_chips = chip ^ jnp.arange(chips, dtype=jnp.int32)

    def swapped(size, j):
        return [(i, i ^ j) for i in range(size)]

    def of_rank(values, rank):
        return lax.dynamic_slice_in_dim(values, rank * mine, mine, 0)

    def norm_rows(i):
        return jnp.stack([norm_gain[i], norm_bias[i]])

    def at(values, i):
        return lax.dynamic_index_in_dim(values, i, 0, keepdims=False)

    def from_ranks(values):
        return [values[0]] + [
            lax.ppermute(values[j], "tp", swapped(tp, j)) for j in range(1, tp)
        ]

    def over_chips(blocks):
        return lax.all_to_all(blocks, "blk", 0, 0, axis_index_groups=plane)

    def other_core(values):
        return lax.ppermute(values, "blk", swapped(blk, 1))

    def spread(w):
        near = over_chips(jnp.broadcast_to(w, (chips,) + w.shape))
        return near, other_core(near)

    def weight_grads(sums, order, apart, deps=(), later=()):
        sums = [
            [(left, r if isinstance(r, tuple) else (r, 0, r.shape[1])) for left, r in terms]
            for terms in sums
        ]
        send = weight_grad_blocks(2 * order + 1 - core, sums, share, apart=True, deps=deps)
        received = [other_core(v) for v in send]
        return weight_grad_blocks(
            2 * order + core, sums, share, received, apart=apart, deps=later
        )

    def from_chips(blocks):
        return [blocks[0]] + [
            lax.ppermute(blocks[j], "blk", swapped(blk, 2 * j)) for j in range(1, chips)
        ]

    def added(values):
        total = values[0].astype(F32)
        for v in values[1:]:
            total += v.astype(F32)
        return total

    def over_ranks(total, *first):
        parts, _, c = total.shape
        split = total.astype(BF).reshape(parts, share, tp, c // tp).transpose(2, 0, 1, 3)
        mine_of, *got = from_ranks([at(split, t ^ j) for j in range(tp)])
        return added([mine_of] + [tied(g, *first) for g in got])

    def share_rows(w):
        return lax.dynamic_slice_in_dim(w, b * share, share, w.ndim - 2)

    def share_cols(w):
        return lax.dynamic_slice_in_dim(w, b * share, share, 1).T

    mem = share_rows(cross_mem)
    shared = [mem[0], mem[1], share_cols(self_out), share_rows(cross_query), share_cols(cross_out)]
    shared = jnp.concatenate(shared, axis=1)
    piece = jnp.concatenate([share_rows(ffn_up), share_cols(ffn_down)], axis=1)

    padded = frames
    if slices * group > streams:
        padded = jnp.pad(frames, ((0, slices * group - streams), (0, 0), (0, 0)))
    pieces, h_all = qkv_pieces(
        padded, norm_rows(0), self_proj, slices, per, width, deps=(shared, piece)
    )
    qkv = lax.all_to_all(pieces.reshape(blk, group, rows, 3 * width), "blk", 0, 0)
    all_ends = jnp.cumsum(clip_lengths, axis=1).astype(jnp.int32)
    ends = of_rank(all_ends, t)
    own_ends = jnp.pad(all_ends, ((0, slices * group - streams), (0, 0)))
    own_ends = lax.dynamic_slice_in_dim(own_ends, b // per * group, group, 0)
    shared = lax.all_gather(shared, "tp")
    memory_weights = spread(tied(shared[:, :, : 2 * local], qkv))
    w_mem = columns(memory_weights, 2 * local, 0)
    attn_own = self_attention(
        own_ends, [qkv], width, self_forward_kernel, width, 0, "self_forward"
    )
    even = slices == tp and group == mine

    attn_rows = lax.all_to_all(tied(attn_own, memory_weights[0]), "blk", 0, 0)
    if even:
        attn = attn_rows.reshape(tp, per, count, width)
    else:
        attn = attn_rows.reshape(slices, per, group, rows, width).transpose(0, 2, 1, 3, 4)
        attn = attn.reshape(slices * group, per, rows, width)[:streams]
        attn = attn.reshape(tp, mine, per, rows, width).transpose(0, 2, 1, 3, 4)
        attn = attn.reshape(tp, per, count, width)
    attn = from_ranks([at(attn, t ^ j) for j in range(tp)])

    weights = spread(tied(shared[:, :, 2 * local :], *attn))
    w_first = columns(weights, 2 * local, 0)
    w_cross_out = columns(weights, local, 2)
    piece = tied(piece, *attn)
    pieces_of = [lax.ppermute(piece, "tp", swapped(tp, 2 * j)) for j in range(1, groups)]
    ffn_others = [
        lax.all_gather(tied(p, weights[0]), "blk", axis=0, tiled=True) for p in pieces_of
    ]

    info = jnp.concatenate(
        [
            ends,
            of_rank(text_lengths, t),
            jnp.full((mine, 1), b * rows, jnp.int32),
            jnp.full((mine, 1), b, jnp.int32),
            jnp.full((mine, 1), t, jnp.int32),
        ],
        axis=1,
    )
    x = of_rank(frames, t).reshape(count, model)
    flat = struct((count, model))
    wide = struct((count, model), F32)
    texts = of_rank(text_states, t).reshape(mine * text_rows, model)
    tile = model // 2
    (ckv,) = call(
        memory_kernel,
        "memory",
        (4,),
        [
            (texts, None),
            *[
                (
                    w,
                    pl.BlockSpec(
                        (chips, tp // 2, share, local), lambda i, _: (0, i % 2, 0, i // 2)
                    ),
                )
                for w in memory_weights
            ],
        ],
        [
            (
                struct((mine * text_rows, 2 * model)),
                pl.BlockSpec((mine * text_rows, tile), lambda i, _: (0, i)),
            )
        ],
        scalars=(device,),
        scratch=[pltpu.VMEM((model, tile), BF)],
        flops=4 * texts.shape[0] * model * model,
    )
    x2, h2, cq, attn = call(
        first_kernel,
        "to_cross",
        (1,),
        [
            (x, None),
            (norm_rows(1), None),
            *w_first,
            *[(a, None) for a in attn],
        ],
        [(wide, None), (flat, None), (flat, None), (flat, None)],
        scalars=(device,),
        scratch=[pltpu.VMEM((model, 2 * model), BF)],
        deps=(ckv,),
        flops=4 * count * model * model,
    )
    ckv = ckv.reshape(mine, text_rows, 2 * model)
    kv_spec = pl.BlockSpec((1, text_rows, 2 * model), lambda s, *_: (s, 0, 0))
    cross_work = count * (model // HEAD_DIM) * text_rows
    cattn, x3, h3 = call(
        functools.partial(second_kernel, slots=slots, rows=rows),
        "cross_forward",
        (mine,),
        [
            (x2, None),
            (cq, None),
            (ckv, kv_spec),
            (norm_rows(2), None),
            *w_cross_out,
        ],
        [(flat, None), (wide, None), (flat, None)],
        scalars=(info,),
        scratch=[pltpu.VMEM((model, model), BF)],
        flops=2 * count * model * model + 4 * cross_work * HEAD_DIM,
        exps=cross_work,
    )

    swap = swapped(tp, 1)
    h3_other = lax.ppermute(h3, "tp", swap)
    ct = of_rank(cotangent, t).reshape(count, model)
    ct_other = of_rank(cotangent, t ^ 1).reshape(count, model)
    own_weights = (ffn_up, ffn_down)
    act, d_up, d_h3, out = feed_forward(h3, ct, own_weights, ffn_others, hidden, False)
    act_other, d_up_other, pair = feed_forward(
        h3_other, ct_other, own_weights, ffn_others, hidden, True, deps=(out,)
    )
    pair_got = lax.ppermute(pair, "tp", swap)
    out = x3 + out + pair_got[1].astype(F32)

    ffn_blocks = weight_grads(
        [[(h3, d_up), (h3_other, d_up_other)], [(ct, act), (ct_other, act_other)]],
        all_chips,
        False,
    )
    ffn_got = over_chips(ffn_blocks)
    ffn_total, *ffn_sent = call(
        ffn_sum_kernel,
        "ffn_sum",
        (1,),
        [(ffn_got, None)],
        [(struct((2, share, hidden), F32), None)]
        + [(struct((2, share, hidden)), None)] * (groups - 1),
    )

    d_c, d_cq, d_x2, d_a, d_attn, d_ckv, early = call(
        functools.partial(third_kernel, slots=slots, rows=rows),
        "cross_backward",
        (mine,),
        [
            (d_h3, None),
            (pair_got, pl.BlockSpec((1, count, model), lambda s, _: (0, 0, 0))),
            (x3, None),
            (ct, None),
            (x2, None),
            (cq, None),
            (ckv, kv_spec),
            (norm_gain, None),
            *w_first,
            *w_cross_out,
        ],
        [
            (flat, None),
            (flat, None),
            (wide, None),
            (flat, None),
            (struct((tp, per, count, width)), None),
            (struct(ckv.shape), kv_spec),
            (struct((4, model), F32), None),
        ],
        scalars=(info,),
        scratch=[
            pltpu.VMEM((count, model), F32),
            pltpu.VMEM((count, model), BF),
            pltpu.VMEM((model, 2 * model), BF),
            pltpu.VMEM((model, model), BF),
        ],
        deps=(ffn_blocks,),
        flops=6 * count * model * model + 10 * cross_work * HEAD_DIM,
        exps=cross_work,
    )


    d_attn = from_ranks([d_attn[j] for j in range(tp)])
    out_all = lax.all_gather(tied(out.astype(BF), *d_attn[1:]), "tp", axis=0, tiled=True)
    d_attn = jnp.stack(d_attn)[jnp.arange(tp) ^ t]
    if not even:
        d_attn = d_attn.reshape(tp, per, mine, rows, width).transpose(0, 2, 1, 3, 4)
        d_attn = d_attn.reshape(streams, per, rows, width)
        d_attn = jnp.pad(d_attn, ((0, slices * group - streams), (0, 0), (0, 0), (0, 0)))
        d_attn = d_attn.reshape(slices, group, per, rows, width).transpose(0, 2, 1, 3, 4)
    d_attn = d_attn.reshape(blk, group, rows, width)
    d_attn = lax.all_to_all(tied(d_attn, ffn_got), "blk", 0, 0)
    d_qkv_own = self_attention(
        own_ends,
        [qkv, d_attn],
        width,
        self_backward_kernel,
        3 * width,
        2,
        "self_backward",
    )

    part = mine * text_rows // blk
    d_ckv = d_ckv.reshape(chips, 2, part, 2 * model)
    received = other_core(lax.dynamic_index_in_dim(d_ckv, 1 - core, 1, keepdims=False))
    d_ckv = lax.dynamic_index_in_dim(d_ckv, core, 1, keepdims=False).astype(F32)
    d_ckv = tied((d_ckv + received.astype(F32)).astype(BF), d_attn)
    d_ckv = jnp.sum(over_chips(d_ckv).astype(F32), axis=0).astype(BF)

    d_qkv = lax.all_to_all(tied(d_qkv_own, d_ckv), "blk", 0, 0)
    texts = lax.dynamic_slice_in_dim(texts, b * part, part, 0)
    (d_text_own,) = call(
        text_grad_kernel,
        "text_grad",
        (1,),
        [(d_ckv, None), *w_mem],
        [(struct((part, model)), None)],
        scalars=(device,),
        scratch=[pltpu.VMEM((model, 2 * model), BF)],
        deps=(d_qkv_own,),
        flops=4 * part * model * model,
    )
    text_got = from_ranks([d_text_own] * tp)

    ffn_back = [
        lax.ppermute(tied(v, out_all), "tp", swapped(tp, 2 * j)) for j, v in enumerate(ffn_sent, 1)
    ]
    attn_blocks = weight_grads(
        [
            [(d_a, attn)],
            [(h2, d_cq)],
            [(d_c, cattn)],
            [(texts, (d_ckv, 0, model))],
            [(texts, (d_ckv, model, model))],
        ],
        near_chips,
        True,
        deps=(d_text_own,),
    )
    d_qkv = d_qkv.reshape(slices, per, group * rows, 3 * width)
    padded_rows = slices * group * rows
    parts, d_qkv = call(
        qkv_grad_kernel,
        "qkv_grad",
        (slices,),
        [
            (d_qkv, pl.BlockSpec((1,) + d_qkv.shape[1:], lambda i: (i, 0, 0, 0))),
            (self_proj, None),
        ],
        [
            (
                struct((slices, group * rows, model)),
                pl.BlockSpec((1, group * rows, model), lambda i: (i, 0, 0)),
            ),
            (
                struct((padded_rows, 3 * local)),
                pl.BlockSpec((group * rows, 3 * local), lambda i: (i, 0)),
            ),
        ],
        deps=(attn_blocks[0], *ffn_back),
        flops=6 * padded_rows * model * local,
    )
    parts_own = parts.reshape(padded_rows, model)[: streams * rows].reshape(tp, count, model)
    parts = lax.all_to_all(parts_own, "tp", 0, 0)
    attn_got = from_chips(attn_blocks)
    qkv_blocks = weight_grads([[(h_all, d_qkv)]], near_chips, True, deps=(parts_own,), later=tuple(attn_got[1:3]))
    qkv_got = from_chips(qkv_blocks)
    d_text = jnp.stack([text_got[0]] + [tied(g, qkv_blocks[0]) for g in text_got[1:]])
    d_text = d_text[jnp.arange(tp) ^ t]

    out_frames = out_all.reshape(streams, rows, model).astype(F32)

    (g_qkv,) = added(qkv_got)
    grad_self_proj = g_qkv.reshape(share, 3, local).transpose(1, 0, 2)

    (late,) = call(
        first_norm_kernel,
        "first_norm",
        (tp,),
        [
            (parts_own, pl.BlockSpec((1, count, model), lambda i: (i, 0, 0))),
            (frames.reshape(tp, count, model), pl.BlockSpec((1, count, model), lambda i: (i, 0, 0))),
        ],
        [(struct((2, model), F32), None)],
        flops=10 * streams * rows * model,
    )
    (d_x,) = call(
        last_kernel,
        "to_frames",
        (1,),
        [(parts, None), (x, None), (d_x2, None), (norm_rows(0), None)],
        [(struct((tp, count, model)), None)],
        deps=(*attn_got[1:], qkv_blocks[0]),
        flops=20 * count * model,
    )
    d_text = lax.all_gather(tied(d_text, d_x), "blk")
    if part % 16:
        d_text = d_text.transpose(1, 0, 2, 3)
        grad_text = d_text.reshape(streams, slots, text, model).astype(F32)
    else:
        (grad_text,) = call(
            text_kernel,
            "text_out",
            (tp,),
            [(d_text, pl.BlockSpec((blk, 1, part, model), lambda i: (0, i, 0, 0)))],
            [
                (
                    struct((tp, mine * text_rows, model), F32),
                    pl.BlockSpec((1, mine * text_rows, model), lambda i: (i, 0, 0)),
                )
            ],
        )
        grad_text = grad_text.reshape(streams, slots, text, model)
    grad_frames = tied(lax.all_to_all(d_x, "tp", 0, 0), grad_text)
    grad_frames = grad_frames.reshape(streams, rows, model).astype(F32)

    sums = tied(jnp.concatenate([early, late], axis=0), d_x)
    for step in (1 << i for i in range(blk.bit_length() - 1)):
        sums = sums + lax.ppermute(sums, "blk", swapped(blk, step))
    sums = lax.dynamic_slice_in_dim(sums, b * share, share, 1)
    sums = added(from_ranks([sums] * tp))
    grad_gain = jnp.stack([sums[4], sums[0], sums[1]])
    grad_bias = jnp.stack([sums[5], sums[2], sums[3]])
    g_attn_own = over_ranks(added(attn_got), grad_frames)
    grad_cross_mem = g_attn_own[3:]
    for back in ffn_back:
        ffn_total += back.astype(F32)
    grad_ffn_up = ffn_total[0]
    grad_ffn_down = ffn_total[1].T
    grad_self_out = g_attn_own[0].T
    grad_cross_query = g_attn_own[1]
    grad_cross_out = g_attn_own[2].T
    return (
        out_frames,
        grad_frames,
        grad_text,
        grad_gain,
        grad_bias,
        grad_self_proj,
        grad_self_out,
        grad_cross_query,
        grad_cross_mem,
        grad_cross_out,
        grad_ffn_up,
        grad_ffn_down,
    )


def solution(mesh):
    in_specs = (
        P(None, "blk", None),
        P(),
        P(),
        P(),
        P(None, "blk", None),
        P(),
        P(),
        P(None, None, "tp"),
        P("tp", None),
        P(None, "tp"),
        P(None, None, "tp"),
        P("tp", None),
        P(None, "tp"),
        P("tp", None),
    )
    out_specs = (
        P(None, "blk", None),
        P(None, "blk", None),
        P(),
        P(None, "blk"),
        P(None, "blk"),
        P(None, "blk", "tp"),
        P("tp", "blk"),
        P("blk", "tp"),
        P(None, "blk", "tp"),
        P("tp", "blk"),
        P("blk", "tp"),
        P("tp", "blk"),
    )
    return jax.shard_map(shards, mesh=mesh, in_specs=in_specs, out_specs=out_specs, check_vma=False)
```

```python
import functools

import jax
import jax.numpy as jnp
from jax import lax
from jax.experimental import pallas as pl
from jax.experimental.pallas import tpu as pltpu
from jax.sharding import PartitionSpec as P

HEAD_DIM = 64
SCALE = 0.125
MASKED = -1e30
EPS = 1e-05
LANES = 128
BF = jnp.bfloat16
F32 = jnp.float32
MIB = 1 << 20

NN = ((1,), (0,))
NT = ((1,), (1,))
TN = ((0,), (0,))


def dot(a, b, dims):
    return lax.dot_general(a, b, (dims, ((), ())), preferred_element_type=F32)


def whole_spec(array):
    zeros = (0,) * len(array.shape)
    return pl.BlockSpec(tuple(array.shape), lambda *_: zeros)


def call(kernel, name, grid, ins, outs, scalars=(), scratch=(), deps=(), flops=0, exps=0):
    count = len(ins)

    def body(*refs):
        kept = len(scalars) + count
        kernel(*refs[:kept], *refs[kept + len(deps) :])

    specs = [whole_spec(a) if s is None else s for a, s in ins]
    specs += [pl.BlockSpec(memory_space=pl.ANY)] * len(deps)
    moved = sum(a.size * a.dtype.itemsize for a, _ in (*ins, *outs))
    return pl.pallas_call(
        body,
        out_shape=[o for o, _ in outs],
        grid_spec=pltpu.PrefetchScalarGridSpec(
            num_scalar_prefetch=len(scalars),
            grid=grid,
            in_specs=specs,
            out_specs=[whole_spec(o) if s is None else s for o, s in outs],
            scratch_shapes=list(scratch),
        ),
        compiler_params=pltpu.CompilerParams(vmem_limit_bytes=56 * MIB),
        cost_estimate=pl.CostEstimate(flops=flops, bytes_accessed=moved, transcendentals=exps),
        name=name,
    )(*scalars, *[a for a, _ in ins], *deps)


def struct(shape, dtype=BF):
    return jax.ShapeDtypeStruct(tuple(shape), dtype)


def assemble(whole_ref, near_ref, far_ref, device, parts=1):
    chips, ranks, share, cols = near_ref.shape
    c = cols // parts
    core = device % 2
    for chip in range(chips):
        for ref, k in ((near_ref, core), (far_ref, 1 - core)):
            rows = pl.ds(pl.multiple_of((2 * chip + k) * share, share), share)
            for p in range(parts):
                for r in range(ranks):
                    to = (p * ranks + r) * c
                    whole_ref[rows, to : to + c] = ref[chip, r, :, p * c : (p + 1) * c]


def columns(pair, size, place):
    return [
        (w, pl.BlockSpec(w.shape[:3] + (size,), lambda *_: (0, 0, 0, place))) for w in pair
    ]


def normalize(values):
    centre = values - jnp.mean(values, axis=-1, keepdims=True)
    inverse = lax.rsqrt(jnp.mean(centre * centre, axis=-1, keepdims=True) + EPS)
    return centre * inverse, inverse


def normed(values, gain, bias):
    return (normalize(values)[0] * gain + bias).astype(BF)


def norm_backward(values, gain, upstream):
    normal, inverse = normalize(values)
    g = upstream * gain
    mean_g = jnp.mean(g, axis=-1, keepdims=True)
    mean_gn = jnp.mean(g * normal, axis=-1, keepdims=True)
    d_values = inverse * (g - mean_g - normal * mean_gn)
    gain_sum = jnp.sum(upstream * normal, axis=0, keepdims=True)
    return d_values, gain_sum, jnp.sum(upstream, axis=0, keepdims=True)


def head_masks(width):
    lane = lax.broadcasted_iota(jnp.int32, (1, width), 1) // HEAD_DIM
    return [lane == h for h in range(width // HEAD_DIM)]


def pick(mask, values):
    return jnp.where(mask, values, jnp.zeros_like(values))


def stacked_heads(values):
    return jnp.concatenate([pick(m, values) for m in head_masks(values.shape[1])], axis=0)


def merged_heads(values, rows):
    total = values[:rows]
    for h, mask in enumerate(head_masks(values.shape[1])):
        if h:
            total = jnp.where(mask, values[h * rows : (h + 1) * rows], total)
    return total


def softmax(scores, allowed):
    scores = jnp.where(allowed, scores, MASKED)
    weights = jnp.exp(scores - jnp.max(scores, axis=1, keepdims=True))
    return weights * (1.0 / jnp.sum(weights, axis=1, keepdims=True))


def qkv_kernel(x_ref, norm_ref, w_ref, out_ref, h_ref):
    width = out_ref.shape[3] // 3
    x = x_ref[...].reshape(-1, x_ref.shape[-1]).astype(F32)
    h = normed(x, norm_ref[0:1], norm_ref[1:2])
    h_ref[...] = h
    for k in range(3):
        result = dot(h, w_ref[k], NN).astype(BF)
        for p in range(out_ref.shape[1]):
            out_ref[0, p, :, k * width : (k + 1) * width] = result[:, p * width : (p + 1) * width]


def qkv_pieces(frames, norm, weights, slices, parts, width, deps=()):
    streams, rows, model = frames.shape
    group = streams // slices
    out = struct((slices, parts, group * rows, 3 * width))
    return call(
        qkv_kernel,
        "qkv",
        (slices,),
        [
            (frames, pl.BlockSpec((group, rows, model), lambda i: (i, 0, 0))),
            (norm, None),
            (weights, None),
        ],
        [
            (out, pl.BlockSpec((1,) + out.shape[1:], lambda i: (i, 0, 0, 0))),
            (
                struct((streams * rows, model)),
                pl.BlockSpec((group * rows, model), lambda i: (i, 0)),
            ),
        ],
        deps=deps,
        flops=2 * streams * rows * weights.size,
    )


def qkv_grad_kernel(grad_ref, w_ref, out_ref, merged_ref):
    parts, width = grad_ref.shape[1], grad_ref.shape[3] // 3
    local = parts * width
    for p in range(parts):
        for k in range(3):
            to = k * local + p * width
            merged_ref[:, to : to + width] = grad_ref[0, p, :, k * width : (k + 1) * width]
    total = 0.0
    for k in range(3):
        total += dot(merged_ref[:, k * local : (k + 1) * local], w_ref[k], NT)
    out_ref[0] = total.astype(BF)


def first_norm_kernel(parts_ref, x_ref, sums_ref):
    d_h1 = parts_ref[0].astype(F32)
    normal, _ = normalize(x_ref[0].astype(F32))
    sums = [jnp.sum(d_h1 * normal, axis=0, keepdims=True), jnp.sum(d_h1, axis=0, keepdims=True)]

    @pl.when(pl.program_id(0) == 0)
    def _():
        sums_ref[...] = jnp.zeros_like(sums_ref)

    sums_ref[...] += jnp.concatenate(sums, axis=0)


def last_kernel(parts_ref, x_ref, dx2_ref, norm_ref, dx_ref):
    d_h1 = parts_ref[0].astype(F32)
    for r in range(1, parts_ref.shape[0]):
        d_h1 += parts_ref[r].astype(F32)
    d_v, _, _ = norm_backward(x_ref[...].astype(F32), norm_ref[0:1], d_h1)
    d_x = (dx2_ref[...] + d_v).astype(BF)
    for r in range(dx_ref.shape[0]):
        dx_ref[r] = d_x


def causal_probs(ends_ref, stream, slots, q, k, first):
    block = q.shape[0]
    rows = first + lax.broadcasted_iota(jnp.int32, (block, 1), 0)
    begin = jnp.zeros((block, 1), jnp.int32)
    for c in range(slots):
        end = ends_ref[stream, c]
        begin = jnp.where(rows >= end, jnp.maximum(begin, end), begin)
    cols = lax.broadcasted_iota(jnp.int32, (block, k.shape[0]), 1)
    return softmax(dot(q, k, NT), (cols <= rows) & (cols >= begin))


def self_forward_kernel(ends_ref, qkv_ref, out_ref, *, slots, width, block):
    stream = pl.program_id(0)
    parts, _, rows, _ = qkv_ref.shape
    length = parts * rows
    qkv = qkv_ref[...].reshape(length, 3 * width)
    q = qkv[:, :width] * jnp.asarray(SCALE, BF)
    k = qkv[:, width : 2 * width]
    v = qkv[:, 2 * width :]
    masks = head_masks(width)
    q_of = [pick(m, q) for m in masks]
    v_of = [pick(m, v) for m in masks]
    per = block // rows
    firsts = range(0, length, block)
    pairs = [(h, first) for first in firsts for h in range(len(masks))]
    probs = [
        causal_probs(
            ends_ref, stream, slots, q_of[h][first : first + block], k[: first + block], first
        ).astype(BF)
        for h, first in pairs
    ]
    results = [
        dot(p, v_of[h][: first + block], NN) for p, (h, first) in zip(probs, pairs)
    ]
    for first in firsts:
        total = sum(r for r, (_, f) in zip(results, pairs) if f == first)
        at = first // rows
        out_ref[at : at + per, 0] = total.astype(BF).reshape(per, rows, width)


def self_backward_kernel(ends_ref, qkv_ref, grad_ref, out_ref, dk_ref, dv_ref, *, slots, width, block):
    stream = pl.program_id(0)
    parts, _, rows, _ = qkv_ref.shape
    length = parts * rows
    qkv = qkv_ref[...].reshape(length, 3 * width)
    q = qkv[:, :width] * jnp.asarray(SCALE, BF)
    k = qkv[:, width : 2 * width]
    v = qkv[:, 2 * width :]
    grad = grad_ref[...].reshape(length, width)
    masks = head_masks(width)
    q_of = [pick(m, q) for m in masks]
    k_of = [pick(m, k) for m in masks]
    g_of = [pick(m, grad) for m in masks]
    dk_ref[...] = jnp.zeros_like(dk_ref)
    dv_ref[...] = jnp.zeros_like(dv_ref)
    per = block // rows
    for first in range(0, length, block):
        top = first + block
        heads = range(len(masks))
        q_part = [q_of[h][first:top] for h in heads]
        g_part = [g_of[h][first:top] for h in heads]
        d_probs = [dot(g, v[:top], NT) for g in g_part]
        probs = [causal_probs(ends_ref, stream, slots, a, k[:top], first) for a in q_part]
        delta = [jnp.sum(a * b, axis=1, keepdims=True) for a, b in zip(probs, d_probs)]
        d_scores = [(a * (b - c)).astype(BF) for a, b, c in zip(probs, d_probs, delta)]
        dq = sum(dot(a, k_of[h][:top], NN) for h, a in zip(heads, d_scores))
        dk_ref[:top] += sum(dot(a, b, TN) for a, b in zip(d_scores, q_part))
        dv_ref[:top] += sum(dot(a.astype(BF), b, TN) for a, b in zip(probs, g_part))
        at = first // rows
        out_ref[at : at + per, 0, :, :width] = (dq * SCALE).astype(BF).reshape(per, rows, width)
    out_ref[:, 0, :, width : 2 * width] = dk_ref[...].astype(BF).reshape(parts, rows, width)
    out_ref[:, 0, :, 2 * width :] = dv_ref[...].astype(BF).reshape(parts, rows, width)


def self_attention(ends, arrays, width, kernel, out_width, scratch, name, deps=()):
    parts, streams, rows, _ = arrays[0].shape
    length = parts * rows
    block = min(length, rows * max(1, 256 // rows))
    work = streams * (width // HEAD_DIM) * length * length

    def spec(c):
        return pl.BlockSpec((parts, 1, rows, c), lambda s, *_: (0, s, 0, 0))

    out = struct((parts, streams, rows, out_width))
    return call(
        functools.partial(kernel, slots=ends.shape[1], width=width, block=block),
        name,
        (streams,),
        [(a, spec(a.shape[3])) for a in arrays],
        [(out, spec(out_width))],
        scalars=(ends,),
        scratch=[pltpu.VMEM((length, width), F32)] * scratch,
        deps=deps,
        flops=4 * len(arrays) * work * HEAD_DIM,
        exps=work,
    )[0]


def first_kernel(device_ref, x_ref, norm_ref, near_ref, far_ref, *refs):
    pieces, (x2_ref, h2_ref, cq_ref, attn_out_ref, w_ref) = refs[:-5], refs[-5:]
    model = x2_ref.shape[1]
    assemble(w_ref, near_ref, far_ref, device_ref[0], 2)
    for j, ref in enumerate(pieces):
        piece = jnp.concatenate([ref[p] for p in range(ref.shape[0])], axis=1)
        local = piece.shape[1]
        to = pl.multiple_of((device_ref[1] ^ j) * local, local)
        attn_out_ref[:, pl.ds(to, local)] = piece
    attn = attn_out_ref[...]
    x2 = x_ref[...].astype(F32) + dot(attn, w_ref[:, :model], NT)
    x2_ref[...] = x2
    h2 = normed(x2, norm_ref[0:1], norm_ref[1:2])
    h2_ref[...] = h2
    cq_ref[...] = dot(h2, w_ref[:, model:], NN).astype(BF)


def memory_kernel(device_ref, text_ref, near_ref, far_ref, out_ref, w_ref):
    assemble(w_ref, near_ref, far_ref, device_ref[0])
    out_ref[...] = dot(text_ref[...], w_ref[...], NN).astype(BF)


def text_grad_kernel(device_ref, rows_ref, near_ref, far_ref, out_ref, w_ref):
    assemble(w_ref, near_ref, far_ref, device_ref[0], 2)
    out_ref[...] = dot(rows_ref[...], w_ref[...], NT).astype(BF)


def cross_allowed(info_ref, stream, slots, rows, keys):
    text = keys // slots
    pos = info_ref[stream, 2 * slots] + lax.broadcasted_iota(jnp.int32, (rows, 1), 0)
    clip = jnp.zeros((rows, 1), jnp.int32)
    for c in range(slots):
        clip += jnp.where(pos >= info_ref[stream, c], 1, 0)
    begin = clip * text
    count = jnp.zeros((rows, 1), jnp.int32)
    for c in range(slots):
        count = jnp.where(clip == c, info_ref[stream, slots + c], count)
    key = lax.broadcasted_iota(jnp.int32, (rows, keys), 1)
    return (key >= begin) & (key < begin + count)


CROSS_LANES = 256


def second_kernel(
    info_ref, x2_ref, cq_ref, kv_ref, norm_ref, near_ref, far_ref, *refs, slots, rows
):
    cattn_ref, x3_ref, h3_ref, wo_ref = refs
    stream = pl.program_id(0)
    model = x2_ref.shape[1]
    keys = kv_ref.shape[1]
    mine = pl.ds(pl.multiple_of(stream * rows, rows), rows)
    once = cross_allowed(info_ref, stream, slots, rows, keys)
    allowed = jnp.concatenate([once] * (CROSS_LANES // HEAD_DIM), axis=0)
    every = [slice(at, at + CROSS_LANES) for at in range(0, model, CROSS_LANES)]
    q = [stacked_heads(cq_ref[mine, c] * jnp.asarray(SCALE, BF)) for c in every]
    scores = [dot(a, kv_ref[0, :, c], NT) for a, c in zip(q, every)]
    probs = [softmax(a, allowed).astype(BF) for a in scores]
    values = [kv_ref[0, :, model + c.start : model + c.stop] for c in every]
    results = [dot(a, v, NN) for a, v in zip(probs, values)]
    for c, a in zip(every, results):
        cattn_ref[mine, c] = merged_heads(a, rows).astype(BF)

    @pl.when(stream == pl.num_programs(0) - 1)
    def _():
        assemble(wo_ref, near_ref, far_ref, info_ref[0, 2 * slots + 1])
        x3 = x2_ref[...] + dot(cattn_ref[...], wo_ref[...], NT)
        x3_ref[...] = x3
        h3_ref[...] = normed(x3, norm_ref[0:1], norm_ref[1:2])


def third_kernel(
    info_ref,
    dh_ref,
    received_ref,
    x3_ref,
    ct_ref,
    x2_ref,
    cq_ref,
    kv_ref,
    gain_ref,
    near1_ref,
    far1_ref,
    near2_ref,
    far2_ref,
    dc_ref,
    dcq_ref,
    dx2_ref,
    da_ref,
    dattn_ref,
    dkv_ref,
    sums_ref,
    dx3_ref,
    dcattn_ref,
    w_first_ref,
    w_cross_ref,
    *,
    slots,
    rows,
):
    device = info_ref[0, 2 * slots + 1]
    stream = pl.program_id(0)
    model = x2_ref.shape[1]
    keys = kv_ref.shape[1]

    @pl.when(stream == 0)
    def _():
        d_h3 = dh_ref[...] + received_ref[0].astype(F32)
        d_v, gain, bias = norm_backward(x3_ref[...], gain_ref[2:3], d_h3)
        sums_ref[1:2] = gain
        sums_ref[3:4] = bias
        d_x3 = ct_ref[...].astype(F32) + d_v
        dx3_ref[...] = d_x3
        d_c = d_x3.astype(BF)
        dc_ref[...] = d_c
        assemble(w_cross_ref, near2_ref, far2_ref, device)
        dcattn_ref[...] = dot(d_c, w_cross_ref[...], NN).astype(BF)

    mine = pl.ds(pl.multiple_of(stream * rows, rows), rows)
    once = cross_allowed(info_ref, stream, slots, rows, keys)
    allowed = jnp.concatenate([once] * (CROSS_LANES // HEAD_DIM), axis=0)
    every = [slice(at, at + CROSS_LANES) for at in range(0, model, CROSS_LANES)]
    k = [kv_ref[0, :, c] for c in every]
    v = [kv_ref[0, :, model + c.start : model + c.stop] for c in every]
    q = [stacked_heads(cq_ref[mine, c] * jnp.asarray(SCALE, BF)) for c in every]
    grad = [stacked_heads(dcattn_ref[mine, c]) for c in every]
    scores = [dot(a, b, NT) for a, b in zip(q, k)]
    d_probs = [dot(a, b, NT) for a, b in zip(grad, v)]
    probs = [softmax(a, allowed) for a in scores]
    delta = [jnp.sum(a * b, axis=1, keepdims=True) for a, b in zip(probs, d_probs)]
    d_scores = [(a * (b - c)).astype(BF) for a, b, c in zip(probs, d_probs, delta)]
    d_q = [dot(a, b, NN) for a, b in zip(d_scores, k)]
    d_k = [dot(a, b, TN) for a, b in zip(d_scores, q)]
    d_v = [dot(a.astype(BF), b, TN) for a, b in zip(probs, grad)]
    for i, c in enumerate(every):
        dcq_ref[mine, c] = (merged_heads(d_q[i], rows) * SCALE).astype(BF)
        dkv_ref[0, :, c] = d_k[i].astype(BF)
        dkv_ref[0, :, model + c.start : model + c.stop] = d_v[i].astype(BF)

    @pl.when(stream == pl.num_programs(0) - 1)
    def _():
        assemble(w_first_ref, near1_ref, far1_ref, device, 2)
        d_h2 = dot(dcq_ref[...], w_first_ref[:, model:], NT)
        d_v, gain, bias = norm_backward(x2_ref[...], gain_ref[1:2], d_h2)
        sums_ref[0:1] = gain
        sums_ref[2:3] = bias
        d_x2 = dx3_ref[...] + d_v
        dx2_ref[...] = d_x2
        d_a = d_x2.astype(BF)
        da_ref[...] = d_a
        d_attn = dot(d_a, w_first_ref[:, :model], NN).astype(BF)
        ranks, parts, _, width = dattn_ref.shape
        for p in range(ranks * parts):
            to = (p // parts) ^ info_ref[0, 2 * slots + 2]
            dattn_ref[to, p % parts] = d_attn[:, p * width : (p + 1) * width]


def ffn_kernel(h_ref, ct_ref, *refs, groups, tiles):
    (act_ref, dup_ref), results = refs[2 * groups : 2 * groups + 2], refs[2 * groups + 2 : -2]
    dh_acc, out_acc = refs[-2:]
    step = pl.program_id(0)

    @pl.when(step == 0)
    def _():
        dh_acc[...] = jnp.zeros_like(dh_acc)
        out_acc[...] = jnp.zeros_like(out_acc)

    for g in range(groups):

        @pl.when(step // tiles == g)
        def _(g=g):
            w_up, w_down = refs[2 * g][...], refs[2 * g + 1][...]
            into, out_of = (NN, NT) if g else (NT, NN)
            up = dot(h_ref[...], w_up, NN)
            d_act = dot(ct_ref[...], w_down, into)
            cdf = 0.5 * (1.0 + lax.erf(up * (0.5**0.5)))
            slope = cdf + up * jnp.exp(-0.5 * up * up) * 0.3989422804014327
            act = (up * cdf).astype(BF)
            d_up = (d_act * slope).astype(BF)
            act_ref[...] = act
            dup_ref[...] = d_up
            dh_acc[...] += dot(d_up, w_up, NT)
            out_acc[...] += dot(act, w_down, out_of)

    @pl.when(step == groups * tiles - 1)
    def _():
        if len(results) == 2:
            results[0][...] = dh_acc[...]
            results[1][...] = out_acc[...]
        else:
            results[0][0] = dh_acc[...].astype(BF)
            results[0][1] = out_acc[...].astype(BF)


def feed_forward(h, ct, own, others, hidden, paired, deps=()):
    count, model = h.shape
    groups = 1 + len(others)
    tile = min(hidden, 512)
    tiles = hidden // tile

    def place(g):
        return lambda i: jnp.clip(i - g * tiles, 0, tiles - 1)

    ins = [(h, None), (ct, None)]
    ins.append((own[0], pl.BlockSpec((model, tile), lambda i: (0, place(0)(i)))))
    ins.append((own[1], pl.BlockSpec((tile, model), lambda i: (place(0)(i), 0))))
    for g, w in enumerate(others, 1):
        for first in (0, tiles):
            spec = pl.BlockSpec((model, tile), lambda i, g=g, f=first: (0, f + place(g)(i)))
            ins.append((w, spec))
    wide = struct((count, groups * hidden))
    results = [(struct((count, model), F32), None)] * 2
    if paired:
        results = [(struct((2, count, model)), None)]
    column = pl.BlockSpec((count, tile), lambda i: (0, i))
    return call(
        functools.partial(ffn_kernel, groups=groups, tiles=tiles),
        "feed_forward",
        (groups * tiles,),
        ins,
        [(wide, column), (wide, column), *results],
        scratch=[pltpu.VMEM((count, model), F32)] * 2,
        deps=deps,
        flops=8 * count * model * groups * hidden,
        exps=2 * count * groups * hidden,
    )


def weight_grad_kernel(index_ref, *refs, sums, chips, plus, apart):
    outs = refs[-chips:] if apart else [refs[-1].at[j] for j in range(chips)]
    at = 0
    for p, terms in enumerate(sums):
        total = 0.0
        for _ in range(terms):
            left = jnp.concatenate([r[...] for r in refs[at : at + chips]], axis=1)
            total += dot(left, refs[at + chips][...], TN)
            at += chips + 1
        share = total.shape[0] // chips
        for j in range(chips):
            block = total[j * share : (j + 1) * share]
            if plus:
                block += refs[sum(sums) * (chips + 1) + j][p].astype(F32)
            outs[j][p] = block.astype(BF)


def weight_grad_blocks(index, sums, share, plus=None, apart=False, deps=()):
    model = sums[0][0][0].shape[1]
    cols = sums[0][0][1][2]
    chips = model // (2 * share)
    if share % LANES:
        parts = []
        for terms in sums:
            total = 0.0
            for left, (right, first, _) in terms:
                left = left.reshape(-1, 2 * chips, share)[:, index]
                right = right[:, first : first + cols]
                total += dot(left.reshape(-1, chips * share), right, TN)
            parts.append(total.reshape(chips, share, cols))
        blocks = jnp.stack(parts, axis=1)
        if plus is not None:
            blocks += jnp.stack(plus).astype(F32)
        blocks = blocks.astype(BF)
        return [blocks[j] for j in range(chips)] if apart else blocks
    tile = 512 if cols % 512 == 0 else cols
    ins = []
    flops = 0
    for terms in sums:
        for left, (right, first, _) in terms:
            for j in range(chips):
                ins.append((left, pl.BlockSpec((left.shape[0], share), lambda i, w, j=j: (0, w[j]))))
            spec = pl.BlockSpec(
                (right.shape[0], tile), lambda i, w, first=first: (0, first // tile + i)
            )
            ins.append((right, spec))
            flops += right.shape[0] * model * cols
    every = struct((chips, len(sums), share, cols))
    every_spec = pl.BlockSpec((chips, len(sums), share, tile), lambda i, w: (0, 0, 0, i))
    one_spec = pl.BlockSpec((len(sums), share, tile), lambda i, w: (0, 0, i))
    outs = [(every, every_spec)]
    if plus is not None:
        ins += [(p, one_spec) for p in plus]
    if apart:
        outs = [(struct(every.shape[1:]), one_spec)] * chips
    result = call(
        functools.partial(
            weight_grad_kernel,
            sums=[len(terms) for terms in sums],
            chips=chips,
            plus=plus is not None,
            apart=apart,
        ),
        "weight_grad",
        (cols // tile,),
        ins,
        outs,
        scalars=(index,),
        deps=deps,
        flops=flops,
    )
    return result if apart else result[0]


def ffn_sum_kernel(in_ref, own_ref, *others):
    total = in_ref[0].astype(F32)
    for c in range(1, in_ref.shape[0]):
        total += in_ref[c].astype(F32)
    hidden = own_ref.shape[2]
    own_ref[...] = total[:, :, :hidden]
    for j, ref in enumerate(others, 1):
        ref[...] = total[:, :, j * hidden : (j + 1) * hidden].astype(BF)


def tie_kernel(*refs):
    pass


def tied(value, *first):
    anywhere = pl.BlockSpec(memory_space=pl.ANY)
    return pl.pallas_call(
        tie_kernel,
        out_shape=struct(value.shape, value.dtype),
        in_specs=[anywhere] * (1 + len(first)),
        out_specs=anywhere,
        input_output_aliases={0: 0},
        cost_estimate=pl.CostEstimate(flops=0, bytes_accessed=0, transcendentals=0),
        name="tied",
    )(value, *first)


def text_kernel(in_ref, out_ref):
    part = in_ref.shape[2]
    for i in range(in_ref.shape[0]):
        out_ref[0, i * part : (i + 1) * part] = in_ref[i, 0].astype(F32)


def shards(
    frames,
    text_states,
    clip_lengths,
    text_lengths,
    cotangent,
    norm_gain,
    norm_bias,
    self_proj,
    self_out,
    cross_query,
    cross_mem,
    cross_out,
    ffn_up,
    ffn_down,
):
    streams, rows, model = frames.shape
    slots, text = text_states.shape[1:3]
    text_rows = slots * text
    blk, tp = lax.axis_size("blk"), lax.axis_size("tp")
    b, t = lax.axis_index("blk"), lax.axis_index("tp")
    mine = streams // tp
    count = mine * rows
    core, chips = b % 2, blk // 2
    local = self_out.shape[0]
    per = min(blk // tp, local // HEAD_DIM)
    width = local // per
    slices = blk // per
    group = -(-streams // slices)
    share = model // blk
    hidden = ffn_up.shape[1]
    groups = tp // 2
    device = jnp.stack([b, t]).astype(jnp.int32)
    plane = [[2 * c + k for c in range(chips)] for k in range(2)]
    chip = b // 2
    all_chips = jnp.arange(chips, dtype=jnp.int32)
    near_chips = chip ^ jnp.arange(chips, dtype=jnp.int32)

    def swapped(size, j):
        return [(i, i ^ j) for i in range(size)]

    def of_rank(values, rank):
        return lax.dynamic_slice_in_dim(values, rank * mine, mine, 0)

    def norm_rows(i):
        return jnp.stack([norm_gain[i], norm_bias[i]])

    def at(values, i):
        return lax.dynamic_index_in_dim(values, i, 0, keepdims=False)

    def from_ranks(values):
        return [values[0]] + [
            lax.ppermute(values[j], "tp", swapped(tp, j)) for j in range(1, tp)
        ]

    def over_chips(blocks):
        return lax.all_to_all(blocks, "blk", 0, 0, axis_index_groups=plane)

    def other_core(values):
        return lax.ppermute(values, "blk", swapped(blk, 1))

    def spread(w, *first):
        near = over_chips(tied(jnp.broadcast_to(w, (chips,) + w.shape), *first))
        return near, other_core(near)

    def weight_grads(sums, order, apart, deps=(), later=()):
        sums = [
            [(left, r if isinstance(r, tuple) else (r, 0, r.shape[1])) for left, r in terms]
            for terms in sums
        ]
        send = weight_grad_blocks(2 * order + 1 - core, sums, share, apart=True, deps=deps)
        received = [other_core(v) for v in send]
        return weight_grad_blocks(
            2 * order + core, sums, share, received, apart=apart, deps=later
        )

    def from_chips(blocks):
        return [blocks[0]] + [
            lax.ppermute(blocks[j], "blk", swapped(blk, 2 * j)) for j in range(1, chips)
        ]

    def added(values):
        total = values[0].astype(F32)
        for v in values[1:]:
            total += v.astype(F32)
        return total

    def over_ranks(total, *first):
        parts, _, c = total.shape
        split = total.astype(BF).reshape(parts, share, tp, c // tp).transpose(2, 0, 1, 3)
        mine_of, *got = from_ranks([at(split, t ^ j) for j in range(tp)])
        return added([mine_of] + [tied(g, *first) for g in got])

    def share_rows(w):
        return lax.dynamic_slice_in_dim(w, b * share, share, w.ndim - 2)

    def share_cols(w):
        return lax.dynamic_slice_in_dim(w, b * share, share, 1).T

    mem = share_rows(cross_mem)
    shared = [mem[0], mem[1], share_cols(self_out), share_rows(cross_query), share_cols(cross_out)]
    shared = jnp.concatenate(shared, axis=1)
    piece = jnp.concatenate([share_rows(ffn_up), share_cols(ffn_down)], axis=1)

    padded = frames
    if slices * group > streams:
        padded = jnp.pad(frames, ((0, slices * group - streams), (0, 0), (0, 0)))
    pieces, h_all = qkv_pieces(
        padded, norm_rows(0), self_proj, slices, per, width, deps=(shared,)
    )
    qkv = lax.all_to_all(pieces.reshape(blk, group, rows, 3 * width), "blk", 0, 0)
    all_ends = jnp.cumsum(clip_lengths, axis=1).astype(jnp.int32)
    ends = of_rank(all_ends, t)
    own_ends = jnp.pad(all_ends, ((0, slices * group - streams), (0, 0)))
    own_ends = lax.dynamic_slice_in_dim(own_ends, b // per * group, group, 0)
    shared = lax.all_gather(shared, "tp")
    memory_weights = spread(shared[:, :, : 2 * local], qkv)
    w_mem = columns(memory_weights, 2 * local, 0)
    ct = of_rank(cotangent, t).reshape(count, model)
    ct_other = of_rank(cotangent, t ^ 1).reshape(count, model)
    x = of_rank(frames, t).reshape(count, model)
    texts = of_rank(text_states, t).reshape(mine * text_rows, model)
    attn_own = self_attention(
        own_ends, [qkv], width, self_forward_kernel, width, 0, "self_forward", deps=(ct, ct_other, x, texts)
    )
    even = slices == tp and group == mine

    attn_rows = lax.all_to_all(tied(attn_own, memory_weights[0]), "blk", 0, 0)
    if even:
        attn = attn_rows.reshape(tp, per, count, width)
    else:
        attn = attn_rows.reshape(slices, per, group, rows, width).transpose(0, 2, 1, 3, 4)
        attn = attn.reshape(slices * group, per, rows, width)[:streams]
        attn = attn.reshape(tp, mine, per, rows, width).transpose(0, 2, 1, 3, 4)
        attn = attn.reshape(tp, per, count, width)
    attn = from_ranks([at(attn, t ^ j) for j in range(tp)])

    weights = spread(shared[:, :, 2 * local :], *attn)
    w_first = columns(weights, 2 * local, 0)
    w_cross_out = columns(weights, local, 2)
    piece = tied(piece, *attn)
    pieces_of = [lax.ppermute(piece, "tp", swapped(tp, 2 * j)) for j in range(1, groups)]
    ffn_others = [
        lax.all_gather(tied(p, weights[0]), "blk", axis=0, tiled=True) for p in pieces_of
    ]

    info = jnp.concatenate(
        [
            ends,
            of_rank(text_lengths, t),
            jnp.full((mine, 1), b * rows, jnp.int32),
            jnp.full((mine, 1), b, jnp.int32),
            jnp.full((mine, 1), t, jnp.int32),
        ],
        axis=1,
    )
    flat = struct((count, model))
    wide = struct((count, model), F32)
    tile = model // 2
    (ckv,) = call(
        memory_kernel,
        "memory",
        (4,),
        [
            (texts, None),
            *[
                (
                    w,
                    pl.BlockSpec(
                        (chips, tp // 2, share, local), lambda i, _: (0, i % 2, 0, i // 2)
                    ),
                )
                for w in memory_weights
            ],
        ],
        [
            (
                struct((mine * text_rows, 2 * model)),
                pl.BlockSpec((mine * text_rows, tile), lambda i, _: (0, i)),
            )
        ],
        scalars=(device,),
        scratch=[pltpu.VMEM((model, tile), BF)],
        flops=4 * texts.shape[0] * model * model,
    )
    x2, h2, cq, attn = call(
        first_kernel,
        "to_cross",
        (1,),
        [
            (x, None),
            (norm_rows(1), None),
            *w_first,
            *[(a, None) for a in attn],
        ],
        [(wide, None), (flat, None), (flat, None), (flat, None)],
        scalars=(device,),
        scratch=[pltpu.VMEM((model, 2 * model), BF)],
        deps=(ckv,),
        flops=4 * count * model * model,
    )
    ckv = ckv.reshape(mine, text_rows, 2 * model)
    kv_spec = pl.BlockSpec((1, text_rows, 2 * model), lambda s, *_: (s, 0, 0))
    cross_work = count * (model // HEAD_DIM) * text_rows
    cattn, x3, h3 = call(
        functools.partial(second_kernel, slots=slots, rows=rows),
        "cross_forward",
        (mine,),
        [
            (x2, None),
            (cq, None),
            (ckv, kv_spec),
            (norm_rows(2), None),
            *w_cross_out,
        ],
        [(flat, None), (wide, None), (flat, None)],
        scalars=(info,),
        scratch=[pltpu.VMEM((model, model), BF)],
        flops=2 * count * model * model + 4 * cross_work * HEAD_DIM,
        exps=cross_work,
    )

    swap = swapped(tp, 1)
    h3_other = lax.ppermute(h3, "tp", swap)
    own_weights = (ffn_up, ffn_down)
    act, d_up, d_h3, out = feed_forward(h3, ct, own_weights, ffn_others, hidden, False)
    act_other, d_up_other, pair = feed_forward(
        h3_other, ct_other, own_weights, ffn_others, hidden, True, deps=(out,)
    )
    pair_got = lax.ppermute(pair, "tp", swap)
    out = x3 + out + pair_got[1].astype(F32)

    ffn_blocks = weight_grads(
        [[(h3, d_up), (h3_other, d_up_other)], [(ct, act), (ct_other, act_other)]],
        all_chips,
        False,
    )
    ffn_got = over_chips(ffn_blocks)
    ffn_total, *ffn_sent = call(
        ffn_sum_kernel,
        "ffn_sum",
        (1,),
        [(ffn_got, None)],
        [(struct((2, share, hidden), F32), None)]
        + [(struct((2, share, hidden)), None)] * (groups - 1),
    )

    d_c, d_cq, d_x2, d_a, d_attn, d_ckv, early = call(
        functools.partial(third_kernel, slots=slots, rows=rows),
        "cross_backward",
        (mine,),
        [
            (d_h3, None),
            (pair_got, pl.BlockSpec((1, count, model), lambda s, _: (0, 0, 0))),
            (x3, None),
            (ct, None),
            (x2, None),
            (cq, None),
            (ckv, kv_spec),
            (norm_gain, None),
            *w_first,
            *w_cross_out,
        ],
        [
            (flat, None),
            (flat, None),
            (wide, None),
            (flat, None),
            (struct((tp, per, count, width)), None),
            (struct(ckv.shape), kv_spec),
            (struct((4, model), F32), None),
        ],
        scalars=(info,),
        scratch=[
            pltpu.VMEM((count, model), F32),
            pltpu.VMEM((count, model), BF),
            pltpu.VMEM((model, 2 * model), BF),
            pltpu.VMEM((model, model), BF),
        ],
        deps=(ffn_blocks,),
        flops=6 * count * model * model + 10 * cross_work * HEAD_DIM,
        exps=cross_work,
    )


    d_attn = from_ranks([d_attn[j] for j in range(tp)])
    out_all = lax.all_gather(tied(out.astype(BF), *d_attn[1:]), "tp", axis=0, tiled=True)
    d_attn = jnp.stack(d_attn)[jnp.arange(tp) ^ t]
    if not even:
        d_attn = d_attn.reshape(tp, per, mine, rows, width).transpose(0, 2, 1, 3, 4)
        d_attn = d_attn.reshape(streams, per, rows, width)
        d_attn = jnp.pad(d_attn, ((0, slices * group - streams), (0, 0), (0, 0), (0, 0)))
        d_attn = d_attn.reshape(slices, group, per, rows, width).transpose(0, 2, 1, 3, 4)
    d_attn = d_attn.reshape(blk, group, rows, width)
    d_attn = lax.all_to_all(tied(d_attn, ffn_got), "blk", 0, 0)
    d_qkv_own = self_attention(
        own_ends,
        [qkv, d_attn],
        width,
        self_backward_kernel,
        3 * width,
        2,
        "self_backward",
    )

    part = mine * text_rows // blk
    d_ckv = d_ckv.reshape(chips, 2, part, 2 * model)
    received = other_core(lax.dynamic_index_in_dim(d_ckv, 1 - core, 1, keepdims=False))
    d_ckv = lax.dynamic_index_in_dim(d_ckv, core, 1, keepdims=False).astype(F32)
    d_ckv = tied((d_ckv + received.astype(F32)).astype(BF), d_attn)
    ckv_got = over_chips(d_ckv)
    d_ckv = jnp.sum(ckv_got.astype(F32), axis=0).astype(BF)

    d_qkv_own = tied(d_qkv_own, ckv_got)
    d_qkv = lax.all_to_all(d_qkv_own, "blk", 0, 0)
    texts = lax.dynamic_slice_in_dim(texts, b * part, part, 0)
    (d_text_own,) = call(
        text_grad_kernel,
        "text_grad",
        (1,),
        [(d_ckv, None), *w_mem],
        [(struct((part, model)), None)],
        scalars=(device,),
        scratch=[pltpu.VMEM((model, 2 * model), BF)],
        deps=(d_qkv_own, ffn_total),
        flops=4 * part * model * model,
    )
    text_got = from_ranks([d_text_own] * tp)

    ffn_back = [
        lax.ppermute(tied(v, out_all), "tp", swapped(tp, 2 * j)) for j, v in enumerate(ffn_sent, 1)
    ]
    attn_blocks = weight_grads(
        [
            [(d_a, attn)],
            [(h2, d_cq)],
            [(d_c, cattn)],
            [(texts, (d_ckv, 0, model))],
            [(texts, (d_ckv, model, model))],
        ],
        near_chips,
        True,
        deps=(d_text_own,),
    )
    d_qkv = d_qkv.reshape(slices, per, group * rows, 3 * width)
    padded_rows = slices * group * rows
    parts, d_qkv = call(
        qkv_grad_kernel,
        "qkv_grad",
        (slices,),
        [
            (d_qkv, pl.BlockSpec((1,) + d_qkv.shape[1:], lambda i: (i, 0, 0, 0))),
            (self_proj, None),
        ],
        [
            (
                struct((slices, group * rows, model)),
                pl.BlockSpec((1, group * rows, model), lambda i: (i, 0, 0)),
            ),
            (
                struct((padded_rows, 3 * local)),
                pl.BlockSpec((group * rows, 3 * local), lambda i: (i, 0)),
            ),
        ],
        deps=(attn_blocks[0], *ffn_back),
        flops=6 * padded_rows * model * local,
    )
    parts_own = parts.reshape(padded_rows, model)[: streams * rows].reshape(tp, count, model)
    parts = lax.all_to_all(parts_own, "tp", 0, 0)
    attn_got = from_chips(attn_blocks)
    qkv_blocks = weight_grads([[(h_all, d_qkv)]], near_chips, True, deps=(parts_own,), later=(attn_got[1],))
    qkv_got = from_chips(qkv_blocks)

    out_frames = out_all.reshape(streams, rows, model).astype(F32)

    (g_qkv,) = added(qkv_got)
    grad_self_proj = g_qkv.reshape(share, 3, local).transpose(1, 0, 2)

    (late,) = call(
        first_norm_kernel,
        "first_norm",
        (tp,),
        [
            (parts_own, pl.BlockSpec((1, count, model), lambda i: (i, 0, 0))),
            (frames.reshape(tp, count, model), pl.BlockSpec((1, count, model), lambda i: (i, 0, 0))),
        ],
        [(struct((2, model), F32), None)],
        flops=10 * streams * rows * model,
    )
    (d_x,) = call(
        last_kernel,
        "to_frames",
        (1,),
        [(parts, None), (x, None), (d_x2, None), (norm_rows(0), None)],
        [(struct((tp, count, model)), None)],
        deps=(*attn_got[1:], qkv_blocks[0]),
        flops=20 * count * model,
    )
    d_text = jnp.stack([text_got[0]] + [tied(g, d_x) for g in text_got[1:]])
    d_text = d_text[jnp.arange(tp) ^ t]
    d_text = lax.all_gather(d_text, "blk")
    if part % 16:
        d_text = d_text.transpose(1, 0, 2, 3)
        grad_text = d_text.reshape(streams, slots, text, model).astype(F32)
    else:
        (grad_text,) = call(
            text_kernel,
            "text_out",
            (tp,),
            [(d_text, pl.BlockSpec((blk, 1, part, model), lambda i: (0, i, 0, 0)))],
            [
                (
                    struct((tp, mine * text_rows, model), F32),
                    pl.BlockSpec((1, mine * text_rows, model), lambda i: (i, 0, 0)),
                )
            ],
        )
        grad_text = grad_text.reshape(streams, slots, text, model)
    grad_frames = tied(lax.all_to_all(d_x, "tp", 0, 0), grad_text)
    grad_frames = grad_frames.reshape(streams, rows, model).astype(F32)

    sums = tied(jnp.concatenate([early, late], axis=0), d_x)
    for step in (1 << i for i in range(blk.bit_length() - 1)):
        sums = sums + lax.ppermute(sums, "blk", swapped(blk, step))
    sums = lax.dynamic_slice_in_dim(sums, b * share, share, 1)
    mine_of, *got = from_ranks([sums] * tp)
    sums = added([mine_of] + [tied(g, grad_frames) for g in got])
    grad_gain = jnp.stack([sums[4], sums[0], sums[1]])
    grad_bias = jnp.stack([sums[5], sums[2], sums[3]])
    g_attn_own = over_ranks(added(attn_got), grad_frames)
    grad_cross_mem = g_attn_own[3:]
    for back in ffn_back:
        ffn_total += back.astype(F32)
    grad_ffn_up = ffn_total[0]
    grad_ffn_down = ffn_total[1].T
    grad_self_out = g_attn_own[0].T
    grad_cross_query = g_attn_own[1]
    grad_cross_out = g_attn_own[2].T
    return (
        out_frames,
        grad_frames,
        grad_text,
        grad_gain,
        grad_bias,
        grad_self_proj,
        grad_self_out,
        grad_cross_query,
        grad_cross_mem,
        grad_cross_out,
        grad_ffn_up,
        grad_ffn_down,
    )


def solution(mesh):
    in_specs = (
        P(None, "blk", None),
        P(),
        P(),
        P(),
        P(None, "blk", None),
        P(),
        P(),
        P(None, None, "tp"),
        P("tp", None),
        P(None, "tp"),
        P(None, None, "tp"),
        P("tp", None),
        P(None, "tp"),
        P("tp", None),
    )
    out_specs = (
        P(None, "blk", None),
        P(None, "blk", None),
        P(),
        P(None, "blk"),
        P(None, "blk"),
        P(None, "blk", "tp"),
        P("tp", "blk"),
        P("blk", "tp"),
        P(None, "blk", "tp"),
        P("tp", "blk"),
        P("blk", "tp"),
        P("tp", "blk"),
    )
    return jax.shard_map(shards, mesh=mesh, in_specs=in_specs, out_specs=out_specs, check_vma=False)
```

```python
import functools

import jax
import jax.numpy as jnp
from jax import lax
from jax.experimental import pallas as pl
from jax.experimental.pallas import tpu as pltpu
from jax.sharding import PartitionSpec as P

HEAD_DIM = 64
SCALE = 0.125
MASKED = -1e30
EPS = 1e-05
LANES = 128
BF = jnp.bfloat16
F32 = jnp.float32
MIB = 1 << 20

NN = ((1,), (0,))
NT = ((1,), (1,))
TN = ((0,), (0,))


def dot(a, b, dims):
    return lax.dot_general(a, b, (dims, ((), ())), preferred_element_type=F32)


def whole_spec(array):
    zeros = (0,) * len(array.shape)
    return pl.BlockSpec(tuple(array.shape), lambda *_: zeros)


def call(kernel, name, grid, ins, outs, scalars=(), scratch=(), deps=(), flops=0, exps=0):
    count = len(ins)

    def body(*refs):
        kept = len(scalars) + count
        kernel(*refs[:kept], *refs[kept + len(deps) :])

    specs = [whole_spec(a) if s is None else s for a, s in ins]
    specs += [pl.BlockSpec(memory_space=pl.ANY)] * len(deps)
    moved = sum(a.size * a.dtype.itemsize for a, _ in (*ins, *outs))
    return pl.pallas_call(
        body,
        out_shape=[o for o, _ in outs],
        grid_spec=pltpu.PrefetchScalarGridSpec(
            num_scalar_prefetch=len(scalars),
            grid=grid,
            in_specs=specs,
            out_specs=[whole_spec(o) if s is None else s for o, s in outs],
            scratch_shapes=list(scratch),
        ),
        compiler_params=pltpu.CompilerParams(vmem_limit_bytes=56 * MIB),
        cost_estimate=pl.CostEstimate(flops=flops, bytes_accessed=moved, transcendentals=exps),
        name=name,
    )(*scalars, *[a for a, _ in ins], *deps)


def struct(shape, dtype=BF):
    return jax.ShapeDtypeStruct(tuple(shape), dtype)


def assemble(whole_ref, near_ref, far_ref, device, parts=1):
    chips, ranks, share, cols = near_ref.shape
    c = cols // parts
    core = device % 2
    for chip in range(chips):
        for ref, k in ((near_ref, core), (far_ref, 1 - core)):
            rows = pl.ds(pl.multiple_of((2 * chip + k) * share, share), share)
            for p in range(parts):
                for r in range(ranks):
                    to = (p * ranks + r) * c
                    whole_ref[rows, to : to + c] = ref[chip, r, :, p * c : (p + 1) * c]


def columns(pair, size, place):
    return [
        (w, pl.BlockSpec(w.shape[:3] + (size,), lambda *_: (0, 0, 0, place))) for w in pair
    ]


def normalize(values):
    centre = values - jnp.mean(values, axis=-1, keepdims=True)
    inverse = lax.rsqrt(jnp.mean(centre * centre, axis=-1, keepdims=True) + EPS)
    return centre * inverse, inverse


def normed(values, gain, bias):
    return (normalize(values)[0] * gain + bias).astype(BF)


def norm_backward(values, gain, upstream):
    normal, inverse = normalize(values)
    g = upstream * gain
    mean_g = jnp.mean(g, axis=-1, keepdims=True)
    mean_gn = jnp.mean(g * normal, axis=-1, keepdims=True)
    d_values = inverse * (g - mean_g - normal * mean_gn)
    gain_sum = jnp.sum(upstream * normal, axis=0, keepdims=True)
    return d_values, gain_sum, jnp.sum(upstream, axis=0, keepdims=True)


def head_masks(width):
    lane = lax.broadcasted_iota(jnp.int32, (1, width), 1) // HEAD_DIM
    return [lane == h for h in range(width // HEAD_DIM)]


def pick(mask, values):
    return jnp.where(mask, values, jnp.zeros_like(values))


def stacked_heads(values):
    return jnp.concatenate([pick(m, values) for m in head_masks(values.shape[1])], axis=0)


def merged_heads(values, rows):
    total = values[:rows]
    for h, mask in enumerate(head_masks(values.shape[1])):
        if h:
            total = jnp.where(mask, values[h * rows : (h + 1) * rows], total)
    return total


def softmax(scores, allowed):
    scores = jnp.where(allowed, scores, MASKED)
    weights = jnp.exp(scores - jnp.max(scores, axis=1, keepdims=True))
    return weights * (1.0 / jnp.sum(weights, axis=1, keepdims=True))


def qkv_kernel(x_ref, norm_ref, w_ref, out_ref, h_ref):
    width = out_ref.shape[3] // 3
    x = x_ref[...].reshape(-1, x_ref.shape[-1]).astype(F32)
    h = normed(x, norm_ref[0:1], norm_ref[1:2])
    h_ref[...] = h
    for k in range(3):
        result = dot(h, w_ref[k], NN).astype(BF)
        for p in range(out_ref.shape[1]):
            out_ref[0, p, :, k * width : (k + 1) * width] = result[:, p * width : (p + 1) * width]


def qkv_pieces(frames, norm, weights, slices, parts, width, deps=()):
    streams, rows, model = frames.shape
    group = streams // slices
    out = struct((slices, parts, group * rows, 3 * width))
    return call(
        qkv_kernel,
        "qkv",
        (slices,),
        [
            (frames, pl.BlockSpec((group, rows, model), lambda i: (i, 0, 0))),
            (norm, None),
            (weights, None),
        ],
        [
            (out, pl.BlockSpec((1,) + out.shape[1:], lambda i: (i, 0, 0, 0))),
            (
                struct((streams * rows, model)),
                pl.BlockSpec((group * rows, model), lambda i: (i, 0)),
            ),
        ],
        deps=deps,
        flops=2 * streams * rows * weights.size,
    )


def qkv_grad_kernel(grad_ref, w_ref, out_ref, merged_ref):
    parts, width = grad_ref.shape[1], grad_ref.shape[3] // 3
    local = parts * width
    for p in range(parts):
        for k in range(3):
            to = k * local + p * width
            merged_ref[:, to : to + width] = grad_ref[0, p, :, k * width : (k + 1) * width]
    total = 0.0
    for k in range(3):
        total += dot(merged_ref[:, k * local : (k + 1) * local], w_ref[k], NT)
    out_ref[0] = total.astype(BF)


def first_norm_kernel(parts_ref, x_ref, sums_ref):
    d_h1 = parts_ref[0].astype(F32)
    normal, _ = normalize(x_ref[0].astype(F32))
    sums = [jnp.sum(d_h1 * normal, axis=0, keepdims=True), jnp.sum(d_h1, axis=0, keepdims=True)]

    @pl.when(pl.program_id(0) == 0)
    def _():
        sums_ref[...] = jnp.zeros_like(sums_ref)

    sums_ref[...] += jnp.concatenate(sums, axis=0)


def last_kernel(parts_ref, x_ref, dx2_ref, norm_ref, dx_ref):
    d_h1 = parts_ref[0].astype(F32)
    for r in range(1, parts_ref.shape[0]):
        d_h1 += parts_ref[r].astype(F32)
    d_v, _, _ = norm_backward(x_ref[...].astype(F32), norm_ref[0:1], d_h1)
    d_x = (dx2_ref[...] + d_v).astype(BF)
    for r in range(dx_ref.shape[0]):
        dx_ref[r] = d_x


def causal_probs(ends_ref, stream, slots, q, k, first):
    block = q.shape[0]
    rows = first + lax.broadcasted_iota(jnp.int32, (block, 1), 0)
    begin = jnp.zeros((block, 1), jnp.int32)
    for c in range(slots):
        end = ends_ref[stream, c]
        begin = jnp.where(rows >= end, jnp.maximum(begin, end), begin)
    cols = lax.broadcasted_iota(jnp.int32, (block, k.shape[0]), 1)
    return softmax(dot(q, k, NT), (cols <= rows) & (cols >= begin))


def self_forward_kernel(ends_ref, qkv_ref, out_ref, *, slots, width, block):
    stream = pl.program_id(0)
    parts, _, rows, _ = qkv_ref.shape
    length = parts * rows
    qkv = qkv_ref[...].reshape(length, 3 * width)
    q = qkv[:, :width] * jnp.asarray(SCALE, BF)
    k = qkv[:, width : 2 * width]
    v = qkv[:, 2 * width :]
    masks = head_masks(width)
    q_of = [pick(m, q) for m in masks]
    v_of = [pick(m, v) for m in masks]
    per = block // rows
    firsts = range(0, length, block)
    pairs = [(h, first) for first in firsts for h in range(len(masks))]
    probs = [
        causal_probs(
            ends_ref, stream, slots, q_of[h][first : first + block], k[: first + block], first
        ).astype(BF)
        for h, first in pairs
    ]
    results = [
        dot(p, v_of[h][: first + block], NN) for p, (h, first) in zip(probs, pairs)
    ]
    for first in firsts:
        total = sum(r for r, (_, f) in zip(results, pairs) if f == first)
        at = first // rows
        out_ref[at : at + per, 0] = total.astype(BF).reshape(per, rows, width)


def self_backward_kernel(ends_ref, qkv_ref, grad_ref, out_ref, dk_ref, dv_ref, *, slots, width, block):
    stream = pl.program_id(0)
    parts, _, rows, _ = qkv_ref.shape
    length = parts * rows
    qkv = qkv_ref[...].reshape(length, 3 * width)
    q = qkv[:, :width] * jnp.asarray(SCALE, BF)
    k = qkv[:, width : 2 * width]
    v = qkv[:, 2 * width :]
    grad = grad_ref[...].reshape(length, width)
    masks = head_masks(width)
    q_of = [pick(m, q) for m in masks]
    k_of = [pick(m, k) for m in masks]
    g_of = [pick(m, grad) for m in masks]
    dk_ref[...] = jnp.zeros_like(dk_ref)
    dv_ref[...] = jnp.zeros_like(dv_ref)
    per = block // rows
    for first in range(0, length, block):
        top = first + block
        heads = range(len(masks))
        q_part = [q_of[h][first:top] for h in heads]
        g_part = [g_of[h][first:top] for h in heads]
        d_probs = [dot(g, v[:top], NT) for g in g_part]
        probs = [causal_probs(ends_ref, stream, slots, a, k[:top], first) for a in q_part]
        delta = [jnp.sum(a * b, axis=1, keepdims=True) for a, b in zip(probs, d_probs)]
        d_scores = [(a * (b - c)).astype(BF) for a, b, c in zip(probs, d_probs, delta)]
        dq = sum(dot(a, k_of[h][:top], NN) for h, a in zip(heads, d_scores))
        dk_ref[:top] += sum(dot(a, b, TN) for a, b in zip(d_scores, q_part))
        dv_ref[:top] += sum(dot(a.astype(BF), b, TN) for a, b in zip(probs, g_part))
        at = first // rows
        out_ref[at : at + per, 0, :, :width] = (dq * SCALE).astype(BF).reshape(per, rows, width)
    out_ref[:, 0, :, width : 2 * width] = dk_ref[...].astype(BF).reshape(parts, rows, width)
    out_ref[:, 0, :, 2 * width :] = dv_ref[...].astype(BF).reshape(parts, rows, width)


def self_attention(ends, arrays, width, kernel, out_width, scratch, name, deps=()):
    parts, streams, rows, _ = arrays[0].shape
    length = parts * rows
    block = min(length, rows * max(1, 256 // rows))
    work = streams * (width // HEAD_DIM) * length * length

    def spec(c):
        return pl.BlockSpec((parts, 1, rows, c), lambda s, *_: (0, s, 0, 0))

    out = struct((parts, streams, rows, out_width))
    return call(
        functools.partial(kernel, slots=ends.shape[1], width=width, block=block),
        name,
        (streams,),
        [(a, spec(a.shape[3])) for a in arrays],
        [(out, spec(out_width))],
        scalars=(ends,),
        scratch=[pltpu.VMEM((length, width), F32)] * scratch,
        deps=deps,
        flops=4 * len(arrays) * work * HEAD_DIM,
        exps=work,
    )[0]


def first_kernel(device_ref, x_ref, norm_ref, near_ref, far_ref, *refs):
    pieces, (x2_ref, h2_ref, cq_ref, attn_out_ref, w_ref) = refs[:-5], refs[-5:]
    model = x2_ref.shape[1]
    assemble(w_ref, near_ref, far_ref, device_ref[0], 2)
    for j, ref in enumerate(pieces):
        piece = jnp.concatenate([ref[p] for p in range(ref.shape[0])], axis=1)
        local = piece.shape[1]
        to = pl.multiple_of((device_ref[1] ^ j) * local, local)
        attn_out_ref[:, pl.ds(to, local)] = piece
    attn = attn_out_ref[...]
    x2 = x_ref[...].astype(F32) + dot(attn, w_ref[:, :model], NT)
    x2_ref[...] = x2
    h2 = normed(x2, norm_ref[0:1], norm_ref[1:2])
    h2_ref[...] = h2
    cq_ref[...] = dot(h2, w_ref[:, model:], NN).astype(BF)


def memory_kernel(device_ref, text_ref, near_ref, far_ref, out_ref, w_ref):
    assemble(w_ref, near_ref, far_ref, device_ref[0])
    out_ref[...] = dot(text_ref[...], w_ref[...], NN).astype(BF)


def text_grad_kernel(device_ref, rows_ref, near_ref, far_ref, out_ref, w_ref):
    assemble(w_ref, near_ref, far_ref, device_ref[0], 2)
    out_ref[...] = dot(rows_ref[...], w_ref[...], NT).astype(BF)


def cross_allowed(info_ref, stream, slots, rows, keys):
    text = keys // slots
    pos = info_ref[stream, 2 * slots] + lax.broadcasted_iota(jnp.int32, (rows, 1), 0)
    clip = jnp.zeros((rows, 1), jnp.int32)
    for c in range(slots):
        clip += jnp.where(pos >= info_ref[stream, c], 1, 0)
    begin = clip * text
    count = jnp.zeros((rows, 1), jnp.int32)
    for c in range(slots):
        count = jnp.where(clip == c, info_ref[stream, slots + c], count)
    key = lax.broadcasted_iota(jnp.int32, (rows, keys), 1)
    return (key >= begin) & (key < begin + count)


CROSS_LANES = 256


def second_kernel(
    info_ref, x2_ref, cq_ref, kv_ref, norm_ref, near_ref, far_ref, *refs, slots, rows
):
    cattn_ref, x3_ref, h3_ref, wo_ref = refs
    stream = pl.program_id(0)
    model = x2_ref.shape[1]
    keys = kv_ref.shape[1]
    mine = pl.ds(pl.multiple_of(stream * rows, rows), rows)
    once = cross_allowed(info_ref, stream, slots, rows, keys)
    allowed = jnp.concatenate([once] * (CROSS_LANES // HEAD_DIM), axis=0)
    every = [slice(at, at + CROSS_LANES) for at in range(0, model, CROSS_LANES)]
    q = [stacked_heads(cq_ref[mine, c] * jnp.asarray(SCALE, BF)) for c in every]
    scores = [dot(a, kv_ref[0, :, c], NT) for a, c in zip(q, every)]
    probs = [softmax(a, allowed).astype(BF) for a in scores]
    values = [kv_ref[0, :, model + c.start : model + c.stop] for c in every]
    results = [dot(a, v, NN) for a, v in zip(probs, values)]
    for c, a in zip(every, results):
        cattn_ref[mine, c] = merged_heads(a, rows).astype(BF)

    @pl.when(stream == pl.num_programs(0) - 1)
    def _():
        assemble(wo_ref, near_ref, far_ref, info_ref[0, 2 * slots + 1])
        x3 = x2_ref[...] + dot(cattn_ref[...], wo_ref[...], NT)
        x3_ref[...] = x3
        h3_ref[...] = normed(x3, norm_ref[0:1], norm_ref[1:2])


def third_kernel(
    info_ref,
    dh_ref,
    received_ref,
    x3_ref,
    ct_ref,
    x2_ref,
    cq_ref,
    kv_ref,
    gain_ref,
    near1_ref,
    far1_ref,
    near2_ref,
    far2_ref,
    dc_ref,
    dcq_ref,
    dx2_ref,
    da_ref,
    dattn_ref,
    dkv_ref,
    sums_ref,
    dx3_ref,
    dcattn_ref,
    w_first_ref,
    w_cross_ref,
    *,
    slots,
    rows,
):
    device = info_ref[0, 2 * slots + 1]
    stream = pl.program_id(0)
    model = x2_ref.shape[1]
    keys = kv_ref.shape[1]

    @pl.when(stream == 0)
    def _():
        d_h3 = dh_ref[...] + received_ref[0].astype(F32)
        d_v, gain, bias = norm_backward(x3_ref[...], gain_ref[2:3], d_h3)
        sums_ref[1:2] = gain
        sums_ref[3:4] = bias
        d_x3 = ct_ref[...].astype(F32) + d_v
        dx3_ref[...] = d_x3
        d_c = d_x3.astype(BF)
        dc_ref[...] = d_c
        assemble(w_cross_ref, near2_ref, far2_ref, device)
        dcattn_ref[...] = dot(d_c, w_cross_ref[...], NN).astype(BF)

    mine = pl.ds(pl.multiple_of(stream * rows, rows), rows)
    once = cross_allowed(info_ref, stream, slots, rows, keys)
    allowed = jnp.concatenate([once] * (CROSS_LANES // HEAD_DIM), axis=0)
    every = [slice(at, at + CROSS_LANES) for at in range(0, model, CROSS_LANES)]
    k = [kv_ref[0, :, c] for c in every]
    v = [kv_ref[0, :, model + c.start : model + c.stop] for c in every]
    q = [stacked_heads(cq_ref[mine, c] * jnp.asarray(SCALE, BF)) for c in every]
    grad = [stacked_heads(dcattn_ref[mine, c]) for c in every]
    scores = [dot(a, b, NT) for a, b in zip(q, k)]
    d_probs = [dot(a, b, NT) for a, b in zip(grad, v)]
    probs = [softmax(a, allowed) for a in scores]
    delta = [jnp.sum(a * b, axis=1, keepdims=True) for a, b in zip(probs, d_probs)]
    d_scores = [(a * (b - c)).astype(BF) for a, b, c in zip(probs, d_probs, delta)]
    d_q = [dot(a, b, NN) for a, b in zip(d_scores, k)]
    d_k = [dot(a, b, TN) for a, b in zip(d_scores, q)]
    d_v = [dot(a.astype(BF), b, TN) for a, b in zip(probs, grad)]
    for i, c in enumerate(every):
        dcq_ref[mine, c] = (merged_heads(d_q[i], rows) * SCALE).astype(BF)
        dkv_ref[0, :, c] = d_k[i].astype(BF)
        dkv_ref[0, :, model + c.start : model + c.stop] = d_v[i].astype(BF)

    @pl.when(stream == pl.num_programs(0) - 1)
    def _():
        assemble(w_first_ref, near1_ref, far1_ref, device, 2)
        d_h2 = dot(dcq_ref[...], w_first_ref[:, model:], NT)
        d_v, gain, bias = norm_backward(x2_ref[...], gain_ref[1:2], d_h2)
        sums_ref[0:1] = gain
        sums_ref[2:3] = bias
        d_x2 = dx3_ref[...] + d_v
        dx2_ref[...] = d_x2
        d_a = d_x2.astype(BF)
        da_ref[...] = d_a
        d_attn = dot(d_a, w_first_ref[:, :model], NN).astype(BF)
        ranks, parts, _, width = dattn_ref.shape
        for p in range(ranks * parts):
            to = (p // parts) ^ info_ref[0, 2 * slots + 2]
            dattn_ref[to, p % parts] = d_attn[:, p * width : (p + 1) * width]


def ffn_kernel(h_ref, ct_ref, *refs, groups, tiles):
    (act_ref, dup_ref), results = refs[2 * groups : 2 * groups + 2], refs[2 * groups + 2 : -2]
    dh_acc, out_acc = refs[-2:]
    step = pl.program_id(0)

    @pl.when(step == 0)
    def _():
        dh_acc[...] = jnp.zeros_like(dh_acc)
        out_acc[...] = jnp.zeros_like(out_acc)

    for g in range(groups):

        @pl.when(step // tiles == g)
        def _(g=g):
            into, out_of = (NN, NT) if g else (NT, NN)
            size = refs[2 * g].shape[1] // 2
            parts = [slice(k * size, (k + 1) * size) for k in range(2)]
            w_up = [refs[2 * g][:, p] for p in parts]
            w_down = [refs[2 * g + 1][:, p] if g else refs[2 * g + 1][p, :] for p in parts]
            ups = [dot(h_ref[...], w, NN) for w in w_up]
            d_acts = [dot(ct_ref[...], w, into) for w in w_down]
            d_h, out = 0.0, 0.0
            for k, p in enumerate(parts):
                up = ups[k]
                cdf = 0.5 * (1.0 + lax.erf(up * (0.5**0.5)))
                slope = cdf + up * jnp.exp(-0.5 * up * up) * 0.3989422804014327
                act = (up * cdf).astype(BF)
                d_up = (d_acts[k] * slope).astype(BF)
                act_ref[:, p] = act
                dup_ref[:, p] = d_up
                d_h += dot(d_up, w_up[k], NT)
                out += dot(act, w_down[k], out_of)
            dh_acc[...] += d_h
            out_acc[...] += out

    @pl.when(step == groups * tiles - 1)
    def _():
        if len(results) == 2:
            results[0][...] = dh_acc[...]
            results[1][...] = out_acc[...]
        else:
            results[0][0] = dh_acc[...].astype(BF)
            results[0][1] = out_acc[...].astype(BF)


def feed_forward(h, ct, own, others, hidden, paired, deps=()):
    count, model = h.shape
    groups = 1 + len(others)
    tile = min(hidden, 512)
    tiles = hidden // tile

    def place(g):
        return lambda i: jnp.clip(i - g * tiles, 0, tiles - 1)

    ins = [(h, None), (ct, None)]
    ins.append((own[0], pl.BlockSpec((model, tile), lambda i: (0, place(0)(i)))))
    ins.append((own[1], pl.BlockSpec((tile, model), lambda i: (place(0)(i), 0))))
    for g, w in enumerate(others, 1):
        for first in (0, tiles):
            spec = pl.BlockSpec((model, tile), lambda i, g=g, f=first: (0, f + place(g)(i)))
            ins.append((w, spec))
    wide = struct((count, groups * hidden))
    results = [(struct((count, model), F32), None)] * 2
    if paired:
        results = [(struct((2, count, model)), None)]
    column = pl.BlockSpec((count, tile), lambda i: (0, i))
    return call(
        functools.partial(ffn_kernel, groups=groups, tiles=tiles),
        "feed_forward",
        (groups * tiles,),
        ins,
        [(wide, column), (wide, column), *results],
        scratch=[pltpu.VMEM((count, model), F32)] * 2,
        deps=deps,
        flops=8 * count * model * groups * hidden,
        exps=2 * count * groups * hidden,
    )


def weight_grad_kernel(index_ref, *refs, sums, chips, plus, apart):
    outs = refs[-chips:] if apart else [refs[-1].at[j] for j in range(chips)]
    at = 0
    for p, terms in enumerate(sums):
        lefts, rights = [], []
        for _ in range(terms):
            lefts.append(jnp.concatenate([r[...] for r in refs[at : at + chips]], axis=1))
            rights.append(refs[at + chips][...])
            at += chips + 1
        total = dot(jnp.concatenate(lefts, axis=0), jnp.concatenate(rights, axis=0), TN)
        share = total.shape[0] // chips
        for j in range(chips):
            block = total[j * share : (j + 1) * share]
            if plus:
                block += refs[sum(sums) * (chips + 1) + j][p].astype(F32)
            outs[j][p] = block.astype(BF)


def weight_grad_blocks(index, sums, share, plus=None, apart=False, deps=()):
    model = sums[0][0][0].shape[1]
    cols = sums[0][0][1][2]
    chips = model // (2 * share)
    if share % LANES:
        parts = []
        for terms in sums:
            total = 0.0
            for left, (right, first, _) in terms:
                left = left.reshape(-1, 2 * chips, share)[:, index]
                right = right[:, first : first + cols]
                total += dot(left.reshape(-1, chips * share), right, TN)
            parts.append(total.reshape(chips, share, cols))
        blocks = jnp.stack(parts, axis=1)
        if plus is not None:
            blocks += jnp.stack(plus).astype(F32)
        blocks = blocks.astype(BF)
        return [blocks[j] for j in range(chips)] if apart else blocks
    tile = 512 if cols % 512 == 0 else cols
    ins = []
    flops = 0
    for terms in sums:
        for left, (right, first, _) in terms:
            for j in range(chips):
                ins.append((left, pl.BlockSpec((left.shape[0], share), lambda i, w, j=j: (0, w[j]))))
            spec = pl.BlockSpec(
                (right.shape[0], tile), lambda i, w, first=first: (0, first // tile + i)
            )
            ins.append((right, spec))
            flops += right.shape[0] * model * cols
    every = struct((chips, len(sums), share, cols))
    every_spec = pl.BlockSpec((chips, len(sums), share, tile), lambda i, w: (0, 0, 0, i))
    one_spec = pl.BlockSpec((len(sums), share, tile), lambda i, w: (0, 0, i))
    outs = [(every, every_spec)]
    if plus is not None:
        ins += [(p, one_spec) for p in plus]
    if apart:
        outs = [(struct(every.shape[1:]), one_spec)] * chips
    result = call(
        functools.partial(
            weight_grad_kernel,
            sums=[len(terms) for terms in sums],
            chips=chips,
            plus=plus is not None,
            apart=apart,
        ),
        "weight_grad",
        (cols // tile,),
        ins,
        outs,
        scalars=(index,),
        deps=deps,
        flops=flops,
    )
    return result if apart else result[0]


def ffn_sum_kernel(in_ref, own_ref, *others):
    total = in_ref[0].astype(F32)
    for c in range(1, in_ref.shape[0]):
        total += in_ref[c].astype(F32)
    hidden = own_ref.shape[2]
    own_ref[...] = total[:, :, :hidden]
    for j, ref in enumerate(others, 1):
        ref[...] = total[:, :, j * hidden : (j + 1) * hidden].astype(BF)


def tie_kernel(*refs):
    pass


def tied(value, *first):
    anywhere = pl.BlockSpec(memory_space=pl.ANY)
    return pl.pallas_call(
        tie_kernel,
        out_shape=struct(value.shape, value.dtype),
        in_specs=[anywhere] * (1 + len(first)),
        out_specs=anywhere,
        input_output_aliases={0: 0},
        cost_estimate=pl.CostEstimate(flops=0, bytes_accessed=0, transcendentals=0),
        name="tied",
    )(value, *first)


def text_kernel(in_ref, out_ref):
    part = in_ref.shape[2]
    for i in range(in_ref.shape[0]):
        out_ref[0, i * part : (i + 1) * part] = in_ref[i, 0].astype(F32)


def shards(
    frames,
    text_states,
    clip_lengths,
    text_lengths,
    cotangent,
    norm_gain,
    norm_bias,
    self_proj,
    self_out,
    cross_query,
    cross_mem,
    cross_out,
    ffn_up,
    ffn_down,
):
    streams, rows, model = frames.shape
    slots, text = text_states.shape[1:3]
    text_rows = slots * text
    blk, tp = lax.axis_size("blk"), lax.axis_size("tp")
    b, t = lax.axis_index("blk"), lax.axis_index("tp")
    mine = streams // tp
    count = mine * rows
    core, chips = b % 2, blk // 2
    local = self_out.shape[0]
    per = min(blk // tp, local // HEAD_DIM)
    width = local // per
    slices = blk // per
    group = -(-streams // slices)
    share = model // blk
    hidden = ffn_up.shape[1]
    groups = tp // 2
    device = jnp.stack([b, t]).astype(jnp.int32)
    plane = [[2 * c + k for c in range(chips)] for k in range(2)]
    chip = b // 2
    all_chips = jnp.arange(chips, dtype=jnp.int32)
    near_chips = chip ^ jnp.arange(chips, dtype=jnp.int32)

    def swapped(size, j):
        return [(i, i ^ j) for i in range(size)]

    def of_rank(values, rank):
        return lax.dynamic_slice_in_dim(values, rank * mine, mine, 0)

    def norm_rows(i):
        return jnp.stack([norm_gain[i], norm_bias[i]])

    def at(values, i):
        return lax.dynamic_index_in_dim(values, i, 0, keepdims=False)

    def from_ranks(values):
        return [values[0]] + [
            lax.ppermute(values[j], "tp", swapped(tp, j)) for j in range(1, tp)
        ]

    def over_chips(blocks):
        return lax.all_to_all(blocks, "blk", 0, 0, axis_index_groups=plane)

    def other_core(values):
        return lax.ppermute(values, "blk", swapped(blk, 1))

    def spread(w, *first):
        near = over_chips(tied(jnp.broadcast_to(w, (chips,) + w.shape), *first))
        return near, other_core(near)

    def weight_grads(sums, order, apart, deps=(), later=()):
        sums = [
            [(left, r if isinstance(r, tuple) else (r, 0, r.shape[1])) for left, r in terms]
            for terms in sums
        ]
        send = weight_grad_blocks(2 * order + 1 - core, sums, share, apart=True, deps=deps)
        received = [other_core(v) for v in send]
        return weight_grad_blocks(
            2 * order + core, sums, share, received, apart=apart, deps=later
        )

    def from_chips(blocks):
        return [blocks[0]] + [
            lax.ppermute(blocks[j], "blk", swapped(blk, 2 * j)) for j in range(1, chips)
        ]

    def added(values):
        total = values[0].astype(F32)
        for v in values[1:]:
            total += v.astype(F32)
        return total

    def over_ranks(total, *first):
        parts, _, c = total.shape
        split = total.astype(BF).reshape(parts, share, tp, c // tp).transpose(2, 0, 1, 3)
        mine_of, *got = from_ranks([at(split, t ^ j) for j in range(tp)])
        return added([mine_of] + [tied(g, *first) for g in got])

    def share_rows(w):
        return lax.dynamic_slice_in_dim(w, b * share, share, w.ndim - 2)

    def share_cols(w):
        return lax.dynamic_slice_in_dim(w, b * share, share, 1).T

    mem = share_rows(cross_mem)
    shared = [mem[0], mem[1], share_cols(self_out), share_rows(cross_query), share_cols(cross_out)]
    shared = jnp.concatenate(shared, axis=1)
    piece = jnp.concatenate([share_rows(ffn_up), share_cols(ffn_down)], axis=1)

    padded = frames
    if slices * group > streams:
        padded = jnp.pad(frames, ((0, slices * group - streams), (0, 0), (0, 0)))
    pieces, h_all = qkv_pieces(
        padded, norm_rows(0), self_proj, slices, per, width, deps=(shared,)
    )
    qkv = lax.all_to_all(pieces.reshape(blk, group, rows, 3 * width), "blk", 0, 0)
    all_ends = jnp.cumsum(clip_lengths, axis=1).astype(jnp.int32)
    ends = of_rank(all_ends, t)
    own_ends = jnp.pad(all_ends, ((0, slices * group - streams), (0, 0)))
    own_ends = lax.dynamic_slice_in_dim(own_ends, b // per * group, group, 0)
    shared = lax.all_gather(shared, "tp")
    memory_weights = spread(shared[:, :, : 2 * local], qkv)
    w_mem = columns(memory_weights, 2 * local, 0)
    ct = of_rank(cotangent, t).reshape(count, model)
    ct_other = of_rank(cotangent, t ^ 1).reshape(count, model)
    x = of_rank(frames, t).reshape(count, model)
    texts = of_rank(text_states, t).reshape(mine * text_rows, model)
    attn_own = self_attention(
        own_ends, [qkv], width, self_forward_kernel, width, 0, "self_forward", deps=(ct, ct_other, x, texts)
    )
    even = slices == tp and group == mine

    attn_rows = lax.all_to_all(tied(attn_own, memory_weights[0]), "blk", 0, 0)
    if even:
        attn = attn_rows.reshape(tp, per, count, width)
    else:
        attn = attn_rows.reshape(slices, per, group, rows, width).transpose(0, 2, 1, 3, 4)
        attn = attn.reshape(slices * group, per, rows, width)[:streams]
        attn = attn.reshape(tp, mine, per, rows, width).transpose(0, 2, 1, 3, 4)
        attn = attn.reshape(tp, per, count, width)
    attn = from_ranks([at(attn, t ^ j) for j in range(tp)])

    weights = spread(shared[:, :, 2 * local :], *attn)
    w_first = columns(weights, 2 * local, 0)
    w_cross_out = columns(weights, local, 2)
    piece = tied(piece, *attn)
    pieces_of = [lax.ppermute(piece, "tp", swapped(tp, 2 * j)) for j in range(1, groups)]
    ffn_others = [
        lax.all_gather(tied(p, weights[0]), "blk", axis=0, tiled=True) for p in pieces_of
    ]

    info = jnp.concatenate(
        [
            ends,
            of_rank(text_lengths, t),
            jnp.full((mine, 1), b * rows, jnp.int32),
            jnp.full((mine, 1), b, jnp.int32),
            jnp.full((mine, 1), t, jnp.int32),
        ],
        axis=1,
    )
    flat = struct((count, model))
    wide = struct((count, model), F32)
    tile = model // 2
    (ckv,) = call(
        memory_kernel,
        "memory",
        (4,),
        [
            (texts, None),
            *[
                (
                    w,
                    pl.BlockSpec(
                        (chips, tp // 2, share, local), lambda i, _: (0, i % 2, 0, i // 2)
                    ),
                )
                for w in memory_weights
            ],
        ],
        [
            (
                struct((mine * text_rows, 2 * model)),
                pl.BlockSpec((mine * text_rows, tile), lambda i, _: (0, i)),
            )
        ],
        scalars=(device,),
        scratch=[pltpu.VMEM((model, tile), BF)],
        flops=4 * texts.shape[0] * model * model,
    )
    x2, h2, cq, attn = call(
        first_kernel,
        "to_cross",
        (1,),
        [
            (x, None),
            (norm_rows(1), None),
            *w_first,
            *[(a, None) for a in attn],
        ],
        [(wide, None), (flat, None), (flat, None), (flat, None)],
        scalars=(device,),
        scratch=[pltpu.VMEM((model, 2 * model), BF)],
        deps=(ckv,),
        flops=4 * count * model * model,
    )
    ckv = ckv.reshape(mine, text_rows, 2 * model)
    kv_spec = pl.BlockSpec((1, text_rows, 2 * model), lambda s, *_: (s, 0, 0))
    cross_work = count * (model // HEAD_DIM) * text_rows
    cattn, x3, h3 = call(
        functools.partial(second_kernel, slots=slots, rows=rows),
        "cross_forward",
        (mine,),
        [
            (x2, None),
            (cq, None),
            (ckv, kv_spec),
            (norm_rows(2), None),
            *w_cross_out,
        ],
        [(flat, None), (wide, None), (flat, None)],
        scalars=(info,),
        scratch=[pltpu.VMEM((model, model), BF)],
        flops=2 * count * model * model + 4 * cross_work * HEAD_DIM,
        exps=cross_work,
    )

    swap = swapped(tp, 1)
    h3_other = lax.ppermute(h3, "tp", swap)
    own_weights = (ffn_up, ffn_down)
    act, d_up, d_h3, out = feed_forward(h3, ct, own_weights, ffn_others, hidden, False)
    act_other, d_up_other, pair = feed_forward(
        h3_other, ct_other, own_weights, ffn_others, hidden, True, deps=(out,)
    )
    pair_got = lax.ppermute(pair, "tp", swap)
    out = x3 + out + pair_got[1].astype(F32)

    ffn_blocks = weight_grads(
        [[(h3, d_up), (h3_other, d_up_other)], [(ct, act), (ct_other, act_other)]],
        all_chips,
        False,
    )
    ffn_got = over_chips(ffn_blocks)
    ffn_total, *ffn_sent = call(
        ffn_sum_kernel,
        "ffn_sum",
        (1,),
        [(ffn_got, None)],
        [(struct((2, share, hidden), F32), None)]
        + [(struct((2, share, hidden)), None)] * (groups - 1),
    )

    d_c, d_cq, d_x2, d_a, d_attn, d_ckv, early = call(
        functools.partial(third_kernel, slots=slots, rows=rows),
        "cross_backward",
        (mine,),
        [
            (d_h3, None),
            (pair_got, pl.BlockSpec((1, count, model), lambda s, _: (0, 0, 0))),
            (x3, None),
            (ct, None),
            (x2, None),
            (cq, None),
            (ckv, kv_spec),
            (norm_gain, None),
            *w_first,
            *w_cross_out,
        ],
        [
            (flat, None),
            (flat, None),
            (wide, None),
            (flat, None),
            (struct((tp, per, count, width)), None),
            (struct(ckv.shape), kv_spec),
            (struct((4, model), F32), None),
        ],
        scalars=(info,),
        scratch=[
            pltpu.VMEM((count, model), F32),
            pltpu.VMEM((count, model), BF),
            pltpu.VMEM((model, 2 * model), BF),
            pltpu.VMEM((model, model), BF),
        ],
        deps=(ffn_blocks,),
        flops=6 * count * model * model + 10 * cross_work * HEAD_DIM,
        exps=cross_work,
    )


    d_attn = from_ranks([d_attn[j] for j in range(tp)])
    out_all = lax.all_gather(tied(out.astype(BF), *d_attn[1:]), "tp", axis=0, tiled=True)
    d_attn = jnp.stack(d_attn)[jnp.arange(tp) ^ t]
    if not even:
        d_attn = d_attn.reshape(tp, per, mine, rows, width).transpose(0, 2, 1, 3, 4)
        d_attn = d_attn.reshape(streams, per, rows, width)
        d_attn = jnp.pad(d_attn, ((0, slices * group - streams), (0, 0), (0, 0), (0, 0)))
        d_attn = d_attn.reshape(slices, group, per, rows, width).transpose(0, 2, 1, 3, 4)
    d_attn = d_attn.reshape(blk, group, rows, width)
    d_attn = lax.all_to_all(tied(d_attn, ffn_got), "blk", 0, 0)
    d_qkv_own = self_attention(
        own_ends,
        [qkv, d_attn],
        width,
        self_backward_kernel,
        3 * width,
        2,
        "self_backward",
    )

    part = mine * text_rows // blk
    d_ckv = d_ckv.reshape(chips, 2, part, 2 * model)
    received = other_core(lax.dynamic_index_in_dim(d_ckv, 1 - core, 1, keepdims=False))
    d_ckv = lax.dynamic_index_in_dim(d_ckv, core, 1, keepdims=False).astype(F32)
    d_ckv = tied((d_ckv + received.astype(F32)).astype(BF), d_attn)
    ckv_got = over_chips(d_ckv)
    d_ckv = jnp.sum(ckv_got.astype(F32), axis=0).astype(BF)

    d_qkv_own = tied(d_qkv_own, ckv_got)
    d_qkv = lax.all_to_all(d_qkv_own, "blk", 0, 0)
    texts = lax.dynamic_slice_in_dim(texts, b * part, part, 0)
    (d_text_own,) = call(
        text_grad_kernel,
        "text_grad",
        (1,),
        [(d_ckv, None), *w_mem],
        [(struct((part, model)), None)],
        scalars=(device,),
        scratch=[pltpu.VMEM((model, 2 * model), BF)],
        deps=(d_qkv_own, ffn_total),
        flops=4 * part * model * model,
    )
    text_got = from_ranks([d_text_own] * tp)

    ffn_back = [
        lax.ppermute(tied(v, out_all), "tp", swapped(tp, 2 * j)) for j, v in enumerate(ffn_sent, 1)
    ]
    attn_blocks = weight_grads(
        [
            [(d_a, attn)],
            [(h2, d_cq)],
            [(d_c, cattn)],
            [(texts, (d_ckv, 0, model))],
            [(texts, (d_ckv, model, model))],
        ],
        near_chips,
        True,
        deps=(d_text_own,),
    )
    d_qkv = d_qkv.reshape(slices, per, group * rows, 3 * width)
    padded_rows = slices * group * rows
    parts, d_qkv = call(
        qkv_grad_kernel,
        "qkv_grad",
        (slices,),
        [
            (d_qkv, pl.BlockSpec((1,) + d_qkv.shape[1:], lambda i: (i, 0, 0, 0))),
            (self_proj, None),
        ],
        [
            (
                struct((slices, group * rows, model)),
                pl.BlockSpec((1, group * rows, model), lambda i: (i, 0, 0)),
            ),
            (
                struct((padded_rows, 3 * local)),
                pl.BlockSpec((group * rows, 3 * local), lambda i: (i, 0)),
            ),
        ],
        deps=(attn_blocks[0], *ffn_back),
        flops=6 * padded_rows * model * local,
    )
    parts_own = parts.reshape(padded_rows, model)[: streams * rows].reshape(tp, count, model)
    parts = lax.all_to_all(parts_own, "tp", 0, 0)
    attn_got = from_chips(attn_blocks)
    qkv_blocks = weight_grads([[(h_all, d_qkv)]], near_chips, True, deps=(parts_own,), later=(attn_got[1],))
    qkv_got = from_chips(qkv_blocks)

    out_frames = out_all.reshape(streams, rows, model).astype(F32)

    (g_qkv,) = added(qkv_got)
    grad_self_proj = g_qkv.reshape(share, 3, local).transpose(1, 0, 2)

    (late,) = call(
        first_norm_kernel,
        "first_norm",
        (tp,),
        [
            (parts_own, pl.BlockSpec((1, count, model), lambda i: (i, 0, 0))),
            (frames.reshape(tp, count, model), pl.BlockSpec((1, count, model), lambda i: (i, 0, 0))),
        ],
        [(struct((2, model), F32), None)],
        flops=10 * streams * rows * model,
    )
    (d_x,) = call(
        last_kernel,
        "to_frames",
        (1,),
        [(parts, None), (x, None), (d_x2, None), (norm_rows(0), None)],
        [(struct((tp, count, model)), None)],
        deps=(*attn_got[1:], qkv_blocks[0]),
        flops=20 * count * model,
    )
    d_text = jnp.stack([text_got[0]] + [tied(g, d_x) for g in text_got[1:]])
    d_text = d_text[jnp.arange(tp) ^ t]
    d_text = lax.all_gather(d_text, "blk")
    if part % 16:
        d_text = d_text.transpose(1, 0, 2, 3)
        grad_text = d_text.reshape(streams, slots, text, model).astype(F32)
    else:
        (grad_text,) = call(
            text_kernel,
            "text_out",
            (tp,),
            [(d_text, pl.BlockSpec((blk, 1, part, model), lambda i: (0, i, 0, 0)))],
            [
                (
                    struct((tp, mine * text_rows, model), F32),
                    pl.BlockSpec((1, mine * text_rows, model), lambda i: (i, 0, 0)),
                )
            ],
        )
        grad_text = grad_text.reshape(streams, slots, text, model)
    grad_frames = tied(lax.all_to_all(d_x, "tp", 0, 0), grad_text)
    grad_frames = grad_frames.reshape(streams, rows, model).astype(F32)

    sums = tied(jnp.concatenate([early, late], axis=0), d_x)
    for step in (1 << i for i in range(blk.bit_length() - 1)):
        sums = sums + lax.ppermute(sums, "blk", swapped(blk, step))
    sums = lax.dynamic_slice_in_dim(sums, b * share, share, 1)
    mine_of, *got = from_ranks([sums] * tp)
    sums = added([mine_of] + [tied(g, grad_frames) for g in got])
    grad_gain = jnp.stack([sums[4], sums[0], sums[1]])
    grad_bias = jnp.stack([sums[5], sums[2], sums[3]])
    g_attn_own = over_ranks(added(attn_got), grad_frames)
    grad_cross_mem = g_attn_own[3:]
    for back in ffn_back:
        ffn_total += back.astype(F32)
    grad_ffn_up = ffn_total[0]
    grad_ffn_down = ffn_total[1].T
    grad_self_out = g_attn_own[0].T
    grad_cross_query = g_attn_own[1]
    grad_cross_out = g_attn_own[2].T
    return (
        out_frames,
        grad_frames,
        grad_text,
        grad_gain,
        grad_bias,
        grad_self_proj,
        grad_self_out,
        grad_cross_query,
        grad_cross_mem,
        grad_cross_out,
        grad_ffn_up,
        grad_ffn_down,
    )


def solution(mesh):
    in_specs = (
        P(None, "blk", None),
        P(),
        P(),
        P(),
        P(None, "blk", None),
        P(),
        P(),
        P(None, None, "tp"),
        P("tp", None),
        P(None, "tp"),
        P(None, None, "tp"),
        P("tp", None),
        P(None, "tp"),
        P("tp", None),
    )
    out_specs = (
        P(None, "blk", None),
        P(None, "blk", None),
        P(),
        P(None, "blk"),
        P(None, "blk"),
        P(None, "blk", "tp"),
        P("tp", "blk"),
        P("blk", "tp"),
        P(None, "blk", "tp"),
        P("tp", "blk"),
        P("blk", "tp"),
        P("tp", "blk"),
    )
    return jax.shard_map(shards, mesh=mesh, in_specs=in_specs, out_specs=out_specs, check_vma=False)
```
